32 devices in a mesh: dp: 8 (over z, y), mp: 4 (over x, core).
Axes of the slice: x: 2, y: 2, z: 4, core: 2. Of those that a mesh axis runs over, the one named last changes fastest.
Arguments:
- mel: bfloat16 [8, 4096, 80], P('dp', 'mp'), may hold values from -6 to 6
- lengths: int32 [8], P('dp'), may hold values from 1 to 4096, 24576 in all
- alignment: int32 [8, 512], P('dp', 'mp'), may hold values from 0 to 1024
- loss_mask: int32 [8, 512], P('dp', 'mp'), may hold values 0 or 1
- ff_in: float32 [3, 2, 512, 2048], P(None, None, 'dp', 'mp')
- ff_out: float32 [3, 2, 2048, 512], P(None, None, 'mp', 'dp')
- mix_in: float32 [3, 512, 6, 512], P(None, 'dp', None, 'mp')
- mix_out: float32 [3, 2, 512, 512], P(None, None, 'mp', 'dp')
- small: float32 [3, 1985280], P(None, ('dp', 'mp'))
Outputs:
- ff_in_new: float32 [2, 512, 2048], P(None, 'dp', 'mp')
- ff_in_first: float32 [2, 512, 2048], P(None, 'dp', 'mp')
- ff_in_second: float32 [2, 512, 2048], P(None, 'dp', 'mp')
- ff_out_new: float32 [2, 2048, 512], P(None, 'mp', 'dp')
- ff_out_first: float32 [2, 2048, 512], P(None, 'mp', 'dp')
- ff_out_second: float32 [2, 2048, 512], P(None, 'mp', 'dp')
- mix_in_new: float32 [512, 6, 512], P('dp', None, 'mp')
- mix_in_first: float32 [512, 6, 512], P('dp', None, 'mp')
- mix_in_second: float32 [512, 6, 512], P('dp', None, 'mp')
- mix_out_new: float32 [2, 512, 512], P(None, 'mp', 'dp')
- mix_out_first: float32 [2, 512, 512], P(None, 'mp', 'dp')
- mix_out_second: float32 [2, 512, 512], P(None, 'mp', 'dp')
- small_new: float32 [1985280], P(('dp', 'mp'))
- small_first: float32 [1985280], P(('dp', 'mp'))
- small_second: float32 [1985280], P(('dp', 'mp'))
- vec_grad: float32 [23, 512], replicated
- loss: float32 [], replicated
- grad_norm: float32 [], replicated
The draws below stay inside these ranges and needn't reach their ends.
Inputs may be any that keep to these rules, and one draw needn't show every extreme that they name: `lengths`: each utterance's mel frame count; the longest has 4096 frames.
All inputs are finite; a program needn't handle non-finite values. No bound on the sum of `lengths` or of `loss_mask` on one device may be relied on, other than what follows from the above.
Results may differ from the reference program's by a relative error of at most 0.014.
The reference program's roundings to bfloat16 on the way count: a program that leaves them out, or rounds other values in their place, can miss the bound.
Values may be sent and summed in bfloat16 or wider, within the bound.
No kernel may reach another device: no remote copies, remote signals or barrier semaphores. Data moves between devices by JAX's collectives and lax.ppermute only.
A program may use at most 512 MiB of HBM per device.

```python
import math
import jax
import jax.numpy as jnp
import numpy as np
from jax import lax

D = 512
HEADS = 8
HEAD_DIM = 64
FF = 2048
CHANNELS = 256
MEL = 80
KERNEL = 9
CLASSES = 1025
STEP = 7
SEQ = 512
BATCH = 8
BLOCK = 512
NSMALL = 1985280
NPARAMS = 8276736


clip_norm = 0.005


def grad_unit():
    return clip_norm / math.sqrt(NPARAMS)


def state_stack(key, array_shape, spread, grad_size):
    subkeys = jax.random.split(key, 3)
    weight = spread * jax.random.normal(subkeys[0], array_shape, jnp.float32)
    first_moment = 0.111 * grad_size * jax.random.normal(subkeys[1], array_shape, jnp.float32)
    factor = jnp.exp(jax.random.uniform(subkeys[2], array_shape, jnp.float32, 0.0, math.log(4.0)))
    second_moment = 0.0204 * grad_size * grad_size * factor
    return jnp.stack([weight, first_moment, second_moment])


def draw_ff_in(key, part):
    return state_stack(key, (2, D, FF), D ** (-0.5), grad_unit())


def draw_ff_out(key, part):
    return state_stack(key, (2, FF, D), FF ** (-0.5), grad_unit())


def draw_mix_in(key, part):
    return state_stack(key, (D, 6, D), D ** (-0.5), grad_unit())


def draw_mix_out(key, part):
    spread = jnp.array([(SEQ / (9.0 * D)) ** 0.5, D ** (-0.5)], jnp.float32)[:, None, None]
    return state_stack(key, (2, D, D), spread, grad_unit())


def draw_small(key, part):
    subkeys = jax.random.split(key, 5)
    unit = grad_unit()
    lin_rows = CHANNELS * (MEL // 8)
    taps_state = state_stack(subkeys[0], (27, CHANNELS), 1.0 / 3.0, unit)
    point_state = state_stack(subkeys[1], (2, CHANNELS, CHANNELS), CHANNELS ** (-0.5), unit)
    linear_state = state_stack(subkeys[2], (lin_rows, D), lin_rows ** (-0.5), unit)
    head_state = state_stack(subkeys[3], (D, CLASSES), D ** (-0.5), unit)
    row_spread = jnp.array([0.1] * 12 + [0.5, 0.5] + [1.0 / 3.0] * 9, jnp.float32)[:, None]
    vector_state = state_stack(subkeys[4], (23, D), row_spread, 4.0 * unit)
    base_rows = jnp.array([1.0] * 5 + [0.0] * 5 + [1.0] + [0.0] * 12, jnp.float32)[:, None]
    vector_state = vector_state.at[0].add(base_rows)
    pieces = (taps_state, point_state, linear_state, head_state, vector_state)
    return jnp.concatenate([state_piece.reshape(3, -1) for state_piece in pieces], 1)


def touch_ends(result, rng, least, largest):
    dims = result.shape
    place = [jax.random.randint(jax.random.fold_in(rng, axis), (), 0, dims[axis]) for axis in range(len(dims))]
    result = result.at[tuple(place)].set(least)
    longest = dims.index(max(dims))
    place[longest] = (place[longest] + 1) % dims[longest]
    return result.at[tuple(place)].set(largest)


def levels(own_key, dims, cuts, least, high):
    loudness, own = 1.0, jax.random.fold_in(own_key, 6)
    for dim, blocks in cuts:
        heights = jnp.exp(jax.random.uniform(jax.random.fold_in(own, dim), (blocks,), jnp.float32, least / len(cuts), high / len(cuts)))
        loudness = loudness * jnp.repeat(heights, dims[dim] // blocks).reshape([-1 if axis == dim else 1 for axis in range(len(dims))])
    return loudness


def split_up(amount, total, reach, skew):
    weights = [(1 << 20) // math.isqrt(rank ** skew) + 1 for rank in range(2, amount + 1)]
    rest, holding = total - reach - (amount - 1), [1] * (amount - 1)
    while rest > 0:
        free = [i for i in range(amount - 1) if holding[i] < reach]
        whole, left = sum([weights[i] for i in free]), rest
        for i in free:
            more = min(reach - holding[i], max(1, left * weights[i] // whole), rest)
            holding[i] = holding[i] + more
            rest = rest - more
    return np.array([reach] + holding)


def uneven_parts(stream_key, number_of, total, limit, skew):
    if number_of == 2:
        one = jax.random.randint(stream_key, (), max(1, total - limit), min(limit, total - 1) + 1)
        return jnp.stack([one, total - one])
    sizes = jnp.asarray(split_up(number_of, total, limit, skew), jnp.int32)
    couples = (number_of - 1) // 2
    source_of, taker = sizes[1:1 + 2 * couples:2], sizes[2:2 + 2 * couples:2]
    margin = jnp.minimum(source_of - 1, limit - taker)
    moved = jax.random.randint(jax.random.fold_in(stream_key, 1), (couples,), 0, 1 << 20) % (margin + 1)
    sizes = sizes.at[1:1 + 2 * couples:2].set(source_of - moved).at[2:2 + 2 * couples:2].set(taker + moved)
    return sizes[jax.random.permutation(jax.random.fold_in(stream_key, 2), number_of)]


def gaussian(stream_key, dims, width, bound, cuts=(), kind=jnp.bfloat16):
    drawn = jax.random.normal(stream_key, dims, jnp.float32) * width
    if len(cuts) > 0:
        drawn = levels(stream_key, dims, cuts, -0.22, 0.18) * drawn
    return jnp.clip(drawn, min=-bound, max=bound).astype(kind)


def setup_inputs(seed: int = 0) -> dict:
    key_list = jax.random.split(jax.random.key(seed), 10)
    return {
        "mel": gaussian(key_list[0], (BATCH, 8 * SEQ, MEL), 1.0, 6.0, ((0, 8), (1, 4))),
        "lengths": uneven_parts(key_list[1], BATCH, 6 * SEQ * BATCH, 8 * SEQ, 2).astype(jnp.int32),
        "alignment": touch_ends(jax.random.randint(key_list[2], (BATCH, SEQ), 0, CLASSES), jax.random.fold_in(key_list[2], 1), 0, CLASSES - 1).astype(jnp.int32),
        "loss_mask": touch_ends((jax.random.randint(key_list[3], (BATCH, SEQ), 0, 4) < 3).astype(jnp.int32), jax.random.fold_in(key_list[3], 1), 0, 1),
        "ff_in": draw_ff_in(jax.random.fold_in(key_list[9], 71), 0),
        "ff_out": draw_ff_out(jax.random.fold_in(key_list[9], 71), 0),
        "mix_in": draw_mix_in(jax.random.fold_in(key_list[9], 71), 0),
        "mix_out": draw_mix_out(jax.random.fold_in(key_list[9], 71), 0),
        "small": draw_small(jax.random.fold_in(key_list[9], 71), 0),
    }


norm_eps = 1e-05
clip_norm = 0.005
beta_one = 0.9
beta_two = 0.98
adam_eps = 1e-08
decay_rate = 0.01
small_rates = (0.8, 0.15, 0.05, 0.1, 0.3)
highest = lax.Precision.HIGHEST

@jax.custom_vjp
def low(v):
    return lax.optimization_barrier(v.astype(jnp.bfloat16)).astype(jnp.float32)

@jax.custom_vjp
def low_back(v):
    return v

def low_keep(v):
    return (low(v), None)

def low_pass(kept, grad):
    return (grad,)

def back_keep(v):
    return (v, None)

def back_low(kept, grad):
    return (low(grad),)
low.defvjp(low_keep, low_pass)
low_back.defvjp(back_keep, back_low)

def matmul(left, right):
    return jnp.dot(left, right, precision=highest, preferred_element_type=jnp.float32)

def layer_norm(values, gain, shift):
    centre = lax.optimization_barrier(jnp.mean(values, -1, keepdims=True))
    centered = values - centre
    variance = lax.optimization_barrier(jnp.mean(centered * centered, -1, keepdims=True))
    return centered * lax.rsqrt(variance + norm_eps) * gain + shift

def strided_taps(field):
    out_count = (field.shape[0] - 1) // 2
    freq_width = field.shape[1]
    padding = [(0, 0), (1, 1)] + [(0, 0)] * (field.ndim - 2)
    padded = jnp.pad(field, padding)
    return [padded[row_tap:row_tap + 2 * out_count - 1:2, col_tap:col_tap + freq_width - 1:2] for row_tap in range(3) for col_tap in range(3)]

def first_conv(field, weight):
    windows = strided_taps(field)
    return sum((window[..., None] * weight[tap_index] for tap_index, window in enumerate(windows)))

def depth_conv(field, weight):
    windows = strided_taps(field)
    return sum((window * weight[tap_index] for tap_index, window in enumerate(windows)))

def pad_time(field):
    return jnp.pad(field, [(1, 1)] + [(0, 0)] * (field.ndim - 1))

def stem(mel_rows, stem_taps, pointwise, linear):
    first = jax.nn.relu(first_conv(pad_time(mel_rows), stem_taps[0:9]))
    second_in = low(depth_conv(pad_time(first), stem_taps[9:18]))
    second = low_back(matmul(second_in, pointwise[0]))
    third_in = low(depth_conv(pad_time(jax.nn.relu(second)), stem_taps[18:27]))
    third = low_back(matmul(third_in, pointwise[1]))
    flattened = low(jax.nn.relu(third)).reshape(third.shape[0], -1)
    return low_back(matmul(flattened, linear))

def position_table(length):
    distance = (length - 1 - jnp.arange(2 * length - 1)).astype(jnp.float32)[:, None]
    inverse_freq = jnp.exp(jnp.arange(D // 2).astype(jnp.float32) * (-2.0 * math.log(10000.0) / D))
    angles = distance * inverse_freq[None, :]
    return jnp.concatenate([jnp.sin(angles), jnp.cos(angles)], 1)

def skew(field, block_rows, length):
    heads_here = field.shape[0]
    flattened = field.reshape(heads_here, -1)[:, block_rows - 1:block_rows - 1 + block_rows * (block_rows + length - 2)]
    return flattened.reshape(heads_here, block_rows, block_rows + length - 2)[:, :, :length]

def feed_forward(x_rows, gain, shift, weight_in, weight_out):
    normed = low(layer_norm(x_rows, gain, shift))
    pre_act = low_back(matmul(normed, weight_in))
    hidden = low(jax.nn.silu(pre_act))
    return x_rows + 0.5 * low_back(matmul(hidden, weight_out))

def attention(x_rows, vectors, weight_in, weight_out, valid_seq):
    length = x_rows.shape[0]
    shape_heads = (length, HEADS, HEAD_DIM)
    normed = low(layer_norm(x_rows, vectors[1], vectors[6]))
    query = low_back(matmul(normed, weight_in[:, 0]))
    query_u = low(query + vectors[12]).reshape(shape_heads)
    query_v = low(query + vectors[13]).reshape(shape_heads)
    keys_h = low_back(low(matmul(normed, weight_in[:, 1]))).reshape(shape_heads)
    values_h = low_back(low(matmul(normed, weight_in[:, 2]))).reshape(shape_heads)
    table = low(position_table(length))
    posit = low_back(low(matmul(table, weight_in[:, 3]))).reshape(2 * length - 1, HEADS, HEAD_DIM)

    def one_block(start):
        q_u = lax.dynamic_slice_in_dim(query_u, start, BLOCK, 0)
        q_v = lax.dynamic_slice_in_dim(query_v, start, BLOCK, 0)
        frame = lax.dynamic_slice_in_dim(posit, (length - BLOCK - start).astype(jnp.int32), BLOCK + length - 1, 0)
        raw = jnp.einsum('rhd,khd->hrk', q_u, keys_h, precision=highest)
        raw = raw + skew(jnp.einsum('rhd,nhd->hrn', q_v, frame, precision=highest), BLOCK, length)
        scores = jnp.where(valid_seq[None, None, :] > 0, low_back(raw) * 0.125, -1e+30)
        probs = jax.nn.softmax(scores, -1)
        return jnp.einsum('hrk,khd->rhd', low(probs), values_h, precision=highest)
    starts = jnp.arange(length // BLOCK, dtype=jnp.int32) * BLOCK
    blocks = lax.map(jax.checkpoint(one_block), starts)
    attended = low_back(low(blocks.reshape(length, D)))
    return x_rows + low_back(matmul(attended, weight_out))

def depth_time(field, kernel):
    half_kernel = KERNEL // 2
    length = field.shape[0]
    padded = jnp.pad(field, ((half_kernel, half_kernel), (0, 0)))
    return sum((padded[tap_index:tap_index + length] * kernel[tap_index] for tap_index in range(KERNEL)))

def glu_depth(gates, kernel, valid_seq):
    half_width = gates.shape[1] // 2
    gated = gates[:, :half_width] * jax.nn.sigmoid(gates[:, half_width:]) * valid_seq[:, None]
    return depth_time(gated, kernel)

def conv_front(x_rows, vectors, weight_in, valid_seq):
    normed = low(layer_norm(x_rows, vectors[2], vectors[7]))
    gates = low_back(matmul(normed, weight_in[:, 4:6].reshape(D, 2 * D)))
    return glu_depth(gates, vectors[14:23], valid_seq)

def conv_rear(x_rows, hidden, mean_vals, inverse, vectors, weight_out):
    normal_h = (hidden - mean_vals) * inverse
    batch_out = normal_h * vectors[10] + vectors[11]
    activated = low(jax.nn.silu(batch_out))
    return x_rows + low_back(matmul(activated, weight_out))

def small_sizes():
    return [27 * CHANNELS, 2 * CHANNELS * CHANNELS, CHANNELS * (MEL // 8) * D, D * CLASSES, 23 * D]

def unpack_small(flattened):
    shapes = [(27, CHANNELS), (2, CHANNELS, CHANNELS), (CHANNELS * (MEL // 8), D), (D, CLASSES), (23, D)]
    pieces = []
    offset = 0
    for piece_size, piece_shape in zip(small_sizes(), shapes):
        pieces.append(flattened[offset:offset + piece_size].reshape(piece_shape))
        offset += piece_size
    return pieces

def total_loss(ff_in_w, ff_out_w, mix_in_w, mix_out_w, small_w, mel_rows, valid_rows, loss_weight, labels, frame_count):
    stem_taps, pointwise, linear, head_w, vectors = unpack_small(small_w)

    def section_one(inputs):
        mel_seq, valid_seq = inputs
        start_x = stem(mel_seq, stem_taps, pointwise, linear)
        after_ff = feed_forward(start_x, vectors[0], vectors[5], ff_in_w[0], ff_out_w[0])
        after_att = attention(after_ff, vectors, mix_in_w, mix_out_w[0], valid_seq)
        return (after_att, conv_front(after_att, vectors, mix_in_w, valid_seq))
    after_att, hidden = lax.map(jax.checkpoint(section_one), (mel_rows, valid_rows))
    mask_cols = valid_rows[:, :, None]
    mean_vals = lax.optimization_barrier(jnp.sum(mask_cols * hidden, (0, 1))) / frame_count
    variance = lax.optimization_barrier(jnp.sum(mask_cols * hidden * hidden, (0, 1))) / frame_count - mean_vals * mean_vals
    inverse = lax.rsqrt(variance + norm_eps)

    def section_two(inputs):
        att_seq, hidden_seq, labels_seq, weight_seq = inputs
        after_conv = conv_rear(att_seq, hidden_seq, mean_vals, inverse, vectors, mix_out_w[1])
        after_ff = feed_forward(after_conv, vectors[3], vectors[8], ff_in_w[1], ff_out_w[1])
        normed = low(layer_norm(after_ff, vectors[4], vectors[9]))
        logits = low_back(matmul(normed, head_w))
        onehot = (jnp.arange(CLASSES, dtype=jnp.int32)[None, :] == labels_seq[:, None]).astype(jnp.float32)
        picked = lax.optimization_barrier(jnp.sum(onehot * logits, -1))
        return jnp.sum(weight_seq * (jax.nn.logsumexp(logits, -1) - picked))
    seq_losses = lax.map(jax.checkpoint(section_two), (after_att, hidden, labels, loss_weight))
    return jnp.sum(seq_losses) / frame_count

def adam(state, grad, rate):
    first_new = beta_one * state[1] + (1.0 - beta_one) * grad
    second_new = beta_two * state[2] + (1.0 - beta_two) * grad * grad
    direction = first_new / (1.0 - beta_one ** STEP) / (jnp.sqrt(second_new / (1.0 - beta_two ** STEP)) + adam_eps)
    weight_new = state[0] - rate * (direction + decay_rate * state[0])
    return (weight_new, first_new, second_new)

def small_rate_table():
    return jnp.concatenate([jnp.full((piece_size,), piece_rate, jnp.float32) for piece_size, piece_rate in zip(small_sizes(), small_rates)])

def reference(mel, lengths, alignment, loss_mask, ff_in, ff_out, mix_in, mix_out, small):
    frames = jnp.arange(8 * SEQ, dtype=jnp.int32)
    keep_frames = (frames[None, :] < lengths[:, None])[:, :, None]
    mel_rows = jnp.where(keep_frames, mel.astype(jnp.float32), 0.0)
    valid_rows = (8 * jnp.arange(SEQ, dtype=jnp.int32)[None, :] < lengths[:, None]).astype(jnp.float32)
    frame_count = jnp.sum(valid_rows)
    loss_weight = valid_rows * loss_mask.astype(jnp.float32)
    states = (ff_in, ff_out, mix_in, mix_out, small)
    params = tuple((low(state[0]) for state in states))

    def loss_fn(w_one, w_two, w_three, w_four, w_five):
        return total_loss(w_one, w_two, w_three, w_four, w_five, mel_rows, valid_rows, loss_weight, alignment, frame_count)
    loss_value, pullback = jax.vjp(loss_fn, params[0], params[1], params[2], params[3], params[4])
    gradients = pullback(jnp.ones((), jnp.float32))
    total_sq = sum((jnp.sum(grad_arr * grad_arr) for grad_arr in gradients))
    grad_norm = jnp.sqrt(total_sq)
    factor = clip_norm / jnp.maximum(grad_norm, clip_norm)
    rates = (0.1, 0.05, 0.1, jnp.array([1.0, 0.1], jnp.float32)[:, None, None], small_rate_table())
    new_states = [adam(state, grad_arr * factor, rate) for state, grad_arr, rate in zip(states, gradients, rates)]
    vec_grad = gradients[4][NSMALL - 23 * D:].reshape(23, D) * factor
    return (new_states[0][0], new_states[0][1], new_states[0][2], new_states[1][0], new_states[1][1], new_states[1][2], new_states[2][0], new_states[2][1], new_states[2][2], new_states[3][0], new_states[3][1], new_states[3][2], new_states[4][0], new_states[4][1], new_states[4][2], vec_grad, loss_value, grad_norm)
```

```python
import functools
import math

import jax
import jax.numpy as jnp
from jax import lax
from jax.experimental import pallas as pl
from jax.experimental.pallas import tpu as pltpu
from jax.sharding import PartitionSpec as P

D = 512
HEADS = 8
HEAD_DIM = 64
CHANNELS = 256
MEL = 80
KERNEL = 9
CLASSES = 1025
STEP = 7
LANES = 128
NPIECE = 4
F1, F2, F3 = MEL // 2, MEL // 4, MEL // 8
CPAD = 1152
HALO = 8
EDGE = 16

norm_eps = 1e-05
clip_norm = 0.005
beta_one = 0.9
beta_two = 0.98
adam_eps = 1e-08
decay_rate = 0.01
small_rates = (0.8, 0.15, 0.05, 0.1, 0.3)
f32 = jnp.float32
bf16 = jnp.bfloat16

SIZES = [27 * CHANNELS, 2 * CHANNELS * CHANNELS, CHANNELS * F3 * D, D * CLASSES, 23 * D]
NSMALL = sum(SIZES)
ROWS = [size // LANES for size in SIZES]
ROW_AT = [sum(ROWS[:k]) for k in range(5)]
NROWS = NSMALL // LANES


CORES, COLS, LINES = 2, 2, 2


def planned(n_dp, n_mp):
    return (n_dp, n_mp) == (8, 4)


def sent(x, name, by=1):
    axis, stride, size = {
        "c": ("mp", 1, 2),
        "x": ("mp", 2, 2),
        "y": ("dp", 1, 2),
        "z": ("dp", 2, lax.axis_size("dp") // 2),
    }[name]
    pairs = []
    for i in range(lax.axis_size(axis)):
        k = (i // stride) % size
        pairs.append((i, i + (((k + by) % size) - k) * stride))
    return lax.ppermute(x, axis, pairs)


def total(*parts):
    return functools.reduce(lambda a, b: a + b, [part.astype(f32) for part in parts])


def low_total(*parts):
    return total(*parts).astype(bf16)


class Reduced:
    def __init__(self, *parts):
        self.parts, self.deep = parts[:2], parts[0].shape[2]
        self.out = [parts[2], parts[3]]

    def cores(self):
        got = [sent(x, "c") for x in self.out]
        self.a, self.b = ([keep, more] for keep, more in zip(self.parts, got))
        self.out = [
            low_total(*[part[1] for part in self.a]),
            low_total(*[part[:, 1] for part in self.b]),
        ]
        return self.out

    def first(self):
        got_a, got_b = sent(self.out[0], "x"), sent(self.out[1], "y")
        self.a = [part[0] for part in self.a] + [got_a]
        self.b = [part[:, 0] for part in self.b] + [got_b]
        self.out = [
            low_total(*[part[1] for part in self.a]),
            low_total(*[part[1] for part in self.b]),
        ]
        return self.out

    def second(self):
        got_a, got_b = sent(self.out[0], "y"), sent(self.out[1], "x")
        self.a = [part[0] for part in self.a] + [got_a]
        self.b = [part[0] for part in self.b] + [got_b]
        self.out = [
            jnp.stack(
                [low_total(*[part[k] for part in self.a]), low_total(*[part[k] for part in self.b])]
            )
            for k in range(1, self.deep)
        ]
        return self.out

    def lines(self):
        got = [sent(x, "z", k + 1) for k, x in enumerate(self.out)]
        return [
            total(*[part[0] for part in side], *[x[k] for x in got])
            for k, side in enumerate((self.a, self.b))
        ]


class Gathered:
    def __init__(self, low):
        self.low = low

    def after(self, *others):
        (self.a, self.b), _ = lax.optimization_barrier(((self.a, self.b), others))
        return self

    def lines(self):
        lines, rows = lax.axis_size("dp") // LINES, self.low.shape[0] // 2
        parts = [self.low] + [sent(self.low, "z", lines - k) for k in range(1, lines)]
        self.a = jnp.stack([part[:rows] for part in parts])
        self.b = jnp.stack([part[rows:] for part in parts])
        return [self.a, self.b]

    def first(self):
        self.a = jnp.stack([self.a, sent(self.a, "x")])
        self.b = jnp.stack([self.b, sent(self.b, "y")])
        return [self.a, self.b]

    def second(self):
        both = [self.a, sent(self.a, "y")], [self.b, sent(self.b, "x")]
        both = jnp.stack([jnp.stack(side) for side in both])
        self.mine = both.reshape((2, -1) + both.shape[4:])
        return [self.mine]

    def cores(self):
        return [self.mine, sent(self.mine, "c")]


def reduced_whole(parts, own_rows):
    own = []
    for keep, send in zip(parts[:2], parts[2:]):
        both = jnp.stack([keep, send], 1)[:, :, 0, 0]
        both = both.reshape((lax.axis_size("mp"), lax.axis_size("dp"), -1, keep.shape[-1]))
        both = lax.psum_scatter(both, "mp", scatter_dimension=0, tiled=True)
        both = lax.psum_scatter(both, "dp", scatter_dimension=1, tiled=True)
        own.append(both.reshape(own_rows, keep.shape[-1]).astype(f32))
    return own


def spread(x):
    return lax.all_to_all(x, ("dp", "mp"), 0, 0, tiled=True)


def passed_along(x, by):
    peers = lax.axis_size("mp")
    pairs = [(i, i + by) for i in range(peers) if 0 <= i + by < peers]
    return lax.ppermute(x, "mp", pairs)


def call(kernel, outs, args, scratch=(), us=1, after=(), out_any=(), name=None):
    whole = pl.BlockSpec(memory_space=pltpu.VMEM)
    specs, arrays = [], []
    for arg in args:
        array, space = arg if isinstance(arg, tuple) else (arg, pltpu.VMEM)
        specs.append(pl.BlockSpec(memory_space=space))
        arrays.append(array)
    used = len(arrays)
    arrays += list(after)
    specs += [pl.BlockSpec(memory_space=pl.ANY)] * len(after)

    def run(*refs):
        kernel(*refs[:used], *refs[len(arrays) :])

    return pl.pallas_call(
        run,
        out_shape=[jax.ShapeDtypeStruct(shape, dtype) for shape, dtype in outs],
        in_specs=specs,
        out_specs=[pl.BlockSpec(memory_space=pl.ANY) if k in out_any else whole for k in range(len(outs))],
        scratch_shapes=list(scratch),
        compiler_params=pltpu.CompilerParams(vmem_limit_bytes=56 * 1024 * 1024),
        cost_estimate=pl.CostEstimate(
            flops=int(us * 1.15e9), bytes_accessed=int(us * 1e6), transcendentals=0
        ),
        name=name,
    )(*arrays)


def fetched(weights, which, lo, hi, buf, sem):
    copies = [
        pltpu.make_async_copy(weights.at[:, m, which, :, lo:hi], buf.at[m], sem.at[m])
        for m in range(buf.shape[0])
    ]
    for copy in copies:
        copy.start()
    return copies


def buffers(weights, *widths):
    deep, n_mp, _, rows, _ = weights.shape
    out = []
    for width in widths:
        out.append(pltpu.VMEM((n_mp, deep, rows, width), bf16))
        out.append(pltpu.SemaphoreType.DMA((n_mp,)))
    return out


def block(buf, m, lanes=slice(None)):
    part = buf[m, :, :, lanes]
    return part.reshape(part.shape[0] * part.shape[1], part.shape[2])


def aligned(at):
    return pl.ds(pl.multiple_of(at, LANES), LANES)


def pieces(spot):
    for c in range(CORES):
        for x in range(COLS):
            if spot is None:
                yield c, x, x * CORES + c
                continue
            yield c, x, ((spot[1] + x) % COLS) * CORES + (spot[0] + c) % CORES


def write_whole(to, half, m, grad):
    rows = to.shape[3]
    for k in range(to.shape[0]):
        to[k, m, half] = grad[rows * k : rows * k + rows].astype(bf16)


def write_piece(spot, parts, half, c, x, grad):
    to = parts[half + 2 * c]
    _, deep, lines, _, _ = to.shape
    rows = D // (lines * deep)
    grad = grad.astype(bf16)
    for z in range(lines):
        for y in range(deep):
            at = (z * deep + y) * rows
            to[x, (y + deep - spot[2]) % deep, (z + lines - spot[3]) % lines] = grad[at : at + rows]


def nn(left, right):
    return jnp.dot(left, right, preferred_element_type=f32)


def nt(left, right):
    return lax.dot_general(left, right, (((1,), (1,)), ((), ())), preferred_element_type=f32)


def tn(left, right):
    return lax.dot_general(left, right, (((0,), (0,)), ((), ())), preferred_element_type=f32)


def sigmoid(v):
    return 1.0 / (1.0 + jnp.exp(-v))


def layer_norm(x, gain, shift):
    centered = x - jnp.mean(x, -1, keepdims=True)
    rstd = lax.rsqrt(jnp.mean(centered * centered, -1, keepdims=True) + norm_eps)
    return centered * rstd * gain + shift


def layer_norm_back(x, gain, grad):
    centered = x - jnp.mean(x, -1, keepdims=True)
    rstd = lax.rsqrt(jnp.mean(centered * centered, -1, keepdims=True) + norm_eps)
    xhat = centered * rstd
    g = grad * gain
    dx = rstd * (
        g - jnp.mean(g, -1, keepdims=True) - xhat * jnp.mean(g * xhat, -1, keepdims=True)
    )
    return dx, jnp.sum(grad * xhat, 0, keepdims=True), jnp.sum(grad, 0, keepdims=True)


def eight(x):
    rows = x.shape[0] // 8
    return jnp.sum(x.reshape(rows, 8, x.shape[1]), 0)


def flip_matrix(size):
    at = lax.broadcasted_iota(jnp.int32, (size, size), 0)
    to = lax.broadcasted_iota(jnp.int32, (size, size), 1)
    return (at + to == size - 1).astype(bf16)


def first_row(shard, device):
    return lax.shift_left(lax.shift_right_logical(shard * device, 11), 4)


def rows_at(at, rows):
    return pl.ds(pl.multiple_of(at, 16), rows)


def piece_place(spot, c, half, q):
    i, j, z = q // 8, (q // 4) % 2, q % 4
    y, x = (j, i) if half else (i, j)
    dp = ((spot[3] + z) % 4) * LINES + (spot[2] + y) % LINES
    return dp, ((spot[1] + x) % COLS) * CORES + (spot[0] + c) % CORES


def unpack_kernel(
    shard, spot, mine_ref, other_ref, taps_ref, one_ref, pw_ref, lin_ref, head_ref, vec_ref, flat
):
    flat[...] = jnp.zeros_like(flat)
    rows = mine_ref.shape[2]
    for c, ref in enumerate((mine_ref, other_ref)):
        for half in range(2):

            def step(q, carry, c=c, ref=ref, half=half):
                dp, mp = piece_place(spot, c, half, q)
                at = first_row(shard, dp * (COLS * CORES) + mp) + rows * half
                flat[rows_at(at, rows), :] += ref[half, q].astype(f32)
                return carry

            lax.fori_loop(0, ref.shape[1], step, 0)
    unpack_flat(flat, taps_ref, one_ref, pw_ref, lin_ref, head_ref, vec_ref)


def unpack_whole_kernel(
    shard, all_ref, taps_ref, one_ref, pw_ref, lin_ref, head_ref, vec_ref, flat
):
    flat[...] = jnp.zeros_like(flat)
    rows = all_ref.shape[1]

    def step(device, carry):
        flat[rows_at(first_row(shard, device), rows), :] += all_ref[device].astype(f32)
        return carry

    lax.fori_loop(0, all_ref.shape[0], step, 0)
    unpack_flat(flat, taps_ref, one_ref, pw_ref, lin_ref, head_ref, vec_ref)


def unpack_flat(flat, taps_ref, one_ref, pw_ref, lin_ref, head_ref, vec_ref):
    one_ref[...] = jnp.zeros_like(one_ref)
    taps_ref[...] = jnp.zeros_like(taps_ref)
    vec_ref[...] = jnp.zeros_like(vec_ref)
    for h in range(2):
        lanes = slice(LANES * h, LANES * h + LANES)
        taps = flat[pl.ds(h, 27, stride=2), :]
        taps_ref[0:27, lanes] = taps
        padded = jnp.concatenate([taps[0:9], jnp.zeros((7, LANES), f32)], 0).astype(bf16)
        for k in range(8):
            one_ref[k, 16 * k : 16 * k + 16, lanes] = padded
        for k in range(2):
            part = flat[pl.ds(ROW_AT[1] + 512 * k + h, CHANNELS, stride=2), :]
            pw_ref[k, :, lanes] = part.astype(bf16)
    for j in range(4):
        lanes = slice(LANES * j, LANES * j + LANES)
        for f in range(F3):
            part = flat[pl.ds(ROW_AT[2] + 1024 * f + j, CHANNELS, stride=4), :]
            lin_ref[f, :, lanes] = part.astype(bf16)
        vec_ref[0:23, lanes] = flat[pl.ds(ROW_AT[4] + j, 23, stride=4), :]
    flip = flip_matrix(LANES)
    column = lax.broadcasted_iota(jnp.int32, (LANES, CPAD), 1)
    for q in range(D // LANES):
        at = ROW_AT[3] + 1025 * q
        wide = jnp.concatenate(
            [flat[pl.ds(at + c, LANES, stride=8), :] for c in range(CPAD // LANES)], 1
        )
        turned = nn(flip, wide.astype(bf16))
        turned = pltpu.roll(turned, CPAD - LANES + 1, 1, stride=1, stride_axis=0)
        turned = jnp.where(column < CLASSES, turned, 0.0)
        head_ref[LANES * q : LANES * q + LANES, :] = nn(flip, turned.astype(bf16)).astype(bf16)


def pack_kernel(shard, n_dp, spot, last_ref, dx_ref, dhead_ref, *refs):
    parts, flat = refs[:4], refs[4]
    dx = dx_ref[...]
    flat[0 : ROW_AT[2], :] = jnp.zeros((ROW_AT[2], LANES), f32)
    flat[ROW_AT[4] :, :] = jnp.zeros((flat.shape[0] - ROW_AT[4], LANES), f32)
    for f in range(F3):
        grad = tn(last_ref[f], dx)
        for j in range(4):
            flat[pl.ds(ROW_AT[2] + 1024 * f + j, CHANNELS, stride=4), :] = grad[
                :, LANES * j : LANES * j + LANES
            ]
    for q in range(D // LANES):
        at = ROW_AT[3] + 1025 * q
        turned = pltpu.roll(
            dhead_ref[LANES * q : LANES * q + LANES, :], 0, 1, stride=1, stride_axis=0
        )
        flat[pl.ds(at + 8, LANES, stride=8), :] = turned[:, 8 * LANES :]
        flat[at : at + 1, :] = turned[0:1, 0:LANES]
        flat[pl.ds(at + 8, LANES - 1, stride=8), :] += turned[1:, 0:LANES]
        for c in range(1, 8):
            flat[pl.ds(at + c, LANES, stride=8), :] = turned[:, LANES * c : LANES * c + LANES]
    _, deep, lines, rows, _ = parts[0].shape
    each = n_dp // (deep * lines)
    rows = rows // each
    for c in range(CORES):

        def step(q, carry, c=c):
            k = q % each
            z, y, x = (q // each) % lines, (q // (each * lines)) % deep, q // (each * lines * deep)
            mp = ((spot[1] + x) % COLS) * CORES + (spot[0] + c) % CORES
            dp = ((spot[3] + z) % lines) * deep + (spot[2] + y) % deep + k
            row = first_row(shard, dp * (COLS * CORES) + mp)
            for half in range(2):
                part = flat[rows_at(row + rows * half, rows), :]
                parts[half + 2 * c][x, y, z, rows_at(rows * k, rows), :] = part.astype(bf16)
            return carry

        lax.fori_loop(0, COLS * deep * lines * each, step, 0)


def stem_chunks(rows):
    for lane in range(0, CHANNELS, LANES):
        for at in range(0, rows, 48):
            yield slice(lane, lane + LANES), at


def stem_scratch(rows):
    return [
        pltpu.VMEM((5, 4 * rows, CHANNELS), f32),
        pltpu.VMEM((F2, 2 * rows, CHANNELS), f32),
        pltpu.VMEM((rows + 8, CHANNELS), f32),
        pltpu.VMEM((rows - EDGE, F3 * CHANNELS), bf16),
        pltpu.VMEM((F3, CHANNELS, D), bf16),
        pltpu.VMEM((F2, 2 * rows, CHANNELS), bf16),
        pltpu.SemaphoreType.DMA((2,)),
    ]


def first_rows(win_ref, one_ref, f):
    return jax.nn.relu(nn(win_ref[f // 8], one_ref[f % 8]))


def staged(sources, targets, sem):
    copies = [pltpu.make_async_copy(s, t, sem.at[k]) for k, (s, t) in enumerate(zip(sources, targets))]
    for copy in copies:
        copy.start()
    return copies


def stem_kernel(
    win_ref,
    one_ref,
    taps_ref,
    pw_ref,
    lin_hbm,
    x0_ref,
    front_hbm,
    mid_ref,
    last_ref,
    t_ref,
    r_ref,
    lag_ref,
    flat,
    lin_ref,
    front_ref,
    sem,
):
    rows = lag_ref.shape[0] - 8
    (lin_copy,) = staged([lin_hbm], [lin_ref], sem.at[pl.ds(0, 1)])
    lag_ref[0:8, :] = jnp.zeros((8, CHANNELS), f32)
    t_ref[4] = jnp.zeros_like(t_ref[4])

    def second(slots, to):
        for lanes, at in stem_chunks(rows):

            def tap(k):
                return taps_ref[k : k + 1, lanes]

            lag, even, odd = 0.0, 0.0, 0.0
            for df, slot in enumerate(slots):
                t0, t1, t2, t3 = (
                    t_ref[slot, a * rows + at : a * rows + at + 48, lanes] for a in range(4)
                )
                lag += t3 * tap(9 + df)
                even += t0 * tap(12 + df) + t1 * tap(15 + df)
                odd += t1 * tap(9 + df) + t2 * tap(12 + df) + t3 * tap(15 + df)
            lag_ref[8 + at : 56 + at, lanes] = lag
            even += lag_ref[7 + at : 55 + at, lanes]
            front_ref[to, at : at + 48, lanes] = even.astype(bf16)
            front_ref[to, rows + at : rows + at + 48, lanes] = odd.astype(bf16)

    def step_front(f, carry):
        for k in range(4):
            t_ref[k] = first_rows(win_ref, one_ref, 4 * f + k)
        second((4, 0, 1), 2 * f)
        second((1, 2, 3), 2 * f + 1)
        t_ref[4] = t_ref[3]
        return carry

    lax.fori_loop(0, F3, step_front, 0)

    def step_point(f, carry):
        for k in range(4):
            r_ref[4 * f + k] = jax.nn.relu(nn(front_ref[4 * f + k], pw_ref[0]))
        return carry

    lax.fori_loop(0, F2 // 4, step_point, 0)

    front_copy = pltpu.make_async_copy(front_ref, front_hbm, sem.at[1])
    front_copy.start()

    def third(f, whole):
        for lanes, at in stem_chunks(rows):

            def tap(k):
                return taps_ref[k : k + 1, lanes]

            lag, out = 0.0, 0.0
            for df in range(0 if whole else 1, 3):
                slot = 2 * f - 1 + df
                even = r_ref[slot, at : at + 48, lanes]
                odd = r_ref[slot, rows + at : rows + at + 48, lanes]
                lag += odd * tap(18 + df)
                out += even * tap(21 + df) + odd * tap(24 + df)
            lag_ref[8 + at : 56 + at, lanes] = lag
            out += lag_ref[7 + at : 55 + at, lanes]
            skip = max(0, EDGE - at)
            mid_ref[f, at + skip - EDGE : at + 48 - EDGE, lanes] = out[skip:].astype(bf16)

    third(0, False)

    def step_mid(f, carry):
        third(f, True)
        return carry

    lax.fori_loop(1, F3, step_mid, 0)
    for f in range(F3):
        last = jax.nn.relu(nn(mid_ref[f], pw_ref[1])).astype(bf16)
        last_ref[f] = last
        flat[:, CHANNELS * f : CHANNELS * f + CHANNELS] = last
    lin_copy.wait()
    x0_ref[...] = nn(flat[...], lin_ref[...].reshape(F3 * CHANNELS, D))
    front_copy.wait()


def back_scratch(rows):
    return [
        pltpu.VMEM((F3, rows - EDGE, CHANNELS), bf16),
        pltpu.VMEM((F3 + 1, rows + 8, CHANNELS), f32),
        pltpu.VMEM((F2 + 1, 3 * rows, CHANNELS), f32),
        pltpu.VMEM((F2, 2 * rows, CHANNELS), f32),
        pltpu.VMEM((F2, 2 * rows, CHANNELS), bf16),
        pltpu.VMEM((2, 4 * rows, CHANNELS), f32),
        pltpu.VMEM((F2, 8 * rows, CHANNELS), bf16),
        pltpu.VMEM((F3, CHANNELS, D), bf16),
        pltpu.VMEM((F3, rows - EDGE, CHANNELS), bf16),
        pltpu.VMEM((F3, rows - EDGE, CHANNELS), bf16),
        pltpu.VMEM((F2, 2 * rows, CHANNELS), bf16),
        pltpu.VMEM((F1 // 8, 4 * rows, LANES), bf16),
        pltpu.VMEM((16, F2 * 8 * rows), bf16),
        pltpu.SemaphoreType.DMA((6,)),
    ]


def stem_back_kernel(
    dx_ref,
    win_hbm,
    turn_hbm,
    one_ref,
    taps_ref,
    pw_ref,
    lin_hbm,
    front_hbm,
    mid_hbm,
    last_hbm,
    g_pw,
    sums,
    g_one,
    g_last,
    g_mid,
    g_front,
    p_ref,
    q_ref,
    t_ref,
    s_ref,
    lin_ref,
    last_ref,
    mid_ref,
    front_ref,
    win_ref,
    turn_ref,
    sem,
):
    copies = staged(
        [lin_hbm, last_hbm, mid_hbm, front_hbm, win_hbm, turn_hbm],
        [lin_ref, last_ref, mid_ref, front_ref, win_ref, turn_ref],
        sem,
    )
    rows = g_mid.shape[1] - 8
    tokens = rows - EDGE
    sums[...] = jnp.zeros_like(sums)
    g_one[...] = jnp.zeros_like(g_one)
    g_mid[:, 0:EDGE, :] = jnp.zeros((F3 + 1, EDGE, CHANNELS), f32)
    g_mid[:, rows:, :] = jnp.zeros((F3 + 1, 8, CHANNELS), f32)
    g_mid[F3] = jnp.zeros_like(g_mid[F3])
    g_front[F2] = jnp.zeros_like(g_front[F2])
    dx = dx_ref[...]
    copies[0].wait()
    copies[1].wait()
    for f in range(F3):
        grad = nt(dx, lin_ref[f])
        grad = jnp.where(last_ref[f].astype(f32) > 0, grad, 0.0).astype(bf16)
        g_last[f] = grad
    for f in range(F3):
        g_mid[f, EDGE:rows, :] = nt(g_last[f], pw_ref[1])
    whole = (F3 * tokens, CHANNELS)
    copies[2].wait()
    g_pw[1] = tn(mid_ref[...].reshape(whole), g_last[...].reshape(whole))

    copies[3].wait()

    def step_point(f, carry):
        for k in range(4):
            p_ref[4 * f + k] = jax.nn.relu(nn(front_ref[4 * f + k], pw_ref[0]))
        return carry

    lax.fori_loop(0, F2 // 4, step_point, 0)

    def step_mid(f, carry):
        for odd in range(2):
            uses = [(f, 2), (f + 1, 0)] if odd else [(f, 1)]
            here = 2 * f + odd
            for lane in range(0, CHANNELS, LANES):
                lanes = slice(lane, lane + LANES)

                def tap(k):
                    return taps_ref[k : k + 1, lanes]

                found = {}
                for at in range(0, rows, 48):
                    p_even = p_ref[here, at : at + 48, lanes]
                    p_odd = p_ref[here, rows + at : rows + at + 48, lanes]
                    d_even, d_odd = 0.0, 0.0
                    for which, df in uses:
                        g = g_mid[which, at : at + 48, lanes]
                        g_up = g_mid[which, at + 1 : at + 49, lanes]
                        d_even += g * tap(21 + df)
                        d_odd += g * tap(24 + df) + g_up * tap(18 + df)
                        for k, x in ((df, g_up * p_odd), (3 + df, g * p_even), (6 + df, g * p_odd)):
                            found[k] = found.get(k, 0.0) + eight(x)
                    q_ref[here, at : at + 48, lanes] = jnp.where(p_even > 0, d_even, 0.0).astype(bf16)
                    q_ref[here, rows + at : rows + at + 48, lanes] = jnp.where(
                        p_odd > 0, d_odd, 0.0
                    ).astype(bf16)
                for k, x in found.items():
                    sums[9 + k, :, lanes] += x
        return carry

    lax.fori_loop(0, F3, step_mid, 0)

    def step_back(f, carry):
        for k in range(4):
            grad = nt(q_ref[4 * f + k], pw_ref[0])
            g_front[4 * f + k, 0 : 2 * rows, :] = grad
            g_front[4 * f + k, 2 * rows :, :] = pltpu.roll(grad[:rows], rows - 1, 0)
        size = (8 * rows, CHANNELS)
        grad = tn(front_ref[pl.ds(4 * f, 4)].reshape(size), q_ref[pl.ds(4 * f, 4)].reshape(size))
        g_pw[0] = jnp.where(f == 0, grad, g_pw[0] + grad)
        return carry

    lax.fori_loop(0, F2 // 4, step_back, 0)

    copies[4].wait()
    copies[5].wait()

    def step_front(f, carry):
        for odd in range(2):
            t_ref[odd] = first_rows(win_ref, one_ref, 2 * f + odd)
        for odd in range(2):
            uses = [(f, 2), (f + 1, 0)] if odd else [(f, 1)]
            for lane in range(0, CHANNELS, LANES):
                lanes = slice(lane, lane + LANES)

                def tap(k):
                    return taps_ref[k : k + 1, lanes]

                found = {}
                for at in range(0, rows, 48):
                    t0, t1, t2, t3 = (
                        t_ref[odd, a * rows + at : a * rows + at + 48, lanes] for a in range(4)
                    )
                    d = [0.0] * 4
                    for which, df in uses:
                        e = g_front[which, at : at + 48, lanes]
                        o = g_front[which, rows + at : rows + at + 48, lanes]
                        e_up = g_front[which, 2 * rows + at : 2 * rows + at + 48, lanes]
                        d[0] += e * tap(12 + df)
                        d[1] += e * tap(15 + df) + o * tap(9 + df)
                        d[2] += o * tap(12 + df)
                        d[3] += o * tap(15 + df) + e_up * tap(9 + df)
                        for k, x in (
                            (df, t1 * o + t3 * e_up),
                            (3 + df, t0 * e + t2 * o),
                            (6 + df, t1 * e + t3 * o),
                        ):
                            found[k] = found.get(k, 0.0) + eight(x)
                    for a, (t, grad) in enumerate(zip((t0, t1, t2, t3), d)):
                        to = (4 * odd + a) * rows + at
                        s_ref[f, to : to + 48, lanes] = jnp.where(t > 0, grad, 0.0).astype(bf16)
                for k, x in found.items():
                    sums[k, :, lanes] += x

        return carry

    lax.fori_loop(0, F2, step_front, 0)
    part = F2 // 4
    for k in range(4):
        at = part * 8 * rows
        g_one[...] += nn(
            turn_ref[:, k * at : (k + 1) * at],
            s_ref[part * k : part * (k + 1)].reshape(at, CHANNELS),
        )


def stem_rows_kernel(
    g_pw, sums, g_one, vg_last, vg_conv, vg_mid, vg_att, out_ref, flat
):
    taps = jnp.concatenate(
        [g_one[0:9, :]]
        + [jnp.sum(sums[k], 0, keepdims=True) for k in range(18)],
        0,
    )
    order = [
        (vg_last, 2),
        (vg_last, 0),
        (vg_conv, 0),
        (vg_mid, 2),
        (vg_mid, 0),
        (vg_last, 3),
        (vg_last, 1),
        (vg_conv, 1),
        (vg_mid, 3),
        (vg_mid, 1),
        (vg_mid, 4),
        (vg_mid, 5),
        (vg_att, 0),
        (vg_att, 1),
    ] + [(vg_conv, k) for k in range(2, 11)]
    flat[ROW_AT[2] + ROWS[4] - 8 :, :] = jnp.zeros((flat.shape[0] - ROW_AT[2] - ROWS[4] + 8, LANES), f32)
    for h in range(2):
        lanes = slice(LANES * h, LANES * h + LANES)
        flat[pl.ds(h, 27, stride=2), :] = taps[:, lanes]
        for k in range(2):
            flat[pl.ds(ROW_AT[1] + 512 * k + h, CHANNELS, stride=2), :] = g_pw[k, :, lanes]
    for k, (ref, row) in enumerate(order):
        for j in range(4):
            at = ROW_AT[2] + 4 * k + j
            flat[at : at + 1, :] = ref[row : row + 1, LANES * j : LANES * j + LANES]
    out_ref[...] = flat[...].astype(bf16)


def ffn_forward(x, vec_ref, which, win, wout, pre_ref, normed_ref):
    normed = layer_norm(x, vec_ref[which : which + 1, :], vec_ref[which + 5 : which + 6, :])
    normed = normed.astype(bf16)
    normed_ref[...] = normed
    total = jnp.zeros_like(x)
    (in_copies, in_buf), (out_copies, out_buf) = win, wout
    for m in range(NPIECE):
        in_copies[m].wait()
        pre = nn(normed, block(in_buf, m))
        pre_ref[m] = pre
        out_copies[m].wait()
        total += nt((pre * sigmoid(pre)).astype(bf16), block(out_buf, m))
    return x + 0.5 * total


def ffn_backward(spot, grad, x, vec_ref, which, in_buf, out_buf, pre_ref, normed_ref, parts):
    low = (0.5 * grad).astype(bf16)
    back = jnp.zeros_like(x)
    for c, col, m in pieces(spot):

        def write(half, piece):
            if spot is None:
                write_whole(parts, half, m, piece)
            else:
                write_piece(spot, parts, half, c, col, piece)

        pre = pre_ref[m]
        sig = sigmoid(pre)
        write(1, tn(low, (pre * sig).astype(bf16)))
        g_pre = (nn(low, block(out_buf, m)) * (sig * (1.0 + pre * (1.0 - sig)))).astype(bf16)
        write(0, tn(normed_ref[...], g_pre))
        back += nt(g_pre, block(in_buf, m))
    dx, gain, shift = layer_norm_back(x, vec_ref[which : which + 1, :], back)
    return grad + dx, gain, shift


def first_kernel(
    weights,
    x_ref,
    vec_ref,
    x1_ref,
    pre_ref,
    n1_ref,
    n2_ref,
    in_buf,
    in_sem,
    out_buf,
    out_sem,
):
    win = fetched(weights, 0, 0, D, in_buf, in_sem)
    wout = fetched(weights, 1, 0, D, out_buf, out_sem)
    x1 = ffn_forward(x_ref[...], vec_ref, 0, (win, in_buf), (wout, out_buf), pre_ref, n1_ref)
    x1_ref[...] = x1
    n2_ref[...] = layer_norm(x1, vec_ref[1:2, :], vec_ref[6:7, :]).astype(bf16)


def position_kernel(
    weights, table_ref, n2_ref, vec_ref, pe_ref, qu_ref, qv_ref, buf, sem, q_buf, q_sem
):
    q_copies = fetched(weights, 2, 0, LANES, q_buf, q_sem)
    copies = fetched(weights, 2, 3 * LANES, 4 * LANES, buf, sem)
    for m in range(NPIECE):
        lanes = slice(LANES * m, LANES * m + LANES)
        q_copies[m].wait()
        query = nn(n2_ref[...], block(q_buf, m))
        qu_ref[:, lanes] = (query + vec_ref[12:13, lanes]).astype(bf16)
        qv_ref[:, lanes] = (query + vec_ref[13:14, lanes]).astype(bf16)
        copies[m].wait()
        pe_ref[:, lanes] = nn(table_ref[...], block(buf, m)).astype(bf16)


def head_lanes(h):
    return h // 2, HEAD_DIM * (h % 2), slice(HEAD_DIM * h, HEAD_DIM * h + HEAD_DIM)


def attention_kernel(
    weights,
    all_ref,
    x1_ref,
    qu_ref,
    qv_ref,
    pe_ref,
    vec_ref,
    keep_ref,
    valid_ref,
    x2_ref,
    kv_ref,
    prob_ref,
    att_ref,
    n3_ref,
    ga_ref,
    gb_ref,
    gated_ref,
    low_ref,
    high_ref,
    kv_buf,
    kv_sem,
    abo_buf,
    abo_sem,
):
    kv_copies = fetched(weights, 2, LANES, 3 * LANES, kv_buf, kv_sem)
    abo_copies = fetched(weights, 3, 0, 3 * LANES, abo_buf, abo_sem)
    rows, length = x1_ref.shape[0], all_ref.shape[0]
    width = rows + length
    for m in range(NPIECE):
        kv_copies[m].wait()
        kv_ref[m] = nn(all_ref[...], block(kv_buf, m)).astype(bf16)
    keep = keep_ref[...] > 0
    for h in range(HEADS):
        m, at, lanes = head_lanes(h)
        raw = nt(qu_ref[:, lanes], kv_ref[m, :, at : at + HEAD_DIM])
        far = nt(qv_ref[:, lanes], pe_ref[:, lanes])
        far = pltpu.roll(far, width - rows + 1, 1, stride=1, stride_axis=0)
        scores = jnp.where(keep, (raw + far[:, :length]) * 0.125, -1e30)
        expo = jnp.exp(scores - jnp.max(scores, -1, keepdims=True))
        prob = expo / jnp.sum(expo, -1, keepdims=True)
        prob_ref[h] = prob
        value = kv_ref[m, :, LANES + at : LANES + at + HEAD_DIM]
        att_ref[:, lanes] = nn(prob.astype(bf16), value).astype(bf16)
    x2 = x1_ref[...]
    for m in range(NPIECE):
        abo_copies[m].wait()
        lanes = slice(LANES * m, LANES * m + LANES)
        x2 += nt(att_ref[:, lanes], block(abo_buf, m, slice(2 * LANES, 3 * LANES)))
    x2_ref[...] = x2
    normed = layer_norm(x2, vec_ref[2:3, :], vec_ref[7:8, :]).astype(bf16)
    n3_ref[...] = normed
    for m in range(NPIECE):
        lanes = slice(LANES * m, LANES * m + LANES)
        gates = nn(normed, block(abo_buf, m, slice(0, 2 * LANES)))
        ga, gb = gates[:, :LANES], gates[:, LANES:]
        ga_ref[:, lanes] = ga
        gb_ref[:, lanes] = gb
        gated_ref[:, lanes] = ga * sigmoid(gb) * valid_ref[...]
    low_ref[...] = gated_ref[0:HALO, :]
    high_ref[...] = gated_ref[rows - HALO :, :]


def write_stats(stat_ref, first, second, number):
    rows = [x[:, LANES * k : LANES * k + LANES] for x in (first, second) for k in range(4)]
    rows.append(jnp.broadcast_to(number, (8, LANES)))
    stat_ref[...] = jnp.broadcast_to(jnp.concatenate(rows, 0)[None], stat_ref.shape)


def read_stats(stat_ref):
    whole = jnp.sum(stat_ref[...], 0)
    first = jnp.concatenate([whole[k : k + 1] for k in range(4)], 1)
    second = jnp.concatenate([whole[k : k + 1] for k in range(4, 8)], 1)
    return first, second, whole[8:9, 0:1]


def conv_kernel(prev_ref, gated_ref, next_ref, vec_ref, valid_ref, hidden_ref, stat_ref, wide):
    rows = gated_ref.shape[0]
    wide[0:HALO, :] = prev_ref[...]
    wide[HALO : HALO + rows, :] = gated_ref[...]
    wide[HALO + rows :, :] = next_ref[...]
    at = HALO - KERNEL // 2
    hidden = sum(wide[at + k : at + k + rows, :] * vec_ref[14 + k : 15 + k, :] for k in range(KERNEL))
    hidden_ref[...] = hidden
    valid = valid_ref[...]
    kept = hidden * valid
    write_stats(
        stat_ref,
        jnp.sum(kept, 0, keepdims=True),
        jnp.sum(kept * hidden, 0, keepdims=True),
        jnp.sum(valid, 0, keepdims=True),
    )


def middle_kernel(
    weights,
    more,
    hidden_ref,
    stat_ref,
    x2_ref,
    head_ref,
    vec_ref,
    label_ref,
    weight_ref,
    valid_ref,
    grad_ref,
    g_head_ref,
    dx3_ref,
    act_ref,
    dy_ref,
    yhat_ref,
    low_ref,
    high_ref,
    part_ref,
    vgrad_ref,
    pre_ref,
    n4_ref,
    c_buf,
    c_sem,
    in_buf,
    in_sem,
    out_buf,
    out_sem,
):
    c_copies = fetched(weights, 3, 3 * LANES, 4 * LANES, c_buf, c_sem)
    win = fetched(more, 0, 0, D, in_buf, in_sem), in_buf
    wout = fetched(more, 1, 0, D, out_buf, out_sem), out_buf
    rows = x2_ref.shape[0]
    first, second, count = read_stats(stat_ref)
    mean = first / count
    inverse = lax.rsqrt(second / count - mean * mean + norm_eps)
    yhat = (hidden_ref[...] - mean) * inverse
    yhat_ref[...] = yhat
    c = yhat * vec_ref[10:11, :] + vec_ref[11:12, :]
    sig = sigmoid(c)
    act = (c * sig).astype(bf16)
    act_ref[...] = act
    x3 = x2_ref[...]
    for m in range(NPIECE):
        c_copies[m].wait()
        x3 += nt(act[:, LANES * m : LANES * m + LANES], block(c_buf, m))
    x4 = ffn_forward(x3, vec_ref, 3, win, wout, pre_ref, n4_ref)
    normed = layer_norm(x4, vec_ref[4:5, :], vec_ref[9:10, :]).astype(bf16)
    logits = nn(normed, head_ref[...])
    column = lax.broadcasted_iota(jnp.int32, logits.shape, 1)
    logits = jnp.where(column < CLASSES, logits, -1e30)
    top = jnp.max(logits, -1, keepdims=True)
    total = top + jnp.log(jnp.sum(jnp.exp(logits - top), -1, keepdims=True))
    hit = column == label_ref[...]
    picked = jnp.sum(jnp.where(hit, logits, 0.0), -1, keepdims=True)
    weight = weight_ref[...]
    loss = jnp.sum(weight * (total - picked), 0, keepdims=True)
    g_logits = (jnp.exp(logits - total) - hit.astype(f32)) * (weight / count)
    g_logits = g_logits.astype(bf16)
    g_head_ref[...] = tn(normed, g_logits)
    dx4, gain, shift = layer_norm_back(x4, vec_ref[4:5, :], nt(g_logits, head_ref[...]))
    vgrad_ref[0:1, :] = gain
    vgrad_ref[1:2, :] = shift
    dx3, gain, shift = ffn_backward(
        None, dx4, x3, vec_ref, 3, in_buf, out_buf, pre_ref, n4_ref, grad_ref
    )
    vgrad_ref[2:3, :] = gain
    vgrad_ref[3:4, :] = shift
    dx3_ref[...] = dx3
    low = dx3.astype(bf16)
    valid = valid_ref[...]
    parts = []
    for m in range(NPIECE):
        lanes = slice(LANES * m, LANES * m + LANES)
        slope = sig[:, lanes] * (1.0 + c[:, lanes] * (1.0 - sig[:, lanes]))
        dc = nn(low, block(c_buf, m)) * slope
        vgrad_ref[4:5, lanes] = jnp.sum(dc * yhat[:, lanes], 0, keepdims=True)
        vgrad_ref[5:6, lanes] = jnp.sum(dc, 0, keepdims=True)
        dy = dc * vec_ref[10:11, lanes]
        dy_ref[:, lanes] = dy
        kept = dy * valid
        parts.append(
            (
                jnp.sum(kept, 0, keepdims=True),
                jnp.sum(kept * yhat[:, lanes], 0, keepdims=True),
            )
        )
    for k, ref in enumerate((dy_ref, yhat_ref)):
        low_ref[HALO * k : HALO * k + HALO, :] = ref[0:HALO, :]
        high_ref[HALO * k : HALO * k + HALO, :] = ref[rows - HALO :, :]
    write_stats(
        part_ref,
        jnp.concatenate([a for a, _ in parts], 1),
        jnp.concatenate([b for _, b in parts], 1),
        loss,
    )


def conv_back_kernel(
    weights,
    dy_ref,
    yhat_ref,
    prev_ref,
    next_ref,
    part_ref,
    stat_ref,
    wide_valid_ref,
    gprev_ref,
    gated_ref,
    gnext_ref,
    ga_ref,
    gb_ref,
    x2_ref,
    dx3_ref,
    vec_ref,
    dgate_ref,
    dx2_ref,
    vgrad_ref,
    loss_ref,
    wide,
    wide_y,
    dh,
    buf,
    sem,
):
    copies = fetched(weights, 3, 0, 2 * LANES, buf, sem)
    rows = dy_ref.shape[0]
    first, second, count = read_stats(stat_ref)
    mean = first / count
    inverse = lax.rsqrt(second / count - mean * mean + norm_eps)
    first, second, loss = read_stats(part_ref)
    loss_ref[...] = loss / count
    wide[0:HALO, :] = prev_ref[0:HALO, :]
    wide[HALO : HALO + rows, :] = dy_ref[...]
    wide[HALO + rows :, :] = next_ref[0:HALO, :]
    wide_y[0:HALO, :] = prev_ref[HALO:, :]
    wide_y[HALO : HALO + rows, :] = yhat_ref[...]
    wide_y[HALO + rows :, :] = next_ref[HALO:, :]
    mean_part = (first + wide_y[...] * second) / count
    dh[...] = inverse * (wide[...] - wide_valid_ref[...] * mean_part)
    wide[0:HALO, :] = gprev_ref[...]
    wide[HALO : HALO + rows, :] = gated_ref[...]
    wide[HALO + rows :, :] = gnext_ref[...]
    half = KERNEL // 2
    own = dh[HALO : HALO + rows, :]
    d_gated = jnp.zeros((rows, D), f32)
    for k in range(KERNEL):
        d_gated += dh[HALO - k + half : HALO - k + half + rows, :] * vec_ref[14 + k : 15 + k, :]
        at = HALO + k - half
        vgrad_ref[2 + k : 3 + k, :] = jnp.sum(own * wide[at : at + rows, :], 0, keepdims=True)
    d_gated = d_gated * wide_valid_ref[HALO : HALO + rows, :]
    sig = sigmoid(gb_ref[...])
    dga = (d_gated * sig).astype(bf16)
    dgb = (d_gated * ga_ref[...] * sig * (1.0 - sig)).astype(bf16)
    back = jnp.zeros((rows, D), f32)
    for m in range(NPIECE):
        lanes = slice(LANES * m, LANES * m + LANES)
        both = jnp.concatenate([dga[:, lanes], dgb[:, lanes]], 1)
        dgate_ref[m] = both
        copies[m].wait()
        back += nt(both, block(buf, m))
    dx, gain, shift = layer_norm_back(x2_ref[...], vec_ref[2:3, :], back)
    vgrad_ref[0:1, :] = gain
    vgrad_ref[1:2, :] = shift
    dx2_ref[...] = dx3_ref[...] + dx


def back_kernel(
    weights,
    dx2_ref,
    prob_ref,
    kv_ref,
    qu_ref,
    qv_ref,
    pe_ref,
    dquery_ref,
    dkv_ref,
    dpe_ref,
    dall_ref,
    down_ref,
    vgrad_ref,
    dq,
    o_buf,
    o_sem,
    mix_buf,
    mix_sem,
):
    o_copies = fetched(weights, 3, 2 * LANES, 3 * LANES, o_buf, o_sem)
    mix_copies = fetched(weights, 2, 0, 3 * LANES, mix_buf, mix_sem)
    rows, length = dx2_ref.shape[0], dall_ref.shape[0]
    low = dx2_ref[...].astype(bf16)
    flip = flip_matrix(rows)
    turned_q = nn(flip, qv_ref[...]).astype(bf16)
    for h in range(HEADS):
        m, at, lanes = head_lanes(h)
        if at == 0:
            o_copies[m].wait()
            d_att = nn(low, block(o_buf, m)).astype(bf16)
        d_out = d_att[:, at : at + HEAD_DIM]
        prob = prob_ref[h]
        key = kv_ref[m, :, at : at + HEAD_DIM]
        value = kv_ref[m, :, LANES + at : LANES + at + HEAD_DIM]
        d_prob = nt(d_out, value)
        d_scores = prob * (d_prob - jnp.sum(prob * d_prob, -1, keepdims=True))
        d_raw = (d_scores * 0.125).astype(bf16)
        dkv_ref[m, :, LANES + at : LANES + at + HEAD_DIM] = tn(prob.astype(bf16), d_out).astype(bf16)
        dkv_ref[m, :, at : at + HEAD_DIM] = tn(d_raw, qu_ref[:, lanes]).astype(bf16)
        dq[0:rows, lanes] = nn(d_raw, key)
        turned = nn(flip, d_raw)
        turned = jnp.concatenate([turned, jnp.zeros((rows, rows), f32)], 1)
        turned = pltpu.roll(turned, 0, 1, stride=1, stride_axis=0).astype(bf16)
        dq[rows : 2 * rows, lanes] = nn(turned, pe_ref[:, lanes])
        dpe_ref[:, lanes] = tn(turned, turned_q[:, lanes]).astype(bf16)
    d_u, d_v = dq[0:rows, :], dq[rows : 2 * rows, :]
    vgrad_ref[0:1, :] = jnp.sum(d_u, 0, keepdims=True)
    vgrad_ref[1:2, :] = jnp.sum(d_v, 0, keepdims=True)
    straight = jnp.dot(
        flip.astype(f32), d_v, precision=lax.Precision.HIGHEST, preferred_element_type=f32
    )
    dquery = (d_u + straight).astype(bf16)
    dquery_ref[...] = dquery
    d_all = jnp.zeros((length, D), f32)
    d_own = jnp.zeros((rows, D), f32)
    for m in range(NPIECE):
        mix_copies[m].wait()
        d_own += nt(dquery[:, LANES * m : LANES * m + LANES], block(mix_buf, m, slice(0, LANES)))
        d_all += nt(dkv_ref[m], block(mix_buf, m, slice(LANES, 3 * LANES)))
    dall_ref[...] = d_all.astype(bf16)
    down_ref[...] = d_own


def mix_grad_kernel(
    spot,
    dx2_ref,
    dx3_ref,
    dgate_ref,
    n3_ref,
    act_ref,
    att_ref,
    n2_ref,
    all_ref,
    table_ref,
    dquery_ref,
    dkv_ref,
    dpe_ref,
    *parts,
):
    low = dx2_ref[...].astype(bf16)
    low_three = dx3_ref[...].astype(bf16)
    for c, x, m in pieces(spot):
        lanes = aligned(LANES * m)
        grads = [
            tn(n2_ref[...], dquery_ref[:, lanes]),
            tn(all_ref[...], dkv_ref[m]),
            tn(table_ref[...], dpe_ref[:, lanes]),
        ]
        write_piece(spot, parts, 0, c, x, jnp.concatenate(grads, 1))
        grads = [
            tn(n3_ref[...], dgate_ref[m]),
            tn(low, att_ref[:, lanes]),
            tn(low_three, act_ref[:, lanes]),
        ]
        write_piece(spot, parts, 1, c, x, jnp.concatenate(grads, 1))


def last_kernel(
    spot,
    weights,
    dx2_ref,
    d_all_ref,
    d_own_ref,
    x1_ref,
    x0_ref,
    pre_ref,
    n1_ref,
    vec_ref,
    a_ref,
    b_ref,
    a_send_ref,
    b_send_ref,
    dx0_ref,
    vgrad_ref,
    in_buf,
    in_sem,
    out_buf,
    out_sem,
):
    copies = fetched(weights, 0, 0, D, in_buf, in_sem)
    copies += fetched(weights, 1, 0, D, out_buf, out_sem)
    grad = total(*[d_all_ref[k] for k in range(d_all_ref.shape[0])]) + d_own_ref[...]
    dx, gain, shift = layer_norm_back(x1_ref[...], vec_ref[1:2, :], grad)
    vgrad_ref[0:1, :] = gain
    vgrad_ref[1:2, :] = shift
    for copy in copies:
        copy.wait()
    dx0, gain, shift = ffn_backward(
        spot,
        dx2_ref[...] + dx,
        x0_ref[...],
        vec_ref,
        0,
        in_buf,
        out_buf,
        pre_ref,
        n1_ref,
        (a_ref, b_ref, a_send_ref, b_send_ref),
    )
    vgrad_ref[2:3, :] = gain
    vgrad_ref[3:4, :] = shift
    dx0_ref[...] = dx0.astype(bf16)


def adam(state, grad, rate):
    first_new = beta_one * state[1] + (1.0 - beta_one) * grad
    second_new = beta_two * state[2] + (1.0 - beta_two) * grad * grad
    direction = (
        first_new
        / (1.0 - beta_one**STEP)
        / (jnp.sqrt(second_new / (1.0 - beta_two**STEP)) + adam_eps)
    )
    weight_new = state[0] - rate * (direction + decay_rate * state[0])
    return (weight_new, first_new, second_new)


def small_rate(positions):
    rate = jnp.full(positions.shape, small_rates[-1], f32)
    for k in range(3, -1, -1):
        rate = jnp.where(positions < sum(SIZES[: k + 1]), small_rates[k], rate)
    return rate


def mel_windows(mel, utter_len, rank, tokens):
    frame = rank * (8 * tokens) + jnp.arange(8 * tokens, dtype=jnp.int32)
    kept = jnp.where((frame < utter_len)[:, None], mel, jnp.zeros((), bf16))
    prior = passed_along(kept[-8:], 1)
    rows = tokens + EDGE
    field = jnp.concatenate([jnp.zeros((8 * (EDGE - 1), MEL), bf16), prior, kept], 0)
    field = field.reshape(rows, 8, MEL).transpose(1, 2, 0)
    lag = jnp.concatenate([jnp.zeros((1, MEL, 1), bf16), field[7:8, :, :-1]], 2)
    field = jnp.concatenate([lag, field], 0)
    field = jnp.pad(field, ((0, 0), (1, 1), (0, 0))).reshape(9, F1 + 1, 2, rows)
    bands = [field[:, :F1, 0], field[:, :F1, 1], field[:, 1:, 0]]
    taps = [bands[df][dt : dt + 7 : 2] for dt in range(3) for df in range(3)]
    taps = jnp.stack(taps + [jnp.zeros_like(taps[0])] * 7, 0)
    turned = taps.transpose(0, 2, 1, 3).reshape(16, F1 * 4 * rows)
    wide = taps.reshape(16, 4, F1 // 8, 8, rows).transpose(2, 1, 4, 3, 0)
    return wide.reshape(F1 // 8, 4 * rows, LANES), turned


def position_table(rank, rows, length):
    distance = (rows * rank + rows - 1 - jnp.arange(rows + length)).astype(f32)[:, None]
    inverse_freq = jnp.exp(jnp.arange(D // 2).astype(f32) * (-2.0 * math.log(10000.0) / D))
    angles = distance * inverse_freq[None, :]
    return jnp.concatenate([jnp.sin(angles), jnp.cos(angles)], 1).astype(bf16)


def gathered_heads(n2, planned_mesh):
    if not planned_mesh:
        return lax.all_gather(n2, "mp", axis=0, tiled=True)
    rows = n2.shape[0]
    pair = jnp.stack([n2, sent(n2, "x")])
    both = jnp.stack([pair, sent(pair, "c")])
    rank = lax.axis_index("mp")
    order = [(rank % 2, rank // 2)]
    whole = jnp.zeros((4, rows, D), bf16)
    c, x = order[0]
    for i in range(2):
        for j in range(2):
            at = ((x + j) % 2) * 2 + (c + i) % 2
            whole = lax.dynamic_update_slice(whole, both[i, j][None], (at, 0, 0))
    return whole.reshape(4 * rows, D)


def body(mel, lengths, alignment, loss_mask, ff_in, ff_out, mix_in, mix_out, small):
    n_dp, n_mp = lax.axis_size("dp"), lax.axis_size("mp")
    ndev = n_dp * n_mp
    plan = planned(n_dp, n_mp)
    rank, dp_rank = lax.axis_index("mp"), lax.axis_index("dp")
    device = lax.axis_index(("dp", "mp"))
    tokens = alignment.shape[1]
    length = tokens * n_mp
    rows = tokens + EDGE
    own_rows = ff_in.shape[2]
    shard = small.shape[1]
    half = -(-(-(-(shard + 16 * LANES - 1) // LANES)) // 32) * 16
    chunk = 2 * half
    flat_rows = max((shard * (ndev - 1)) // (16 * LANES) * 16 + chunk, NROWS)
    flat_rows = -(-flat_rows // 8) * 8
    if plan:
        spot = jnp.stack([rank % 2, rank // 2, dp_rank % 2, dp_rank // 2])
        deep, lines = LINES, n_dp // LINES
    else:
        spot = jnp.zeros((4,), jnp.int32)
        deep, lines = 1, 1
    spot = spot.astype(jnp.int32), pltpu.SMEM
    piece_rows = D // (deep * lines)
    small_rows = half * (n_dp // (deep * lines))

    row = first_row(shard, device)
    offset = shard * device - row * LANES
    small_low = lax.dynamic_update_slice_in_dim(
        jnp.zeros((chunk * LANES,), bf16), small[0].astype(bf16), offset, 0
    ).reshape(chunk, LANES)
    in_low = ff_in[0].astype(bf16)
    out_low = ff_out[0].astype(bf16).transpose(0, 2, 1)
    mix_low = mix_in[0].astype(bf16)
    mixo_low = mix_out[0].astype(bf16).transpose(0, 2, 1)
    qkvp_low = mix_low[:, 0:4].reshape(own_rows, 4 * LANES)
    abo_low = jnp.concatenate([mix_low[:, 4], mix_low[:, 5], mixo_low[0], mixo_low[1]], 1)
    def gathered(low):
        whole = lax.all_gather(jnp.stack(low), ("dp", "mp"), axis=0)
        whole = whole.reshape(n_dp, n_mp, len(low), own_rows, D)
        if not plan:
            whole = whole.transpose(1, 2, 0, 3, 4).reshape(1, n_mp, len(low), D, D)
        return whole

    big_all = gathered([in_low[0], out_low[0], qkvp_low, abo_low])
    more_all = gathered([in_low[1], out_low[1]])
    weights, more = (big_all, pl.ANY), (more_all, pl.ANY)
    utter_len = lengths[0]
    windows, windows_t = mel_windows(mel[0], utter_len, rank, tokens)
    table = position_table(rank, tokens, length)
    if plan:
        few_all = Gathered(small_low)
        few_all.lines(), few_all.after(windows, windows_t, table).first(), few_all.second()
        small_all = few_all.cores()
    else:
        small_all = [lax.all_gather(small_low, ("dp", "mp"), axis=0)]

    frames = jnp.arange(length, dtype=jnp.int32)
    keep_row = (8 * frames < utter_len).astype(f32)[None, :]
    wide_frame = rank * tokens - HALO + jnp.arange(tokens + 2 * HALO, dtype=jnp.int32)
    wide_valid = (wide_frame >= 0) & (wide_frame < length) & (8 * wide_frame < utter_len)
    wide_valid = wide_valid.astype(f32)[:, None]
    valid = wide_valid[HALO : HALO + tokens]
    weight = valid * loss_mask[0].astype(f32)[:, None]

    def split(each):
        return [((COLS, deep, lines, each, D), bf16)] * 4

    unpack = functools.partial(unpack_kernel if plan else unpack_whole_kernel, shard)
    taps, tap_one, pointwise, linear, head, vec = call(
        unpack,
        [
            ((32, CHANNELS), f32),
            ((8, LANES, CHANNELS), bf16),
            ((2, CHANNELS, CHANNELS), bf16),
            ((F3, CHANNELS, D), bf16),
            ((D, CPAD), bf16),
            ((24, D), f32),
        ],
        ([spot] if plan else []) + small_all,
        [pltpu.VMEM((flat_rows, LANES), f32)],
        us=7,
        name="unpack",
    )
    x0, front, mid, last = call(
        stem_kernel,
        [
            ((tokens, D), f32),
            ((F2, 2 * rows, CHANNELS), bf16),
            ((F3, tokens, CHANNELS), bf16),
            ((F3, tokens, CHANNELS), bf16),
        ],
        [windows, tap_one, taps, pointwise, (linear, pl.ANY)],
        stem_scratch(rows),
        us=13,
        out_any=(1,),
        name="stem",
    )
    x1, pre_one, n1, n2 = call(
        first_kernel,
        [
            ((tokens, D), f32),
            ((n_mp, tokens, D), f32),
            ((tokens, D), bf16),
            ((tokens, D), bf16),
        ],
        [weights, x0, vec],
        buffers(big_all, D, D),
        us=6,
        name="first",
    )
    n_all = gathered_heads(n2, plan)
    pe, qu, qv = call(
        position_kernel,
        [((tokens + length, D), bf16), ((tokens, D), bf16), ((tokens, D), bf16)],
        [weights, table, n2, vec],
        buffers(big_all, LANES, LANES),
        us=5,
        name="position",
    )
    x2, kv, prob, att, n3, ga, gb, gated, g_low, g_high = call(
        attention_kernel,
        [
            ((tokens, D), f32),
            ((n_mp, length, 2 * LANES), bf16),
            ((HEADS, tokens, length), f32),
            ((tokens, D), bf16),
            ((tokens, D), bf16),
            ((tokens, D), f32),
            ((tokens, D), f32),
            ((tokens, D), f32),
            ((HALO, D), f32),
            ((HALO, D), f32),
        ],
        [weights, n_all, x1, qu, qv, pe, vec, keep_row, valid],
        buffers(big_all, 2 * LANES, 3 * LANES),
        us=10,
        name="attention",
    )
    g_prev, g_next = passed_along(g_high, 1), passed_along(g_low, -1)
    stat_shape = ((ndev, 16, LANES), f32)
    wide = pltpu.VMEM((tokens + 2 * HALO, D), f32)
    hidden, stat = call(
        conv_kernel,
        [((tokens, D), f32), stat_shape],
        [g_prev, gated, g_next, vec, valid],
        [wide],
        us=2,
        name="conv",
    )
    stat = spread(stat)
    two, g_head, dx3, act, dy, yhat, b_low, b_high, part, vg_mid = call(
        middle_kernel,
        [
            ((n_dp if plan else 1, n_mp, 2, own_rows if plan else D, D), bf16),
            ((D, CPAD), f32),
            ((tokens, D), f32),
            ((tokens, D), bf16),
            ((tokens, D), f32),
            ((tokens, D), f32),
            ((2 * HALO, D), f32),
            ((2 * HALO, D), f32),
            stat_shape,
            ((6, D), f32),
        ],
        [weights, more, hidden, stat, x2, head, vec, alignment[0][:, None], weight, valid],
        [
            pltpu.VMEM((n_mp, tokens, D), f32),
            pltpu.VMEM((tokens, D), bf16),
            *buffers(big_all, LANES, D, D),
        ],
        us=13,
        name="middle",
    )
    b_prev, b_next = passed_along(b_high, 1), passed_along(b_low, -1)
    part = spread(part)
    if not plan:
        two = two.reshape(n_mp, 2, n_dp, own_rows, D).transpose(2, 0, 1, 3, 4)
    two = lax.psum_scatter(
        two.reshape(ndev, 2 * own_rows, D), ("dp", "mp"), scatter_dimension=0, tiled=True
    )
    own_in_two, own_out_two = two.reshape(2, own_rows, D).astype(f32)
    dgate, dx2, vg_conv, loss = call(
        conv_back_kernel,
        [
            ((n_mp, tokens, 2 * LANES), bf16),
            ((tokens, D), f32),
            ((11, D), f32),
            ((1, 1), f32),
        ],
        [
            weights,
            dy,
            yhat,
            b_prev,
            b_next,
            part,
            stat,
            wide_valid,
            g_prev,
            gated,
            g_next,
            ga,
            gb,
            x2,
            dx3,
            vec,
        ],
        [wide, wide, wide, *buffers(big_all, 2 * LANES)],
        us=4,
        name="conv_back",
    )
    dquery, dkv, dpe, d_all, d_own, vg_att = call(
        back_kernel,
        [
            ((tokens, D), bf16),
            ((n_mp, length, 2 * LANES), bf16),
            ((tokens + length, D), bf16),
            ((length, D), bf16),
            ((tokens, D), f32),
            ((2, D), f32),
        ],
        [weights, dx2, prob, kv, qu, qv, pe],
        [pltpu.VMEM((2 * tokens, D), f32), *buffers(big_all, LANES, 3 * LANES)],
        us=10,
        name="back",
    )
    if plan:
        pair = d_all.reshape(2, 2, tokens, D)
        core, col = rank % 2, rank // 2
        other = lax.dynamic_slice_in_dim(pair, 1 - core, 1, 1)[:, 0]
        own = lax.dynamic_slice_in_dim(pair, core, 1, 1)[:, 0]
        pair = low_total(own, sent(other, "c"))
        wait = [pair]
        other = lax.dynamic_slice_in_dim(pair, 1 - col, 1, 0)
        own = lax.dynamic_slice_in_dim(pair, col, 1, 0)
        d_mine = jnp.concatenate([own, sent(other, "x")], 0)
    else:
        d_mine = lax.psum_scatter(d_all, "mp", scatter_dimension=0, tiled=True)[None]
        wait = ()
    mix = call(
        mix_grad_kernel,
        split(piece_rows),
        [spot, dx2, dx3, dgate, n3, act, att, n2, n_all, table, dquery, dkv, dpe],
        us=7,
        after=wait,
        name="mix_grad",
    )
    mix_sum = Reduced(*mix)
    *one, dx0, vg_last = call(
        last_kernel,
        [*split(piece_rows), ((tokens, D), bf16), ((4, D), f32)],
        [spot, weights, dx2, d_mine, d_own, x1, x0, pre_one, n1, vec],
        buffers(big_all, D, D),
        us=8,
        after=mix[:1],
        name="last",
    )
    one_sum = Reduced(*one)
    few_parts = call(
        functools.partial(pack_kernel, shard, n_dp),
        [((COLS, deep, lines, small_rows, LANES), bf16)] * 4,
        [spot, last, dx0, g_head],
        [pltpu.VMEM((flat_rows, LANES), f32)],
        us=5,
        after=mix_sum.cores() if plan else (),
        name="pack",
    )
    few_sum = Reduced(*few_parts)
    g_pw, sums, g_one = call(
        stem_back_kernel,
        [
            ((2, CHANNELS, CHANNELS), f32),
            ((18, 8, CHANNELS), f32),
            ((16, CHANNELS), f32),
        ],
        [
            dx0,
            (windows, pl.ANY),
            (windows_t, pl.ANY),
            tap_one,
            taps,
            pointwise,
            (linear, pl.ANY),
            (front, pl.ANY),
            (mid, pl.ANY),
            (last, pl.ANY),
        ],
        back_scratch(rows),
        us=27,
        after=one_sum.cores() if plan else (),
        name="stem_back",
    )
    used = ROW_AT[2] + ROWS[4]
    share = -(-(-(-used // ndev)) // 16) * 16
    (few,) = call(
        stem_rows_kernel,
        [((ndev * share, LANES), bf16)],
        [g_pw, sums, g_one, vg_last, vg_conv, vg_mid, vg_att],
        [pltpu.VMEM((ndev * share, LANES), f32)],
        us=2,
        after=mix_sum.first() + one_sum.first() + few_sum.cores() if plan else (),
        name="stem_rows",
    )
    few = jnp.sum(spread(few.reshape(ndev, share, LANES)).astype(f32), 0)

    if plan:
        mix_sum.second()
        own_mix, own_abo = mix_sum.lines()
        few_sum.first()
        one_sum.second()
        own_in_one, own_out_one = one_sum.lines()
        few_sum.second()
        own_few = few_sum.lines()
    else:
        own_mix, own_abo = reduced_whole(mix, own_rows)
        own_in_one, own_out_one = reduced_whole(one, own_rows)
        own_few = reduced_whole(few_parts, half)
    own_chunk = jnp.concatenate(own_few, 0)

    start = shard * device
    positions = start + jnp.arange(shard, dtype=jnp.int32)
    own = [own_in_one, own_out_one, own_mix, own_abo, own_in_two, own_out_two]
    packed = lax.dynamic_slice_in_dim(own_chunk.reshape(-1), offset, shard, 0)
    local_sq = sum(jnp.sum(grad * grad) for grad in own) + jnp.sum(packed * packed)
    high = local_sq.astype(bf16)
    rest = local_sq - high.astype(f32)
    middle = rest.astype(bf16)
    lowest = (rest - middle.astype(f32)).astype(bf16)
    lane = jnp.arange(LANES)[None, :]
    number = jnp.where(lane == 0, high, jnp.where(lane == 1, middle, jnp.where(lane == 2, lowest, 0)))
    number = jnp.broadcast_to(number, (16, LANES)).astype(bf16)
    known = jnp.concatenate([few.astype(bf16), number], 0)
    known = spread(jnp.broadcast_to(known[None], (ndev, share + 16, LANES))).astype(f32)
    few = known[:, :share].reshape(ndev * share, LANES)
    total_sq = jnp.sum(known[:, share, 0:3]) + jnp.sum(few * few)
    grad_norm = jnp.sqrt(total_sq)
    factor = clip_norm / jnp.maximum(grad_norm, clip_norm)

    gap = jnp.zeros((chunk, LANES), f32)
    def window(part, at):
        padded = jnp.concatenate([gap, part, gap], 0)
        where = jnp.clip(row - at + chunk, 0, chunk + part.shape[0])
        return lax.dynamic_slice_in_dim(padded, where, chunk, 0)

    own_chunk = own_chunk + window(few[: ROW_AT[2]], 0) + window(few[ROW_AT[2] : used], ROW_AT[4])
    own_small = lax.dynamic_slice_in_dim(own_chunk.reshape(-1), offset, shard, 0)

    grad_in = jnp.stack([own_in_one, own_in_two])
    grad_out = jnp.stack([own_out_one, own_out_two]).transpose(0, 2, 1)
    grad_mix = jnp.concatenate([own_mix, own_abo[:, : 2 * LANES]], 1).reshape(own_rows, 6, LANES)
    grad_mixo = own_abo[:, 2 * LANES :].reshape(own_rows, 2, LANES).transpose(1, 2, 0)
    rates = (0.1, 0.05, 0.1, jnp.array([1.0, 0.1], f32)[:, None, None])
    states = (ff_in, ff_out, mix_in, mix_out)
    grads = (grad_in, grad_out, grad_mix, grad_mixo)
    outs = []
    for state, grad, rate in zip(states, grads, rates):
        outs.extend(adam(state, grad * factor, rate))
    outs.extend(adam(small, own_small * factor, small_rate(positions)))
    vec_grad = few[ROW_AT[2] : used].reshape(23, D) * factor
    return (*outs, vec_grad, loss[0, 0], grad_norm)


def solution(mesh):
    in_specs = (
        P("dp", "mp", None),
        P("dp"),
        P("dp", "mp"),
        P("dp", "mp"),
        P(None, None, "dp", "mp"),
        P(None, None, "mp", "dp"),
        P(None, "dp", None, "mp"),
        P(None, None, "mp", "dp"),
        P(None, ("dp", "mp")),
    )
    in_block, out_block = P(None, "dp", "mp"), P(None, "mp", "dp")
    mix_block, flat = P("dp", None, "mp"), P(("dp", "mp"))
    out_specs = (
        (in_block,) * 3 + (out_block,) * 3 + (mix_block,) * 3 + (out_block,) * 3 + (flat,) * 3
    )
    out_specs = out_specs + (P(), P(), P())
    return jax.shard_map(body, mesh=mesh, in_specs=in_specs, out_specs=out_specs, check_vma=False)
```

```python
import functools
import math

import jax
import jax.numpy as jnp
from jax import lax
from jax.experimental import pallas as pl
from jax.experimental.pallas import tpu as pltpu
from jax.sharding import PartitionSpec as P

D = 512
HEADS = 8
HEAD_DIM = 64
CHANNELS = 256
MEL = 80
KERNEL = 9
CLASSES = 1025
STEP = 7
LANES = 128
NPIECE = 4
F1, F2, F3 = MEL // 2, MEL // 4, MEL // 8
CPAD = 1152
HALO = 8
EDGE = 16

norm_eps = 1e-05
clip_norm = 0.005
beta_one = 0.9
beta_two = 0.98
adam_eps = 1e-08
decay_rate = 0.01
small_rates = (0.8, 0.15, 0.05, 0.1, 0.3)
f32 = jnp.float32
bf16 = jnp.bfloat16

SIZES = [27 * CHANNELS, 2 * CHANNELS * CHANNELS, CHANNELS * F3 * D, D * CLASSES, 23 * D]
NSMALL = sum(SIZES)
ROWS = [size // LANES for size in SIZES]
ROW_AT = [sum(ROWS[:k]) for k in range(5)]
NROWS = NSMALL // LANES


CORES, COLS, LINES = 2, 2, 2


def planned(n_dp, n_mp):
    return (n_dp, n_mp) == (8, 4)


def sent(x, name, by=1):
    axis, stride, size = {
        "c": ("mp", 1, 2),
        "x": ("mp", 2, 2),
        "y": ("dp", 1, 2),
        "z": ("dp", 2, lax.axis_size("dp") // 2),
    }[name]
    pairs = []
    for i in range(lax.axis_size(axis)):
        k = (i // stride) % size
        pairs.append((i, i + (((k + by) % size) - k) * stride))
    return lax.ppermute(x, axis, pairs)


def held(values, others):
    return lax.optimization_barrier((values, others))[0] if others else values


def total(*parts):
    return functools.reduce(lambda a, b: a + b, [part.astype(f32) for part in parts])


def low_total(*parts):
    return total(*parts).astype(bf16)


class Reduced:
    def __init__(self, *parts):
        self.parts, self.deep = parts[:2], parts[0].shape[2]
        self.out = [parts[2], parts[3]]

    def cores(self):
        got = [sent(x, "c") for x in self.out]
        self.a, self.b = ([keep, more] for keep, more in zip(self.parts, got))
        self.out = [
            low_total(*[part[1] for part in self.a]),
            low_total(*[part[:, 1] for part in self.b]),
        ]
        return self.out

    def first(self):
        got_a, got_b = sent(self.out[0], "x"), sent(self.out[1], "y")
        self.a = [part[0] for part in self.a] + [got_a]
        self.b = [part[:, 0] for part in self.b] + [got_b]
        self.out = [
            low_total(*[part[1] for part in self.a]),
            low_total(*[part[1] for part in self.b]),
        ]
        return self.out

    def second(self):
        got_a, got_b = sent(self.out[0], "y"), sent(self.out[1], "x")
        self.a = [part[0] for part in self.a] + [got_a]
        self.b = [part[0] for part in self.b] + [got_b]
        self.out = [
            jnp.stack(
                [low_total(*[part[k] for part in self.a]), low_total(*[part[k] for part in self.b])]
            )
            for k in range(1, self.deep)
        ]
        return self.out

    def lines(self):
        got = [sent(x, "z", k + 1) for k, x in enumerate(self.out)]
        return [
            total(*[part[0] for part in side], *[x[k] for x in got])
            for k, side in enumerate((self.a, self.b))
        ]


class ReducedOneWay:
    def __init__(self, keep, send, axes):
        self.keep, self.out, self.axes = keep, send, axes

    def side(self, array, *index):
        index = dict(zip(self.axes, index))
        return array[tuple(index.get(axis, slice(None)) for axis in "xy")]

    def cores(self):
        self.got = sent(self.out, "c")
        self.out = low_total(self.side(self.keep, 1), self.side(self.got, 1))
        return [self.out]

    def first(self):
        self.more = sent(self.out, self.axes[0])
        self.out = low_total(self.side(self.keep, 0, 1), self.side(self.got, 0, 1), self.more[1])
        return [self.out]

    def second(self):
        last = sent(self.out, self.axes[1])
        self.parts = self.side(self.keep, 0, 0), self.side(self.got, 0, 0), self.more[0], last
        self.out = [low_total(*[x[k] for x in self.parts]) for k in range(1, last.shape[0])]
        return self.out

    def lines(self):
        got = [sent(x, "z", k + 1) for k, x in enumerate(self.out)]
        own = total(*[x[0] for x in self.parts], *got)
        rows = own.shape[0] // 2
        return [own[:rows], own[rows:]]


class Gathered:
    def __init__(self, low):
        self.low = low

    def after(self, *others):
        (self.a, self.b), _ = lax.optimization_barrier(((self.a, self.b), others))
        return self

    def lines(self):
        lines, rows = lax.axis_size("dp") // LINES, self.low.shape[0] // 2
        parts = [self.low] + [sent(self.low, "z", lines - k) for k in range(1, lines)]
        self.a = jnp.stack([part[:rows] for part in parts])
        self.b = jnp.stack([part[rows:] for part in parts])
        return [self.a, self.b]

    def first(self):
        self.a = jnp.stack([self.a, sent(self.a, "x")])
        self.b = jnp.stack([self.b, sent(self.b, "y")])
        return [self.a, self.b]

    def second(self):
        both = [self.a, sent(self.a, "y")], [self.b, sent(self.b, "x")]
        both = jnp.stack([jnp.stack(side) for side in both])
        self.mine = both.reshape((2, -1) + both.shape[4:])
        return [self.mine]

    def cores(self):
        return [self.mine, sent(self.mine, "c")]


def reduced_whole(parts, own_rows):
    own = []
    for keep, send in zip(parts[:2], parts[2:]):
        both = jnp.stack([keep, send], 1)[:, :, 0, 0]
        both = both.reshape((lax.axis_size("mp"), lax.axis_size("dp"), -1, keep.shape[-1]))
        both = lax.psum_scatter(both, "mp", scatter_dimension=0, tiled=True)
        both = lax.psum_scatter(both, "dp", scatter_dimension=1, tiled=True)
        own.append(both.reshape(own_rows, keep.shape[-1]).astype(f32))
    return own


def reduced_cores(keep, send, plan):
    if plan:
        both = low_total(keep, sent(send, "c"))
        ndev = lax.axis_size("dp") * lax.axis_size("mp")
        groups = [list(range(core, ndev, CORES)) for core in range(CORES)]
        both = both.reshape(ndev // CORES, 2, *both.shape[3:])
        own = lax.psum_scatter(
            both, ("dp", "mp"), scatter_dimension=0, axis_index_groups=groups, tiled=True
        )
        return [both], own
    both = jnp.stack([keep, send], 2)[0].reshape(lax.axis_size("mp"), 2, lax.axis_size("dp"), -1, D)
    both = lax.psum_scatter(both, "mp", scatter_dimension=0, tiled=True)
    both = lax.psum_scatter(both, "dp", scatter_dimension=2, tiled=True)
    return (), both


def spread(x):
    return lax.all_to_all(x, ("dp", "mp"), 0, 0, tiled=True)


def passed_along(x, by):
    peers = lax.axis_size("mp")
    pairs = [(i, i + by) for i in range(peers) if 0 <= i + by < peers]
    return lax.ppermute(x, "mp", pairs)


def call(kernel, outs, args, scratch=(), us=1, after=(), out_any=(), name=None):
    whole = pl.BlockSpec(memory_space=pltpu.VMEM)
    specs, arrays = [], []
    for arg in args:
        array, space = arg if isinstance(arg, tuple) else (arg, pltpu.VMEM)
        specs.append(pl.BlockSpec(memory_space=space))
        arrays.append(array)
    used = len(arrays)
    arrays += list(after)
    specs += [pl.BlockSpec(memory_space=pl.ANY)] * len(after)

    def run(*refs):
        kernel(*refs[:used], *refs[len(arrays) :])

    return pl.pallas_call(
        run,
        out_shape=[jax.ShapeDtypeStruct(shape, dtype) for shape, dtype in outs],
        in_specs=specs,
        out_specs=[pl.BlockSpec(memory_space=pl.ANY) if k in out_any else whole for k in range(len(outs))],
        scratch_shapes=list(scratch),
        compiler_params=pltpu.CompilerParams(vmem_limit_bytes=56 * 1024 * 1024),
        cost_estimate=pl.CostEstimate(
            flops=int(us * 1.15e9), bytes_accessed=int(us * 1e6), transcendentals=0
        ),
        name=name,
    )(*arrays)


def fetched(weights, which, lo, hi, buf, sem):
    copies = [
        pltpu.make_async_copy(weights.at[:, m, which, :, lo:hi], buf.at[m], sem.at[m])
        for m in range(buf.shape[0])
    ]
    for copy in copies:
        copy.start()
    return copies


def buffers(weights, *widths):
    deep, n_mp, _, rows, _ = weights.shape
    out = []
    for width in widths:
        out.append(pltpu.VMEM((n_mp, deep, rows, width), bf16))
        out.append(pltpu.SemaphoreType.DMA((n_mp,)))
    return out


def block(buf, m, lanes=slice(None)):
    part = buf[m, :, :, lanes]
    return part.reshape(part.shape[0] * part.shape[1], part.shape[2])


def aligned(at):
    return pl.ds(pl.multiple_of(at, LANES), LANES)


def pieces(spot):
    for c in range(CORES):
        for x in range(COLS):
            yield c, x, ((spot[1] + x) % COLS) * CORES + (spot[0] + c) % CORES


def core_pieces(spot):
    for c in range(CORES):
        for x in range(COLS):
            yield c, x, x * CORES + (spot[0] + c) % CORES


def write_core_piece(to, x, half, grad):
    rows = to.shape[3]
    grad = grad.astype(bf16)
    for k in range(to.shape[0]):
        to[k, x, half] = grad[rows * k : rows * k + rows]


def write_piece(spot, to, half, x, grad):
    _, deep, lines, rows, _ = to.shape
    rows = rows // 2
    grad = grad.astype(bf16)
    for z in range(lines):
        for y in range(deep):
            at = (z * deep + y) * rows
            index = x, (y + deep - spot[2]) % deep, (z + lines - spot[3]) % lines
            to[(*index, slice(rows * half, rows * half + rows))] = grad[at : at + rows]


def nn(left, right):
    return jnp.dot(left, right, preferred_element_type=f32)


def nt(left, right):
    return lax.dot_general(left, right, (((1,), (1,)), ((), ())), preferred_element_type=f32)


def tn(left, right):
    return lax.dot_general(left, right, (((0,), (0,)), ((), ())), preferred_element_type=f32)


def sigmoid(v):
    return 1.0 / (1.0 + jnp.exp(-v))


def layer_norm(x, gain, shift):
    centered = x - jnp.mean(x, -1, keepdims=True)
    rstd = lax.rsqrt(jnp.mean(centered * centered, -1, keepdims=True) + norm_eps)
    return centered * rstd * gain + shift


def layer_norm_back(x, gain, grad):
    centered = x - jnp.mean(x, -1, keepdims=True)
    rstd = lax.rsqrt(jnp.mean(centered * centered, -1, keepdims=True) + norm_eps)
    xhat = centered * rstd
    g = grad * gain
    dx = rstd * (
        g - jnp.mean(g, -1, keepdims=True) - xhat * jnp.mean(g * xhat, -1, keepdims=True)
    )
    return dx, jnp.sum(grad * xhat, 0, keepdims=True), jnp.sum(grad, 0, keepdims=True)


def eight(x):
    rows = x.shape[0] // 8
    return jnp.sum(x.reshape(rows, 8, x.shape[1]), 0)


def flip_matrix(size):
    at = lax.broadcasted_iota(jnp.int32, (size, size), 0)
    to = lax.broadcasted_iota(jnp.int32, (size, size), 1)
    return (at + to == size - 1).astype(bf16)


def first_row(shard, device):
    return lax.shift_left(lax.shift_right_logical(shard * device, 11), 4)


def rows_at(at, rows):
    return pl.ds(pl.multiple_of(at, 16), rows)


def piece_place(spot, c, half, q):
    i, j, z = q // 8, (q // 4) % 2, q % 4
    y, x = (j, i) if half else (i, j)
    dp = ((spot[3] + z) % 4) * LINES + (spot[2] + y) % LINES
    return dp, ((spot[1] + x) % COLS) * CORES + (spot[0] + c) % CORES


def unpack_kernel(
    shard, spot, mine_ref, other_ref, taps_ref, one_ref, pw_ref, lin_ref, head_ref, vec_ref, flat
):
    flat[...] = jnp.zeros_like(flat)
    rows = mine_ref.shape[2]
    for c, ref in enumerate((mine_ref, other_ref)):
        for half in range(2):

            def step(q, carry, c=c, ref=ref, half=half):
                dp, mp = piece_place(spot, c, half, q)
                at = first_row(shard, dp * (COLS * CORES) + mp) + rows * half
                flat[rows_at(at, rows), :] += ref[half, q].astype(f32)
                return carry

            lax.fori_loop(0, ref.shape[1], step, 0)
    unpack_flat(flat, taps_ref, one_ref, pw_ref, lin_ref, head_ref, vec_ref)


def unpack_whole_kernel(
    shard, all_ref, taps_ref, one_ref, pw_ref, lin_ref, head_ref, vec_ref, flat
):
    flat[...] = jnp.zeros_like(flat)
    rows = all_ref.shape[1]

    def step(device, carry):
        flat[rows_at(first_row(shard, device), rows), :] += all_ref[device].astype(f32)
        return carry

    lax.fori_loop(0, all_ref.shape[0], step, 0)
    unpack_flat(flat, taps_ref, one_ref, pw_ref, lin_ref, head_ref, vec_ref)


def unpack_flat(flat, taps_ref, one_ref, pw_ref, lin_ref, head_ref, vec_ref):
    one_ref[...] = jnp.zeros_like(one_ref)
    taps_ref[...] = jnp.zeros_like(taps_ref)
    vec_ref[...] = jnp.zeros_like(vec_ref)
    for h in range(2):
        lanes = slice(LANES * h, LANES * h + LANES)
        taps = flat[pl.ds(h, 27, stride=2), :]
        taps_ref[0:27, lanes] = taps
        padded = jnp.concatenate([taps[0:9], jnp.zeros((7, LANES), f32)], 0).astype(bf16)
        for k in range(8):
            one_ref[k, 16 * k : 16 * k + 16, lanes] = padded
        for k in range(2):
            part = flat[pl.ds(ROW_AT[1] + 512 * k + h, CHANNELS, stride=2), :]
            pw_ref[k, :, lanes] = part.astype(bf16)
    for j in range(4):
        lanes = slice(LANES * j, LANES * j + LANES)
        for f in range(F3):
            part = flat[pl.ds(ROW_AT[2] + 1024 * f + j, CHANNELS, stride=4), :]
            lin_ref[f, :, lanes] = part.astype(bf16)
        vec_ref[0:23, lanes] = flat[pl.ds(ROW_AT[4] + j, 23, stride=4), :]
    flip = flip_matrix(LANES)
    column = lax.broadcasted_iota(jnp.int32, (LANES, CPAD), 1)
    for q in range(D // LANES):
        at = ROW_AT[3] + 1025 * q
        wide = jnp.concatenate(
            [flat[pl.ds(at + c, LANES, stride=8), :] for c in range(CPAD // LANES)], 1
        )
        turned = nn(flip, wide.astype(bf16))
        turned = pltpu.roll(turned, CPAD - LANES + 1, 1, stride=1, stride_axis=0)
        turned = jnp.where(column < CLASSES, turned, 0.0)
        head_ref[LANES * q : LANES * q + LANES, :] = nn(flip, turned.astype(bf16)).astype(bf16)


def pack_kernel(shard, n_dp, spot, last_ref, dx_ref, dhead_ref, *refs):
    outs, flat, parts, sem = refs[:4], refs[4], refs[5], refs[6]
    dx = dx_ref[...]
    flat[0 : ROW_AT[2], :] = jnp.zeros((ROW_AT[2], LANES), f32)
    flat[ROW_AT[4] :, :] = jnp.zeros((flat.shape[0] - ROW_AT[4], LANES), f32)
    for f in range(F3):
        grad = tn(last_ref[f], dx)
        for j in range(4):
            flat[pl.ds(ROW_AT[2] + 1024 * f + j, CHANNELS, stride=4), :] = grad[
                :, LANES * j : LANES * j + LANES
            ]
    for q in range(D // LANES):
        at = ROW_AT[3] + 1025 * q
        turned = pltpu.roll(
            dhead_ref[LANES * q : LANES * q + LANES, :].astype(f32), 0, 1, stride=1, stride_axis=0
        )
        flat[pl.ds(at + 8, LANES, stride=8), :] = turned[:, 8 * LANES :]
        flat[at : at + 1, :] = turned[0:1, 0:LANES]
        flat[pl.ds(at + 8, LANES - 1, stride=8), :] += turned[1:, 0:LANES]
        for c in range(1, 8):
            flat[pl.ds(at + c, LANES, stride=8), :] = turned[:, LANES * c : LANES * c + LANES]
    _, _, deep, lines, rows, _ = parts.shape
    copies = []
    each = n_dp // (deep * lines)
    rows = rows // each
    for c in range(CORES):

        def step(q, carry, c=c):
            k = q % each
            z, y, x = (q // each) % lines, (q // (each * lines)) % deep, q // (each * lines * deep)
            mp = ((spot[1] + x) % COLS) * CORES + (spot[0] + c) % CORES
            dp = ((spot[3] + z) % lines) * deep + (spot[2] + y) % deep + k
            row = first_row(shard, dp * (COLS * CORES) + mp)
            for half in range(2):
                part = flat[rows_at(row + rows * half, rows), :]
                parts[half + 2 * c, x, y, z, rows_at(rows * k, rows), :] = part.astype(bf16)
            return carry

        lax.fori_loop(0, COLS * deep * lines * each, step, 0)
        for half in range(2):
            part = half + 2 * c
            copies.append(pltpu.make_async_copy(parts.at[part], outs[part], sem.at[part]))
            copies[-1].start()
    for copy in copies:
        copy.wait()


def stem_chunks(rows):
    for lane in range(0, CHANNELS, LANES):
        for at in range(0, rows, 48):
            yield slice(lane, lane + LANES), at


def stem_scratch(rows):
    return [
        pltpu.VMEM((5, 4 * rows, CHANNELS), f32),
        pltpu.VMEM((F2, 2 * rows, CHANNELS), f32),
        pltpu.VMEM((rows + 8, CHANNELS), f32),
        pltpu.VMEM((rows - EDGE, F3 * CHANNELS), bf16),
        pltpu.VMEM((F3, CHANNELS, D), bf16),
        pltpu.VMEM((F2, 2 * rows, CHANNELS), bf16),
        pltpu.SemaphoreType.DMA((2,)),
    ]


def first_rows(win_ref, one_ref, f):
    return jax.nn.relu(nn(win_ref[f // 8], one_ref[f % 8]))


def staged(sources, targets, sem):
    copies = [pltpu.make_async_copy(s, t, sem.at[k]) for k, (s, t) in enumerate(zip(sources, targets))]
    for copy in copies:
        copy.start()
    return copies


def stem_kernel(
    win_ref,
    one_ref,
    taps_ref,
    pw_ref,
    lin_hbm,
    x0_ref,
    front_hbm,
    mid_ref,
    last_ref,
    t_ref,
    r_ref,
    lag_ref,
    flat,
    lin_ref,
    front_ref,
    sem,
):
    rows = lag_ref.shape[0] - 8
    (lin_copy,) = staged([lin_hbm], [lin_ref], sem.at[pl.ds(0, 1)])
    lag_ref[0:8, :] = jnp.zeros((8, CHANNELS), f32)
    t_ref[4] = jnp.zeros_like(t_ref[4])

    def second(slots, to):
        for lanes, at in stem_chunks(rows):

            def tap(k):
                return taps_ref[k : k + 1, lanes]

            lag, even, odd = 0.0, 0.0, 0.0
            for df, slot in enumerate(slots):
                t0, t1, t2, t3 = (
                    t_ref[slot, a * rows + at : a * rows + at + 48, lanes] for a in range(4)
                )
                lag += t3 * tap(9 + df)
                even += t0 * tap(12 + df) + t1 * tap(15 + df)
                odd += t1 * tap(9 + df) + t2 * tap(12 + df) + t3 * tap(15 + df)
            lag_ref[8 + at : 56 + at, lanes] = lag
            even += lag_ref[7 + at : 55 + at, lanes]
            front_ref[to, at : at + 48, lanes] = even.astype(bf16)
            front_ref[to, rows + at : rows + at + 48, lanes] = odd.astype(bf16)

    def step_front(f, carry):
        for k in range(4):
            t_ref[k] = first_rows(win_ref, one_ref, 4 * f + k)
        second((4, 0, 1), 2 * f)
        second((1, 2, 3), 2 * f + 1)
        t_ref[4] = t_ref[3]
        return carry

    lax.fori_loop(0, F3, step_front, 0)

    def step_point(f, carry):
        for k in range(4):
            r_ref[4 * f + k] = jax.nn.relu(nn(front_ref[4 * f + k], pw_ref[0]))
        return carry

    lax.fori_loop(0, F2 // 4, step_point, 0)

    front_copy = pltpu.make_async_copy(front_ref, front_hbm, sem.at[1])
    front_copy.start()

    def third(f, whole):
        for lanes, at in stem_chunks(rows):

            def tap(k):
                return taps_ref[k : k + 1, lanes]

            lag, out = 0.0, 0.0
            for df in range(0 if whole else 1, 3):
                slot = 2 * f - 1 + df
                even = r_ref[slot, at : at + 48, lanes]
                odd = r_ref[slot, rows + at : rows + at + 48, lanes]
                lag += odd * tap(18 + df)
                out += even * tap(21 + df) + odd * tap(24 + df)
            lag_ref[8 + at : 56 + at, lanes] = lag
            out += lag_ref[7 + at : 55 + at, lanes]
            skip = max(0, EDGE - at)
            mid_ref[f, at + skip - EDGE : at + 48 - EDGE, lanes] = out[skip:].astype(bf16)

    third(0, False)

    def step_mid(f, carry):
        third(f, True)
        return carry

    lax.fori_loop(1, F3, step_mid, 0)
    for f in range(F3):
        last = jax.nn.relu(nn(mid_ref[f], pw_ref[1])).astype(bf16)
        last_ref[f] = last
        flat[:, CHANNELS * f : CHANNELS * f + CHANNELS] = last
    lin_copy.wait()
    x0_ref[...] = nn(flat[...], lin_ref[...].reshape(F3 * CHANNELS, D))
    front_copy.wait()


def back_scratch(rows):
    return [
        pltpu.VMEM((F3, rows - EDGE, CHANNELS), bf16),
        pltpu.VMEM((F3 + 1, rows + 8, CHANNELS), f32),
        pltpu.VMEM((F2 + 1, 3 * rows, CHANNELS), f32),
        pltpu.VMEM((F2, 2 * rows, CHANNELS), f32),
        pltpu.VMEM((F2, 2 * rows, CHANNELS), bf16),
        pltpu.VMEM((2, 4 * rows, CHANNELS), f32),
        pltpu.VMEM((F2, 8 * rows, CHANNELS), bf16),
        pltpu.VMEM((F3, CHANNELS, D), bf16),
        pltpu.VMEM((F3, rows - EDGE, CHANNELS), bf16),
        pltpu.VMEM((F3, rows - EDGE, CHANNELS), bf16),
        pltpu.VMEM((F2, 2 * rows, CHANNELS), bf16),
        pltpu.VMEM((F1 // 8, 4 * rows, LANES), bf16),
        pltpu.VMEM((16, F2 * 8 * rows), bf16),
        pltpu.SemaphoreType.DMA((6,)),
    ]


def stem_back_kernel(
    dx_ref,
    win_hbm,
    turn_hbm,
    one_ref,
    taps_ref,
    pw_ref,
    lin_hbm,
    front_hbm,
    mid_hbm,
    last_hbm,
    g_pw,
    sums,
    g_one,
    g_last,
    g_mid,
    g_front,
    p_ref,
    q_ref,
    t_ref,
    s_ref,
    lin_ref,
    last_ref,
    mid_ref,
    front_ref,
    win_ref,
    turn_ref,
    sem,
):
    copies = staged(
        [lin_hbm, last_hbm, mid_hbm, front_hbm, win_hbm, turn_hbm],
        [lin_ref, last_ref, mid_ref, front_ref, win_ref, turn_ref],
        sem,
    )
    rows = g_mid.shape[1] - 8
    tokens = rows - EDGE
    sums[...] = jnp.zeros_like(sums)
    g_one[...] = jnp.zeros_like(g_one)
    g_mid[:, 0:EDGE, :] = jnp.zeros((F3 + 1, EDGE, CHANNELS), f32)
    g_mid[:, rows:, :] = jnp.zeros((F3 + 1, 8, CHANNELS), f32)
    g_mid[F3] = jnp.zeros_like(g_mid[F3])
    g_front[F2] = jnp.zeros_like(g_front[F2])
    dx = dx_ref[...]
    copies[0].wait()
    copies[1].wait()
    for f in range(F3):
        grad = nt(dx, lin_ref[f])
        grad = jnp.where(last_ref[f].astype(f32) > 0, grad, 0.0).astype(bf16)
        g_last[f] = grad
    for f in range(F3):
        g_mid[f, EDGE:rows, :] = nt(g_last[f], pw_ref[1])
    whole = (F3 * tokens, CHANNELS)
    copies[2].wait()
    g_pw[1] = tn(mid_ref[...].reshape(whole), g_last[...].reshape(whole))

    copies[3].wait()

    def step_point(f, carry):
        for k in range(4):
            p_ref[4 * f + k] = jax.nn.relu(nn(front_ref[4 * f + k], pw_ref[0]))
        return carry

    lax.fori_loop(0, F2 // 4, step_point, 0)

    def step_mid(f, carry):
        for odd in range(2):
            uses = [(f, 2), (f + 1, 0)] if odd else [(f, 1)]
            here = 2 * f + odd
            for lane in range(0, CHANNELS, LANES):
                lanes = slice(lane, lane + LANES)

                def tap(k):
                    return taps_ref[k : k + 1, lanes]

                found = {}
                for at in range(0, rows, 48):
                    p_even = p_ref[here, at : at + 48, lanes]
                    p_odd = p_ref[here, rows + at : rows + at + 48, lanes]
                    d_even, d_odd = 0.0, 0.0
                    for which, df in uses:
                        g = g_mid[which, at : at + 48, lanes]
                        g_up = g_mid[which, at + 1 : at + 49, lanes]
                        d_even += g * tap(21 + df)
                        d_odd += g * tap(24 + df) + g_up * tap(18 + df)
                        for k, x in ((df, g_up * p_odd), (3 + df, g * p_even), (6 + df, g * p_odd)):
                            found[k] = found.get(k, 0.0) + eight(x)
                    q_ref[here, at : at + 48, lanes] = jnp.where(p_even > 0, d_even, 0.0).astype(bf16)
                    q_ref[here, rows + at : rows + at + 48, lanes] = jnp.where(
                        p_odd > 0, d_odd, 0.0
                    ).astype(bf16)
                for k, x in found.items():
                    sums[9 + k, :, lanes] += x
        return carry

    lax.fori_loop(0, F3, step_mid, 0)

    def step_back(f, carry):
        for k in range(4):
            grad = nt(q_ref[4 * f + k], pw_ref[0])
            g_front[4 * f + k, 0 : 2 * rows, :] = grad
            g_front[4 * f + k, 2 * rows :, :] = pltpu.roll(grad[:rows], rows - 1, 0)
        size = (8 * rows, CHANNELS)
        grad = tn(front_ref[pl.ds(4 * f, 4)].reshape(size), q_ref[pl.ds(4 * f, 4)].reshape(size))
        g_pw[0] = jnp.where(f == 0, grad, g_pw[0] + grad)
        return carry

    lax.fori_loop(0, F2 // 4, step_back, 0)

    copies[4].wait()
    copies[5].wait()

    def step_front(f, carry):
        for odd in range(2):
            t_ref[odd] = first_rows(win_ref, one_ref, 2 * f + odd)
        for odd in range(2):
            uses = [(f, 2), (f + 1, 0)] if odd else [(f, 1)]
            for lane in range(0, CHANNELS, LANES):
                lanes = slice(lane, lane + LANES)

                def tap(k):
                    return taps_ref[k : k + 1, lanes]

                found = {}
                for at in range(0, rows, 48):
                    t0, t1, t2, t3 = (
                        t_ref[odd, a * rows + at : a * rows + at + 48, lanes] for a in range(4)
                    )
                    d = [0.0] * 4
                    for which, df in uses:
                        e = g_front[which, at : at + 48, lanes]
                        o = g_front[which, rows + at : rows + at + 48, lanes]
                        e_up = g_front[which, 2 * rows + at : 2 * rows + at + 48, lanes]
                        d[0] += e * tap(12 + df)
                        d[1] += e * tap(15 + df) + o * tap(9 + df)
                        d[2] += o * tap(12 + df)
                        d[3] += o * tap(15 + df) + e_up * tap(9 + df)
                        for k, x in (
                            (df, t1 * o + t3 * e_up),
                            (3 + df, t0 * e + t2 * o),
                            (6 + df, t1 * e + t3 * o),
                        ):
                            found[k] = found.get(k, 0.0) + eight(x)
                    for a, (t, grad) in enumerate(zip((t0, t1, t2, t3), d)):
                        to = (4 * odd + a) * rows + at
                        s_ref[f, to : to + 48, lanes] = jnp.where(t > 0, grad, 0.0).astype(bf16)
                for k, x in found.items():
                    sums[k, :, lanes] += x

        return carry

    lax.fori_loop(0, F2, step_front, 0)
    part = F2 // 4
    for k in range(4):
        at = part * 8 * rows
        g_one[...] += nn(
            turn_ref[:, k * at : (k + 1) * at],
            s_ref[part * k : part * (k + 1)].reshape(at, CHANNELS),
        )


def stem_rows_kernel(
    g_pw, sums, g_one, vg_last, vg_conv, vg_mid, vg_att, out_ref, flat
):
    taps = jnp.concatenate(
        [g_one[0:9, :]]
        + [jnp.sum(sums[k], 0, keepdims=True) for k in range(18)],
        0,
    )
    order = [
        (vg_last, 2),
        (vg_last, 0),
        (vg_conv, 0),
        (vg_mid, 2),
        (vg_mid, 0),
        (vg_last, 3),
        (vg_last, 1),
        (vg_conv, 1),
        (vg_mid, 3),
        (vg_mid, 1),
        (vg_mid, 4),
        (vg_mid, 5),
        (vg_att, 0),
        (vg_att, 1),
    ] + [(vg_conv, k) for k in range(2, 11)]
    flat[ROW_AT[2] + ROWS[4] - 8 :, :] = jnp.zeros((flat.shape[0] - ROW_AT[2] - ROWS[4] + 8, LANES), f32)
    for h in range(2):
        lanes = slice(LANES * h, LANES * h + LANES)
        flat[pl.ds(h, 27, stride=2), :] = taps[:, lanes]
        for k in range(2):
            flat[pl.ds(ROW_AT[1] + 512 * k + h, CHANNELS, stride=2), :] = g_pw[k, :, lanes]
    for k, (ref, row) in enumerate(order):
        for j in range(4):
            at = ROW_AT[2] + 4 * k + j
            flat[at : at + 1, :] = ref[row : row + 1, LANES * j : LANES * j + LANES]
    out_ref[...] = flat[...].astype(bf16)


def ffn_forward(x, vec_ref, which, win, wout, pre_ref, normed_ref):
    normed = layer_norm(x, vec_ref[which : which + 1, :], vec_ref[which + 5 : which + 6, :])
    normed = normed.astype(bf16)
    normed_ref[...] = normed
    total = jnp.zeros_like(x)
    (in_copies, in_buf), (out_copies, out_buf) = win, wout
    for m in range(NPIECE):
        in_copies[m].wait()
        pre = nn(normed, block(in_buf, m))
        pre_ref[m] = pre
        out_copies[m].wait()
        total += nt((pre * sigmoid(pre)).astype(bf16), block(out_buf, m))
    return x + 0.5 * total


def ffn_backward(grad, x, vec_ref, which, in_buf, out_buf, pre_ref, normed_ref, order, write):
    low = (0.5 * grad).astype(bf16)
    back = jnp.zeros_like(x)
    for c, col, m in order:
        pre = pre_ref[m]
        sig = sigmoid(pre)
        write(c, col, 1, tn(low, (pre * sig).astype(bf16)))
        g_pre = (nn(low, block(out_buf, m)) * (sig * (1.0 + pre * (1.0 - sig)))).astype(bf16)
        write(c, col, 0, tn(normed_ref[...], g_pre))
        back += nt(g_pre, block(in_buf, m))
    dx, gain, shift = layer_norm_back(x, vec_ref[which : which + 1, :], back)
    return grad + dx, gain, shift


def first_kernel(
    weights,
    x_ref,
    vec_ref,
    x1_ref,
    pre_ref,
    n1_ref,
    n2_ref,
    in_buf,
    in_sem,
    out_buf,
    out_sem,
):
    win = fetched(weights, 0, 0, D, in_buf, in_sem)
    wout = fetched(weights, 1, 0, D, out_buf, out_sem)
    x1 = ffn_forward(x_ref[...], vec_ref, 0, (win, in_buf), (wout, out_buf), pre_ref, n1_ref)
    x1_ref[...] = x1
    n2_ref[...] = layer_norm(x1, vec_ref[1:2, :], vec_ref[6:7, :]).astype(bf16)


def position_kernel(
    weights, table_ref, n2_ref, vec_ref, pe_ref, qu_ref, qv_ref, buf, sem, q_buf, q_sem
):
    q_copies = fetched(weights, 2, 0, LANES, q_buf, q_sem)
    copies = fetched(weights, 2, 3 * LANES, 4 * LANES, buf, sem)
    for m in range(NPIECE):
        lanes = slice(LANES * m, LANES * m + LANES)
        q_copies[m].wait()
        query = nn(n2_ref[...], block(q_buf, m))
        qu_ref[:, lanes] = (query + vec_ref[12:13, lanes]).astype(bf16)
        qv_ref[:, lanes] = (query + vec_ref[13:14, lanes]).astype(bf16)
        copies[m].wait()
        pe_ref[:, lanes] = nn(table_ref[...], block(buf, m)).astype(bf16)


def head_lanes(h):
    return h // 2, HEAD_DIM * (h % 2), slice(HEAD_DIM * h, HEAD_DIM * h + HEAD_DIM)


def attention_kernel(
    weights,
    all_ref,
    x1_ref,
    qu_ref,
    qv_ref,
    pe_ref,
    vec_ref,
    keep_ref,
    valid_ref,
    x2_ref,
    kv_ref,
    prob_ref,
    att_ref,
    n3_ref,
    ga_ref,
    gb_ref,
    gated_ref,
    low_ref,
    high_ref,
    kv_buf,
    kv_sem,
    abo_buf,
    abo_sem,
):
    kv_copies = fetched(weights, 2, LANES, 3 * LANES, kv_buf, kv_sem)
    abo_copies = fetched(weights, 3, 0, 3 * LANES, abo_buf, abo_sem)
    rows, length = x1_ref.shape[0], all_ref.shape[0]
    width = rows + length
    for m in range(NPIECE):
        kv_copies[m].wait()
        kv_ref[m] = nn(all_ref[...], block(kv_buf, m)).astype(bf16)
    keep = keep_ref[...] > 0
    for h in range(HEADS):
        m, at, lanes = head_lanes(h)
        raw = nt(qu_ref[:, lanes], kv_ref[m, :, at : at + HEAD_DIM])
        far = nt(qv_ref[:, lanes], pe_ref[:, lanes])
        far = pltpu.roll(far, width - rows + 1, 1, stride=1, stride_axis=0)
        scores = jnp.where(keep, (raw + far[:, :length]) * 0.125, -1e30)
        expo = jnp.exp(scores - jnp.max(scores, -1, keepdims=True))
        prob = expo / jnp.sum(expo, -1, keepdims=True)
        prob_ref[h] = prob
        value = kv_ref[m, :, LANES + at : LANES + at + HEAD_DIM]
        att_ref[:, lanes] = nn(prob.astype(bf16), value).astype(bf16)
    x2 = x1_ref[...]
    for m in range(NPIECE):
        abo_copies[m].wait()
        lanes = slice(LANES * m, LANES * m + LANES)
        x2 += nt(att_ref[:, lanes], block(abo_buf, m, slice(2 * LANES, 3 * LANES)))
    x2_ref[...] = x2
    normed = layer_norm(x2, vec_ref[2:3, :], vec_ref[7:8, :]).astype(bf16)
    n3_ref[...] = normed
    for m in range(NPIECE):
        lanes = slice(LANES * m, LANES * m + LANES)
        gates = nn(normed, block(abo_buf, m, slice(0, 2 * LANES)))
        ga, gb = gates[:, :LANES], gates[:, LANES:]
        ga_ref[:, lanes] = ga
        gb_ref[:, lanes] = gb
        gated_ref[:, lanes] = ga * sigmoid(gb) * valid_ref[...]
    low_ref[...] = gated_ref[0:HALO, :]
    high_ref[...] = gated_ref[rows - HALO :, :]


def write_stats(stat_ref, first, second, number):
    rows = [x[:, LANES * k : LANES * k + LANES] for x in (first, second) for k in range(4)]
    rows.append(jnp.broadcast_to(number, (8, LANES)))
    stat_ref[...] = jnp.broadcast_to(jnp.concatenate(rows, 0)[None], stat_ref.shape)


def read_stats(stat_ref):
    whole = jnp.sum(stat_ref[...], 0)
    first = jnp.concatenate([whole[k : k + 1] for k in range(4)], 1)
    second = jnp.concatenate([whole[k : k + 1] for k in range(4, 8)], 1)
    return first, second, whole[8:9, 0:1]


def conv_kernel(prev_ref, gated_ref, next_ref, vec_ref, valid_ref, hidden_ref, stat_ref, wide):
    rows = gated_ref.shape[0]
    wide[0:HALO, :] = prev_ref[...]
    wide[HALO : HALO + rows, :] = gated_ref[...]
    wide[HALO + rows :, :] = next_ref[...]
    at = HALO - KERNEL // 2
    hidden = sum(wide[at + k : at + k + rows, :] * vec_ref[14 + k : 15 + k, :] for k in range(KERNEL))
    hidden_ref[...] = hidden
    valid = valid_ref[...]
    kept = hidden * valid
    write_stats(
        stat_ref,
        jnp.sum(kept, 0, keepdims=True),
        jnp.sum(kept * hidden, 0, keepdims=True),
        jnp.sum(valid, 0, keepdims=True),
    )


def middle_kernel(
    spot,
    weights,
    more,
    hidden_ref,
    stat_ref,
    x2_ref,
    head_ref,
    vec_ref,
    label_ref,
    weight_ref,
    valid_ref,
    keep_ref,
    send_ref,
    g_head_ref,
    dx3_ref,
    act_ref,
    dy_ref,
    yhat_ref,
    low_ref,
    high_ref,
    part_ref,
    vgrad_ref,
    pre_ref,
    n4_ref,
    c_buf,
    c_sem,
    in_buf,
    in_sem,
    out_buf,
    out_sem,
):
    c_copies = fetched(weights, 3, 3 * LANES, 4 * LANES, c_buf, c_sem)
    win = fetched(more, 0, 0, D, in_buf, in_sem), in_buf
    wout = fetched(more, 1, 0, D, out_buf, out_sem), out_buf
    rows = x2_ref.shape[0]
    first, second, count = read_stats(stat_ref)
    mean = first / count
    inverse = lax.rsqrt(second / count - mean * mean + norm_eps)
    yhat = (hidden_ref[...] - mean) * inverse
    yhat_ref[...] = yhat
    c = yhat * vec_ref[10:11, :] + vec_ref[11:12, :]
    sig = sigmoid(c)
    act = (c * sig).astype(bf16)
    act_ref[...] = act
    x3 = x2_ref[...]
    for m in range(NPIECE):
        c_copies[m].wait()
        x3 += nt(act[:, LANES * m : LANES * m + LANES], block(c_buf, m))
    x4 = ffn_forward(x3, vec_ref, 3, win, wout, pre_ref, n4_ref)
    normed = layer_norm(x4, vec_ref[4:5, :], vec_ref[9:10, :]).astype(bf16)
    logits = nn(normed, head_ref[...])
    column = lax.broadcasted_iota(jnp.int32, logits.shape, 1)
    logits = jnp.where(column < CLASSES, logits, -1e30)
    top = jnp.max(logits, -1, keepdims=True)
    total = top + jnp.log(jnp.sum(jnp.exp(logits - top), -1, keepdims=True))
    hit = column == label_ref[...]
    picked = jnp.sum(jnp.where(hit, logits, 0.0), -1, keepdims=True)
    weight = weight_ref[...]
    loss = jnp.sum(weight * (total - picked), 0, keepdims=True)
    g_logits = (jnp.exp(logits - total) - hit.astype(f32)) * (weight / count)
    g_logits = g_logits.astype(bf16)
    g_head_ref[...] = tn(normed, g_logits).astype(bf16)
    dx4, gain, shift = layer_norm_back(x4, vec_ref[4:5, :], nt(g_logits, head_ref[...]))
    vgrad_ref[0:1, :] = gain
    vgrad_ref[1:2, :] = shift
    dx3, gain, shift = ffn_backward(
        dx4,
        x3,
        vec_ref,
        3,
        in_buf,
        out_buf,
        pre_ref,
        n4_ref,
        core_pieces(spot),
        lambda c, *place: write_core_piece((keep_ref, send_ref)[c], *place),
    )
    vgrad_ref[2:3, :] = gain
    vgrad_ref[3:4, :] = shift
    dx3_ref[...] = dx3
    low = dx3.astype(bf16)
    valid = valid_ref[...]
    parts = []
    for m in range(NPIECE):
        lanes = slice(LANES * m, LANES * m + LANES)
        slope = sig[:, lanes] * (1.0 + c[:, lanes] * (1.0 - sig[:, lanes]))
        dc = nn(low, block(c_buf, m)) * slope
        vgrad_ref[4:5, lanes] = jnp.sum(dc * yhat[:, lanes], 0, keepdims=True)
        vgrad_ref[5:6, lanes] = jnp.sum(dc, 0, keepdims=True)
        dy = dc * vec_ref[10:11, lanes]
        dy_ref[:, lanes] = dy
        kept = dy * valid
        parts.append(
            (
                jnp.sum(kept, 0, keepdims=True),
                jnp.sum(kept * yhat[:, lanes], 0, keepdims=True),
            )
        )
    for k, ref in enumerate((dy_ref, yhat_ref)):
        low_ref[HALO * k : HALO * k + HALO, :] = ref[0:HALO, :]
        high_ref[HALO * k : HALO * k + HALO, :] = ref[rows - HALO :, :]
    write_stats(
        part_ref,
        jnp.concatenate([a for a, _ in parts], 1),
        jnp.concatenate([b for _, b in parts], 1),
        loss,
    )


def conv_back_kernel(
    weights,
    dy_ref,
    yhat_ref,
    prev_ref,
    next_ref,
    part_ref,
    stat_ref,
    wide_valid_ref,
    gprev_ref,
    gated_ref,
    gnext_ref,
    ga_ref,
    gb_ref,
    x2_ref,
    dx3_ref,
    vec_ref,
    dgate_ref,
    dx2_ref,
    vgrad_ref,
    loss_ref,
    wide,
    wide_y,
    dh,
    buf,
    sem,
):
    copies = fetched(weights, 3, 0, 2 * LANES, buf, sem)
    rows = dy_ref.shape[0]
    first, second, count = read_stats(stat_ref)
    mean = first / count
    inverse = lax.rsqrt(second / count - mean * mean + norm_eps)
    first, second, loss = read_stats(part_ref)
    loss_ref[...] = loss / count
    wide[0:HALO, :] = prev_ref[0:HALO, :]
    wide[HALO : HALO + rows, :] = dy_ref[...]
    wide[HALO + rows :, :] = next_ref[0:HALO, :]
    wide_y[0:HALO, :] = prev_ref[HALO:, :]
    wide_y[HALO : HALO + rows, :] = yhat_ref[...]
    wide_y[HALO + rows :, :] = next_ref[HALO:, :]
    mean_part = (first + wide_y[...] * second) / count
    dh[...] = inverse * (wide[...] - wide_valid_ref[...] * mean_part)
    wide[0:HALO, :] = gprev_ref[...]
    wide[HALO : HALO + rows, :] = gated_ref[...]
    wide[HALO + rows :, :] = gnext_ref[...]
    half = KERNEL // 2
    own = dh[HALO : HALO + rows, :]
    d_gated = jnp.zeros((rows, D), f32)
    for k in range(KERNEL):
        d_gated += dh[HALO - k + half : HALO - k + half + rows, :] * vec_ref[14 + k : 15 + k, :]
        at = HALO + k - half
        vgrad_ref[2 + k : 3 + k, :] = jnp.sum(own * wide[at : at + rows, :], 0, keepdims=True)
    d_gated = d_gated * wide_valid_ref[HALO : HALO + rows, :]
    sig = sigmoid(gb_ref[...])
    dga = (d_gated * sig).astype(bf16)
    dgb = (d_gated * ga_ref[...] * sig * (1.0 - sig)).astype(bf16)
    back = jnp.zeros((rows, D), f32)
    for m in range(NPIECE):
        lanes = slice(LANES * m, LANES * m + LANES)
        both = jnp.concatenate([dga[:, lanes], dgb[:, lanes]], 1)
        dgate_ref[m] = both
        copies[m].wait()
        back += nt(both, block(buf, m))
    dx, gain, shift = layer_norm_back(x2_ref[...], vec_ref[2:3, :], back)
    vgrad_ref[0:1, :] = gain
    vgrad_ref[1:2, :] = shift
    dx2_ref[...] = dx3_ref[...] + dx


def back_kernel(
    weights,
    dx2_ref,
    prob_ref,
    kv_ref,
    qu_ref,
    qv_ref,
    pe_ref,
    dquery_ref,
    dkv_ref,
    dpe_ref,
    dall_ref,
    down_ref,
    vgrad_ref,
    dq,
    o_buf,
    o_sem,
    mix_buf,
    mix_sem,
):
    o_copies = fetched(weights, 3, 2 * LANES, 3 * LANES, o_buf, o_sem)
    mix_copies = fetched(weights, 2, 0, 3 * LANES, mix_buf, mix_sem)
    rows, length = dx2_ref.shape[0], dall_ref.shape[0]
    low = dx2_ref[...].astype(bf16)
    flip = flip_matrix(rows)
    turned_q = nn(flip, qv_ref[...]).astype(bf16)
    for h in range(HEADS):
        m, at, lanes = head_lanes(h)
        if at == 0:
            o_copies[m].wait()
            d_att = nn(low, block(o_buf, m)).astype(bf16)
        d_out = d_att[:, at : at + HEAD_DIM]
        prob = prob_ref[h]
        key = kv_ref[m, :, at : at + HEAD_DIM]
        value = kv_ref[m, :, LANES + at : LANES + at + HEAD_DIM]
        d_prob = nt(d_out, value)
        d_scores = prob * (d_prob - jnp.sum(prob * d_prob, -1, keepdims=True))
        d_raw = (d_scores * 0.125).astype(bf16)
        dkv_ref[m, :, LANES + at : LANES + at + HEAD_DIM] = tn(prob.astype(bf16), d_out).astype(bf16)
        dkv_ref[m, :, at : at + HEAD_DIM] = tn(d_raw, qu_ref[:, lanes]).astype(bf16)
        dq[0:rows, lanes] = nn(d_raw, key)
        turned = nn(flip, d_raw)
        turned = jnp.concatenate([turned, jnp.zeros((rows, rows), f32)], 1)
        turned = pltpu.roll(turned, 0, 1, stride=1, stride_axis=0).astype(bf16)
        dq[rows : 2 * rows, lanes] = nn(turned, pe_ref[:, lanes])
        dpe_ref[:, lanes] = tn(turned, turned_q[:, lanes]).astype(bf16)
    d_u, d_v = dq[0:rows, :], dq[rows : 2 * rows, :]
    vgrad_ref[0:1, :] = jnp.sum(d_u, 0, keepdims=True)
    vgrad_ref[1:2, :] = jnp.sum(d_v, 0, keepdims=True)
    straight = jnp.dot(
        flip.astype(f32), d_v, precision=lax.Precision.HIGHEST, preferred_element_type=f32
    )
    dquery = (d_u + straight).astype(bf16)
    dquery_ref[...] = dquery
    d_all = jnp.zeros((length, D), f32)
    d_own = jnp.zeros((rows, D), f32)
    for m in range(NPIECE):
        mix_copies[m].wait()
        d_own += nt(dquery[:, LANES * m : LANES * m + LANES], block(mix_buf, m, slice(0, LANES)))
        d_all += nt(dkv_ref[m], block(mix_buf, m, slice(LANES, 3 * LANES)))
    dall_ref[...] = d_all.astype(bf16)
    down_ref[...] = d_own


def mix_grad_kernel(
    spot,
    dx2_ref,
    dx3_ref,
    dgate_ref,
    n3_ref,
    act_ref,
    att_ref,
    n2_ref,
    all_ref,
    table_ref,
    dquery_ref,
    dkv_ref,
    dpe_ref,
    *parts,
):
    low = dx2_ref[...].astype(bf16)
    low_three = dx3_ref[...].astype(bf16)
    for c, x, m in pieces(spot):
        lanes = aligned(LANES * m)
        grads = [
            tn(n2_ref[...], dquery_ref[:, lanes]),
            tn(all_ref[...], dkv_ref[m]),
            tn(table_ref[...], dpe_ref[:, lanes]),
        ]
        write_piece(spot, parts[c], 0, x, jnp.concatenate(grads, 1))
        grads = [
            tn(n3_ref[...], dgate_ref[m]),
            tn(low, att_ref[:, lanes]),
            tn(low_three, act_ref[:, lanes]),
        ]
        write_piece(spot, parts[c], 1, x, jnp.concatenate(grads, 1))


def last_kernel(
    spot,
    weights,
    dx2_ref,
    d_all_ref,
    d_own_ref,
    x1_ref,
    x0_ref,
    pre_ref,
    n1_ref,
    vec_ref,
    keep_ref,
    send_ref,
    dx0_ref,
    vgrad_ref,
    in_buf,
    in_sem,
    out_buf,
    out_sem,
):
    copies = fetched(weights, 0, 0, D, in_buf, in_sem)
    copies += fetched(weights, 1, 0, D, out_buf, out_sem)
    grad = total(*[d_all_ref[k] for k in range(d_all_ref.shape[0])]) + d_own_ref[...]
    dx, gain, shift = layer_norm_back(x1_ref[...], vec_ref[1:2, :], grad)
    vgrad_ref[0:1, :] = gain
    vgrad_ref[1:2, :] = shift
    for copy in copies:
        copy.wait()
    dx0, gain, shift = ffn_backward(
        dx2_ref[...] + dx,
        x0_ref[...],
        vec_ref,
        0,
        in_buf,
        out_buf,
        pre_ref,
        n1_ref,
        pieces(spot),
        lambda c, x, half, grad: write_piece(spot, (keep_ref, send_ref)[c], half, x, grad),
    )
    vgrad_ref[2:3, :] = gain
    vgrad_ref[3:4, :] = shift
    dx0_ref[...] = dx0.astype(bf16)


def adam(state, grad, rate):
    first_new = beta_one * state[1] + (1.0 - beta_one) * grad
    second_new = beta_two * state[2] + (1.0 - beta_two) * grad * grad
    direction = (
        first_new
        / (1.0 - beta_one**STEP)
        / (jnp.sqrt(second_new / (1.0 - beta_two**STEP)) + adam_eps)
    )
    weight_new = state[0] - rate * (direction + decay_rate * state[0])
    return (weight_new, first_new, second_new)


def small_rate(positions):
    rate = jnp.full(positions.shape, small_rates[-1], f32)
    for k in range(3, -1, -1):
        rate = jnp.where(positions < sum(SIZES[: k + 1]), small_rates[k], rate)
    return rate


def mel_windows(mel, utter_len, rank, tokens):
    frame = rank * (8 * tokens) + jnp.arange(8 * tokens, dtype=jnp.int32)
    kept = jnp.where((frame < utter_len)[:, None], mel, jnp.zeros((), bf16))
    prior = passed_along(kept[-8:], 1)
    rows = tokens + EDGE
    field = jnp.concatenate([jnp.zeros((8 * (EDGE - 1), MEL), bf16), prior, kept], 0)
    field = field.reshape(rows, 8, MEL).transpose(1, 2, 0)
    lag = jnp.concatenate([jnp.zeros((1, MEL, 1), bf16), field[7:8, :, :-1]], 2)
    field = jnp.concatenate([lag, field], 0)
    field = jnp.pad(field, ((0, 0), (1, 1), (0, 0))).reshape(9, F1 + 1, 2, rows)
    bands = [field[:, :F1, 0], field[:, :F1, 1], field[:, 1:, 0]]
    taps = [bands[df][dt : dt + 7 : 2] for dt in range(3) for df in range(3)]
    taps = jnp.stack(taps + [jnp.zeros_like(taps[0])] * 7, 0)
    turned = taps.transpose(0, 2, 1, 3).reshape(16, F1 * 4 * rows)
    wide = taps.reshape(16, 4, F1 // 8, 8, rows).transpose(2, 1, 4, 3, 0)
    return wide.reshape(F1 // 8, 4 * rows, LANES), turned


def position_table(rank, rows, length):
    distance = (rows * rank + rows - 1 - jnp.arange(rows + length)).astype(f32)[:, None]
    inverse_freq = jnp.exp(jnp.arange(D // 2).astype(f32) * (-2.0 * math.log(10000.0) / D))
    angles = distance * inverse_freq[None, :]
    return jnp.concatenate([jnp.sin(angles), jnp.cos(angles)], 1).astype(bf16)


def gathered_heads(n2, planned_mesh):
    if not planned_mesh:
        return lax.all_gather(n2, "mp", axis=0, tiled=True)
    rows = n2.shape[0]
    pair = jnp.stack([n2, sent(n2, "x")])
    both = jnp.stack([pair, sent(pair, "c")])
    rank = lax.axis_index("mp")
    order = [(rank % 2, rank // 2)]
    whole = jnp.zeros((4, rows, D), bf16)
    c, x = order[0]
    for i in range(2):
        for j in range(2):
            at = ((x + j) % 2) * 2 + (c + i) % 2
            whole = lax.dynamic_update_slice(whole, both[i, j][None], (at, 0, 0))
    return whole.reshape(4 * rows, D)


def body(mel, lengths, alignment, loss_mask, ff_in, ff_out, mix_in, mix_out, small):
    n_dp, n_mp = lax.axis_size("dp"), lax.axis_size("mp")
    ndev = n_dp * n_mp
    plan = planned(n_dp, n_mp)
    rank, dp_rank = lax.axis_index("mp"), lax.axis_index("dp")
    device = lax.axis_index(("dp", "mp"))
    tokens = alignment.shape[1]
    length = tokens * n_mp
    rows = tokens + EDGE
    own_rows = ff_in.shape[2]
    shard = small.shape[1]
    half = -(-(-(-(shard + 16 * LANES - 1) // LANES)) // 32) * 16
    chunk = 2 * half
    flat_rows = max((shard * (ndev - 1)) // (16 * LANES) * 16 + chunk, NROWS)
    flat_rows = -(-flat_rows // 8) * 8
    if plan:
        spot = jnp.stack([rank % 2, rank // 2, dp_rank % 2, dp_rank // 2])
        deep, lines = LINES, n_dp // LINES
    else:
        spot = jnp.zeros((4,), jnp.int32)
        deep, lines = 1, 1
    spot = spot.astype(jnp.int32), pltpu.SMEM
    piece_rows = D // (deep * lines)
    small_rows = half * (n_dp // (deep * lines))

    row = first_row(shard, device)
    offset = shard * device - row * LANES
    small_low = lax.dynamic_update_slice_in_dim(
        jnp.zeros((chunk * LANES,), bf16), small[0].astype(bf16), offset, 0
    ).reshape(chunk, LANES)
    in_low = ff_in[0].astype(bf16)
    out_low = ff_out[0].astype(bf16).transpose(0, 2, 1)
    mix_low = mix_in[0].astype(bf16)
    mixo_low = mix_out[0].astype(bf16).transpose(0, 2, 1)
    qkvp_low = mix_low[:, 0:4].reshape(own_rows, 4 * LANES)
    abo_low = jnp.concatenate([mix_low[:, 4], mix_low[:, 5], mixo_low[0], mixo_low[1]], 1)
    def gathered(low):
        whole = lax.all_gather(jnp.stack(low), ("dp", "mp"), axis=0)
        whole = whole.reshape(n_dp, n_mp, len(low), own_rows, D)
        if not plan:
            whole = whole.transpose(1, 2, 0, 3, 4).reshape(1, n_mp, len(low), D, D)
        return whole

    big_all = gathered([in_low[0], out_low[0], qkvp_low, abo_low])
    more_all = gathered([in_low[1], out_low[1]])
    weights, more = (big_all, pl.ANY), (more_all, pl.ANY)
    utter_len = lengths[0]
    windows, windows_t = mel_windows(mel[0], utter_len, rank, tokens)
    table = position_table(rank, tokens, length)
    if plan:
        few_all = Gathered(small_low)
        few_all.lines(), few_all.after(windows, windows_t, table).first(), few_all.second()
        small_all = few_all.cores()
    else:
        small_all = [lax.all_gather(small_low, ("dp", "mp"), axis=0)]

    frames = jnp.arange(length, dtype=jnp.int32)
    keep_row = (8 * frames < utter_len).astype(f32)[None, :]
    wide_frame = rank * tokens - HALO + jnp.arange(tokens + 2 * HALO, dtype=jnp.int32)
    wide_valid = (wide_frame >= 0) & (wide_frame < length) & (8 * wide_frame < utter_len)
    wide_valid = wide_valid.astype(f32)[:, None]
    valid = wide_valid[HALO : HALO + tokens]
    weight = valid * loss_mask[0].astype(f32)[:, None]

    def split(each):
        return [((COLS, deep, lines, each, D), bf16)] * 4

    unpack = functools.partial(unpack_kernel if plan else unpack_whole_kernel, shard)
    taps, tap_one, pointwise, linear, head, vec = call(
        unpack,
        [
            ((32, CHANNELS), f32),
            ((8, LANES, CHANNELS), bf16),
            ((2, CHANNELS, CHANNELS), bf16),
            ((F3, CHANNELS, D), bf16),
            ((D, CPAD), bf16),
            ((24, D), f32),
        ],
        ([spot] if plan else []) + small_all,
        [pltpu.VMEM((flat_rows, LANES), f32)],
        us=7,
        name="unpack",
    )
    x0, front, mid, last = call(
        stem_kernel,
        [
            ((tokens, D), f32),
            ((F2, 2 * rows, CHANNELS), bf16),
            ((F3, tokens, CHANNELS), bf16),
            ((F3, tokens, CHANNELS), bf16),
        ],
        [windows, tap_one, taps, pointwise, (linear, pl.ANY)],
        stem_scratch(rows),
        us=13,
        out_any=(1,),
        name="stem",
    )
    x1, pre_one, n1, n2 = call(
        first_kernel,
        [
            ((tokens, D), f32),
            ((n_mp, tokens, D), f32),
            ((tokens, D), bf16),
            ((tokens, D), bf16),
        ],
        [weights, x0, vec],
        buffers(big_all, D, D),
        us=6,
        name="first",
    )
    n_all = gathered_heads(n2, plan)
    pe, qu, qv = call(
        position_kernel,
        [((tokens + length, D), bf16), ((tokens, D), bf16), ((tokens, D), bf16)],
        [weights, table, n2, vec],
        buffers(big_all, LANES, LANES),
        us=5,
        name="position",
    )
    x2, kv, prob, att, n3, ga, gb, gated, g_low, g_high = call(
        attention_kernel,
        [
            ((tokens, D), f32),
            ((n_mp, length, 2 * LANES), bf16),
            ((HEADS, tokens, length), f32),
            ((tokens, D), bf16),
            ((tokens, D), bf16),
            ((tokens, D), f32),
            ((tokens, D), f32),
            ((tokens, D), f32),
            ((HALO, D), f32),
            ((HALO, D), f32),
        ],
        [weights, n_all, x1, qu, qv, pe, vec, keep_row, valid],
        buffers(big_all, 2 * LANES, 3 * LANES),
        us=10,
        name="attention",
    )
    g_prev, g_next = passed_along(g_high, 1), passed_along(g_low, -1)
    stat_shape = ((ndev, 16, LANES), f32)
    wide = pltpu.VMEM((tokens + 2 * HALO, D), f32)
    hidden, stat = call(
        conv_kernel,
        [((tokens, D), f32), stat_shape],
        [g_prev, gated, g_next, vec, valid],
        [wide],
        us=2,
        name="conv",
    )
    stat = spread(stat)
    two_keep, two_send, g_head, dx3, act, dy, yhat, b_low, b_high, part, vg_mid = call(
        middle_kernel,
        [
            *[((n_dp if plan else 1, COLS, 2, own_rows if plan else D, D), bf16)] * 2,
            ((D, CPAD), bf16),
            ((tokens, D), f32),
            ((tokens, D), bf16),
            ((tokens, D), f32),
            ((tokens, D), f32),
            ((2 * HALO, D), f32),
            ((2 * HALO, D), f32),
            stat_shape,
            ((6, D), f32),
        ],
        [spot, weights, more, hidden, stat, x2, head, vec, alignment[0][:, None], weight, valid],
        [
            pltpu.VMEM((n_mp, tokens, D), f32),
            pltpu.VMEM((tokens, D), bf16),
            *buffers(big_all, LANES, D, D),
        ],
        us=13,
        name="middle",
    )
    b_prev, b_next = passed_along(b_high, 1), passed_along(b_low, -1)
    part = spread(part)
    two_both, own_two = reduced_cores(two_keep, two_send, plan)
    dgate, dx2, vg_conv, loss = call(
        conv_back_kernel,
        [
            ((n_mp, tokens, 2 * LANES), bf16),
            ((tokens, D), f32),
            ((11, D), f32),
            ((1, 1), f32),
        ],
        [
            weights,
            dy,
            yhat,
            b_prev,
            b_next,
            part,
            stat,
            wide_valid,
            g_prev,
            gated,
            g_next,
            ga,
            gb,
            x2,
            dx3,
            vec,
        ],
        [wide, wide, wide, *buffers(big_all, 2 * LANES)],
        us=4,
        name="conv_back",
    )
    dquery, dkv, dpe, d_all, d_own, vg_att = call(
        back_kernel,
        [
            ((tokens, D), bf16),
            ((n_mp, length, 2 * LANES), bf16),
            ((tokens + length, D), bf16),
            ((length, D), bf16),
            ((tokens, D), f32),
            ((2, D), f32),
        ],
        [weights, dx2, prob, kv, qu, qv, pe],
        [pltpu.VMEM((2 * tokens, D), f32), *buffers(big_all, LANES, 3 * LANES)],
        us=10,
        after=two_both,
        name="back",
    )
    if plan:
        pair = d_all.reshape(2, 2, tokens, D)
        core, col = rank % 2, rank // 2
        other = lax.dynamic_slice_in_dim(pair, 1 - core, 1, 1)[:, 0]
        own = lax.dynamic_slice_in_dim(pair, core, 1, 1)[:, 0]
        pair = low_total(own, sent(other, "c"))
        wait = [pair]
        other = lax.dynamic_slice_in_dim(pair, 1 - col, 1, 0)
        own = lax.dynamic_slice_in_dim(pair, col, 1, 0)
        d_mine = jnp.concatenate([own, sent(other, "x")], 0)
    else:
        d_mine = lax.psum_scatter(d_all, "mp", scatter_dimension=0, tiled=True)[None]
        wait = ()
    one_way = [((COLS, deep, lines, 2 * piece_rows, D), bf16)] * 2
    mix = call(
        mix_grad_kernel,
        one_way,
        [spot, dx2, dx3, dgate, n3, act, att, n2, n_all, table, dquery, dkv, dpe],
        us=7,
        after=wait,
        name="mix_grad",
    )
    mix_sum = ReducedOneWay(*mix, "xy")
    *one, dx0, vg_last = call(
        last_kernel,
        [*one_way, ((tokens, D), bf16), ((4, D), f32)],
        [spot, weights, dx2, d_mine, d_own, x1, x0, pre_one, n1, vec],
        buffers(big_all, D, D),
        us=8,
        after=mix[:1],
        name="last",
    )
    one_sum = ReducedOneWay(*one, "yx")
    few_parts = call(
        functools.partial(pack_kernel, shard, n_dp),
        [((COLS, deep, lines, small_rows, LANES), bf16)] * 4,
        [spot, last, dx0, g_head],
        [
            pltpu.VMEM((flat_rows, LANES), f32),
            pltpu.VMEM((4, COLS, deep, lines, small_rows, LANES), bf16),
            pltpu.SemaphoreType.DMA((4,)),
        ],
        out_any=(0, 1, 2, 3),
        us=5,
        after=mix_sum.cores() if plan else (),
        name="pack",
    )
    few_sum = Reduced(*few_parts)
    g_pw, sums, g_one = call(
        stem_back_kernel,
        [
            ((2, CHANNELS, CHANNELS), f32),
            ((18, 8, CHANNELS), f32),
            ((16, CHANNELS), f32),
        ],
        [
            dx0,
            (windows, pl.ANY),
            (windows_t, pl.ANY),
            tap_one,
            taps,
            pointwise,
            (linear, pl.ANY),
            (front, pl.ANY),
            (mid, pl.ANY),
            (last, pl.ANY),
        ],
        back_scratch(rows),
        us=27,
        after=one_sum.cores() if plan else (),
        name="stem_back",
    )
    used = ROW_AT[2] + ROWS[4]
    share = -(-(-(-used // ndev)) // 16) * 16
    (few,) = call(
        stem_rows_kernel,
        [((ndev * share, LANES), bf16)],
        [g_pw, sums, g_one, vg_last, vg_conv, vg_mid, vg_att],
        [pltpu.VMEM((ndev * share, LANES), f32)],
        us=2,
        after=mix_sum.first() + one_sum.first() + few_sum.cores() if plan else (),
        name="stem_rows",
    )
    few = jnp.sum(spread(few.reshape(ndev, share, LANES)).astype(f32), 0)

    if plan:
        mix_sum.second()
        own_mix, own_abo = mix_sum.lines()
        few_sum.first()
        one_sum.second()
        own_in_one, own_out_one = one_sum.lines()
        few_sum.second()
        own_few = few_sum.lines()
    else:

        def halves(keep, send):
            return [x[..., D * k : D * k + D, :] for x in (keep, send) for k in range(2)]

        own_mix, own_abo = reduced_whole(halves(*mix), own_rows)
        own_in_one, own_out_one = reduced_whole(halves(*one), own_rows)
        own_few = reduced_whole(few_parts, half)
    own_chunk = jnp.concatenate(own_few, 0)

    own_in_two, own_out_two = held(own_two, [few]).reshape(2, own_rows, D).astype(f32)
    start = shard * device
    positions = start + jnp.arange(shard, dtype=jnp.int32)
    own = [own_in_one, own_out_one, own_mix, own_abo, own_in_two, own_out_two]
    packed = lax.dynamic_slice_in_dim(own_chunk.reshape(-1), offset, shard, 0)
    local_sq = sum(jnp.sum(grad * grad) for grad in own) + jnp.sum(packed * packed)
    high = local_sq.astype(bf16)
    rest = local_sq - high.astype(f32)
    middle = rest.astype(bf16)
    lowest = (rest - middle.astype(f32)).astype(bf16)
    lane = jnp.arange(LANES)[None, :]
    number = jnp.where(lane == 0, high, jnp.where(lane == 1, middle, jnp.where(lane == 2, lowest, 0)))
    number = jnp.broadcast_to(number, (16, LANES)).astype(bf16)
    known = jnp.concatenate([few.astype(bf16), number], 0)
    known = spread(jnp.broadcast_to(known[None], (ndev, share + 16, LANES))).astype(f32)
    few = known[:, :share].reshape(ndev * share, LANES)
    total_sq = jnp.sum(known[:, share, 0:3]) + jnp.sum(few * few)
    grad_norm = jnp.sqrt(total_sq)
    factor = clip_norm / jnp.maximum(grad_norm, clip_norm)

    rows_of = row + jnp.arange(chunk, dtype=jnp.int32)[:, None]
    few = jnp.concatenate([few, jnp.zeros((chunk, LANES), f32)], 0)

    def window(begin, end, at):
        start_at = jnp.clip(row - begin + at, 0, few.shape[0] - chunk)
        part = lax.dynamic_slice_in_dim(few, start_at, chunk, 0)
        return jnp.where((rows_of >= begin) & (rows_of < end), part, 0.0)

    own_chunk = own_chunk + window(0, ROW_AT[2], 0) + window(ROW_AT[4], NROWS, ROW_AT[2])
    own_small = lax.dynamic_slice_in_dim(own_chunk.reshape(-1), offset, shard, 0)

    grad_in = jnp.stack([own_in_one, own_in_two])
    grad_out = jnp.stack([own_out_one, own_out_two]).transpose(0, 2, 1)
    grad_mix = jnp.concatenate([own_mix, own_abo[:, : 2 * LANES]], 1).reshape(own_rows, 6, LANES)
    grad_mixo = own_abo[:, 2 * LANES :].reshape(own_rows, 2, LANES).transpose(1, 2, 0)
    rates = (0.1, 0.05, 0.1, jnp.array([1.0, 0.1], f32)[:, None, None])
    states = (ff_in, ff_out, mix_in, mix_out)
    grads = (grad_in, grad_out, grad_mix, grad_mixo)
    outs = []
    for state, grad, rate in zip(states, grads, rates):
        outs.extend(adam(state, grad * factor, rate))
    outs.extend(adam(small, own_small * factor, small_rate(positions)))
    vec_grad = few[ROW_AT[2] : used].reshape(23, D) * factor
    return (*outs, vec_grad, loss[0, 0], grad_norm)


def solution(mesh):
    in_specs = (
        P("dp", "mp", None),
        P("dp"),
        P("dp", "mp"),
        P("dp", "mp"),
        P(None, None, "dp", "mp"),
        P(None, None, "mp", "dp"),
        P(None, "dp", None, "mp"),
        P(None, None, "mp", "dp"),
        P(None, ("dp", "mp")),
    )
    in_block, out_block = P(None, "dp", "mp"), P(None, "mp", "dp")
    mix_block, flat = P("dp", None, "mp"), P(("dp", "mp"))
    out_specs = (
        (in_block,) * 3 + (out_block,) * 3 + (mix_block,) * 3 + (out_block,) * 3 + (flat,) * 3
    )
    out_specs = out_specs + (P(), P(), P())
    return jax.shard_map(body, mesh=mesh, in_specs=in_specs, out_specs=out_specs, check_vma=False)
```

```python
import functools
import math

import jax
import jax.numpy as jnp
from jax import lax
from jax.experimental import pallas as pl
from jax.experimental.pallas import tpu as pltpu
from jax.sharding import PartitionSpec as P

D = 512
HEADS = 8
HEAD_DIM = 64
CHANNELS = 256
MEL = 80
KERNEL = 9
CLASSES = 1025
STEP = 7
LANES = 128
NPIECE = 4
F1, F2, F3 = MEL // 2, MEL // 4, MEL // 8
CPAD = 1152
HALO = 8
EDGE = 16

norm_eps = 1e-05
clip_norm = 0.005
beta_one = 0.9
beta_two = 0.98
adam_eps = 1e-08
decay_rate = 0.01
small_rates = (0.8, 0.15, 0.05, 0.1, 0.3)
f32 = jnp.float32
bf16 = jnp.bfloat16

SIZES = [27 * CHANNELS, 2 * CHANNELS * CHANNELS, CHANNELS * F3 * D, D * CLASSES, 23 * D]
NSMALL = sum(SIZES)
ROWS = [size // LANES for size in SIZES]
ROW_AT = [sum(ROWS[:k]) for k in range(5)]
NROWS = NSMALL // LANES


CORES, COLS, LINES = 2, 2, 2


def planned(n_dp, n_mp):
    return (n_dp, n_mp) == (8, 4)


def sent(x, name, by=1):
    axis, stride, size = {
        "c": ("mp", 1, 2),
        "x": ("mp", 2, 2),
        "y": ("dp", 1, 2),
        "z": ("dp", 2, lax.axis_size("dp") // 2),
    }[name]
    pairs = []
    for i in range(lax.axis_size(axis)):
        k = (i // stride) % size
        pairs.append((i, i + (((k + by) % size) - k) * stride))
    return lax.ppermute(x, axis, pairs)


def held(values, others):
    return lax.optimization_barrier((values, others))[0] if others else values


def total(*parts):
    return functools.reduce(lambda a, b: a + b, [part.astype(f32) for part in parts])


def low_total(*parts):
    return total(*parts).astype(bf16)


class Reduced:
    def __init__(self, *parts):
        self.parts, self.deep = parts[:2], parts[0].shape[2]
        self.out = [parts[2], parts[3]]

    def cores(self):
        got = [sent(x, "c") for x in self.out]
        self.a, self.b = ([keep, more] for keep, more in zip(self.parts, got))
        self.out = [
            low_total(*[part[1] for part in self.a]),
            low_total(*[part[:, 1] for part in self.b]),
        ]
        return self.out

    def first(self):
        got_a, got_b = sent(self.out[0], "x"), sent(self.out[1], "y")
        self.a = [part[0] for part in self.a] + [got_a]
        self.b = [part[:, 0] for part in self.b] + [got_b]
        self.out = [
            low_total(*[part[1] for part in self.a]),
            low_total(*[part[1] for part in self.b]),
        ]
        return self.out

    def second(self):
        got_a, got_b = sent(self.out[0], "y"), sent(self.out[1], "x")
        self.a = [part[0] for part in self.a] + [got_a]
        self.b = [part[0] for part in self.b] + [got_b]
        self.out = [
            jnp.stack(
                [low_total(*[part[k] for part in self.a]), low_total(*[part[k] for part in self.b])]
            )
            for k in range(1, self.deep)
        ]
        return self.out

    def lines(self):
        got = [sent(x, "z", k + 1) for k, x in enumerate(self.out)]
        return [
            total(*[part[0] for part in side], *[x[k] for x in got])
            for k, side in enumerate((self.a, self.b))
        ]


class ReducedOneWay:
    def __init__(self, keep, send, axes):
        self.keep, self.out, self.axes = keep, send, axes

    def side(self, array, *index):
        index = dict(zip(self.axes, index))
        return array[tuple(index.get(axis, slice(None)) for axis in "xy")]

    def cores(self):
        self.got = sent(self.out, "c")
        self.out = low_total(self.side(self.keep, 1), self.side(self.got, 1))
        return [self.out]

    def first(self):
        self.more = sent(self.out, self.axes[0])
        self.out = low_total(self.side(self.keep, 0, 1), self.side(self.got, 0, 1), self.more[1])
        return [self.out]

    def second(self):
        last = sent(self.out, self.axes[1])
        self.parts = self.side(self.keep, 0, 0), self.side(self.got, 0, 0), self.more[0], last
        self.out = [low_total(*[x[k] for x in self.parts]) for k in range(1, last.shape[0])]
        return self.out

    def lines(self):
        got = [sent(x, "z", k + 1) for k, x in enumerate(self.out)]
        own = total(*[x[0] for x in self.parts], *got)
        rows = own.shape[0] // 2
        return [own[:rows], own[rows:]]


class Gathered:
    def __init__(self, low):
        self.low = low

    def after(self, *others):
        (self.a, self.b), _ = lax.optimization_barrier(((self.a, self.b), others))
        return self

    def lines(self):
        lines, rows = lax.axis_size("dp") // LINES, self.low.shape[0] // 2
        parts = [self.low] + [sent(self.low, "z", lines - k) for k in range(1, lines)]
        self.a = jnp.stack([part[:rows] for part in parts])
        self.b = jnp.stack([part[rows:] for part in parts])
        return [self.a, self.b]

    def first(self):
        self.a = jnp.stack([self.a, sent(self.a, "x")])
        self.b = jnp.stack([self.b, sent(self.b, "y")])
        return [self.a, self.b]

    def second(self):
        both = [self.a, sent(self.a, "y")], [self.b, sent(self.b, "x")]
        both = jnp.stack([jnp.stack(side) for side in both])
        self.mine = both.reshape((2, -1) + both.shape[4:])
        return [self.mine]

    def cores(self):
        return [self.mine, sent(self.mine, "c")]


def reduced_whole(parts, own_rows):
    own = []
    for keep, send in zip(parts[:2], parts[2:]):
        both = jnp.stack([keep, send], 1)[:, :, 0, 0]
        both = both.reshape((lax.axis_size("mp"), lax.axis_size("dp"), -1, keep.shape[-1]))
        both = lax.psum_scatter(both, "mp", scatter_dimension=0, tiled=True)
        both = lax.psum_scatter(both, "dp", scatter_dimension=1, tiled=True)
        own.append(both.reshape(own_rows, keep.shape[-1]).astype(f32))
    return own


def reduced_cores(keep, send, plan):
    if plan:
        both = low_total(keep, sent(send, "c"))
        ndev = lax.axis_size("dp") * lax.axis_size("mp")
        groups = [list(range(core, ndev, CORES)) for core in range(CORES)]
        both = both.reshape(ndev // CORES, 2, *both.shape[3:])
        own = lax.psum_scatter(
            both, ("dp", "mp"), scatter_dimension=0, axis_index_groups=groups, tiled=True
        )
        return [both], own
    both = jnp.stack([keep, send], 2)[0].reshape(lax.axis_size("mp"), 2, lax.axis_size("dp"), -1, D)
    both = lax.psum_scatter(both, "mp", scatter_dimension=0, tiled=True)
    both = lax.psum_scatter(both, "dp", scatter_dimension=2, tiled=True)
    return (), both


def spread(x):
    return lax.all_to_all(x, ("dp", "mp"), 0, 0, tiled=True)


def passed_along(x, by):
    peers = lax.axis_size("mp")
    pairs = [(i, i + by) for i in range(peers) if 0 <= i + by < peers]
    return lax.ppermute(x, "mp", pairs)


def call(kernel, outs, args, scratch=(), us=1, after=(), out_any=(), name=None):
    whole = pl.BlockSpec(memory_space=pltpu.VMEM)
    specs, arrays = [], []
    for arg in args:
        array, space = arg if isinstance(arg, tuple) else (arg, pltpu.VMEM)
        specs.append(pl.BlockSpec(memory_space=space))
        arrays.append(array)
    used = len(arrays)
    arrays += list(after)
    specs += [pl.BlockSpec(memory_space=pl.ANY)] * len(after)

    def run(*refs):
        kernel(*refs[:used], *refs[len(arrays) :])

    return pl.pallas_call(
        run,
        out_shape=[jax.ShapeDtypeStruct(shape, dtype) for shape, dtype in outs],
        in_specs=specs,
        out_specs=[pl.BlockSpec(memory_space=pl.ANY) if k in out_any else whole for k in range(len(outs))],
        scratch_shapes=list(scratch),
        compiler_params=pltpu.CompilerParams(vmem_limit_bytes=56 * 1024 * 1024),
        cost_estimate=pl.CostEstimate(
            flops=int(us * 1.15e9), bytes_accessed=int(us * 1e6), transcendentals=0
        ),
        name=name,
    )(*arrays)


def fetched(weights, which, lo, hi, buf, sem):
    copies = [
        pltpu.make_async_copy(weights.at[:, m, which, :, lo:hi], buf.at[m], sem.at[m])
        for m in range(buf.shape[0])
    ]
    for copy in copies:
        copy.start()
    return copies


def buffers(weights, *widths):
    deep, n_mp, _, rows, _ = weights.shape
    out = []
    for width in widths:
        out.append(pltpu.VMEM((n_mp, deep, rows, width), bf16))
        out.append(pltpu.SemaphoreType.DMA((n_mp,)))
    return out


def block(buf, m, lanes=slice(None)):
    part = buf[m, :, :, lanes]
    return part.reshape(part.shape[0] * part.shape[1], part.shape[2])


def aligned(at):
    return pl.ds(pl.multiple_of(at, LANES), LANES)


def pieces(spot):
    for c in range(CORES):
        for x in range(COLS):
            yield c, x, ((spot[1] + x) % COLS) * CORES + (spot[0] + c) % CORES


def core_pieces(spot):
    for c in range(CORES):
        for x in range(COLS):
            yield c, x, x * CORES + (spot[0] + c) % CORES


def write_core_piece(to, x, half, grad):
    rows = to.shape[3]
    grad = grad.astype(bf16)
    for k in range(to.shape[0]):
        to[k, x, half] = grad[rows * k : rows * k + rows]


def write_piece(spot, to, half, x, grad):
    _, deep, lines, rows, _ = to.shape
    rows = rows // 2
    grad = grad.astype(bf16)
    for z in range(lines):
        for y in range(deep):
            at = (z * deep + y) * rows
            index = x, (y + deep - spot[2]) % deep, (z + lines - spot[3]) % lines
            to[(*index, slice(rows * half, rows * half + rows))] = grad[at : at + rows]


def nn(left, right):
    return jnp.dot(left, right, preferred_element_type=f32)


def nt(left, right):
    return lax.dot_general(left, right, (((1,), (1,)), ((), ())), preferred_element_type=f32)


def tn(left, right):
    return lax.dot_general(left, right, (((0,), (0,)), ((), ())), preferred_element_type=f32)


def sigmoid(v):
    return 1.0 / (1.0 + jnp.exp(-v))


def layer_norm(x, gain, shift):
    centered = x - jnp.mean(x, -1, keepdims=True)
    rstd = lax.rsqrt(jnp.mean(centered * centered, -1, keepdims=True) + norm_eps)
    return centered * rstd * gain + shift


def layer_norm_back(x, gain, grad):
    centered = x - jnp.mean(x, -1, keepdims=True)
    rstd = lax.rsqrt(jnp.mean(centered * centered, -1, keepdims=True) + norm_eps)
    xhat = centered * rstd
    g = grad * gain
    dx = rstd * (
        g - jnp.mean(g, -1, keepdims=True) - xhat * jnp.mean(g * xhat, -1, keepdims=True)
    )
    return dx, jnp.sum(grad * xhat, 0, keepdims=True), jnp.sum(grad, 0, keepdims=True)


def eight(x):
    rows = x.shape[0] // 8
    return jnp.sum(x.reshape(rows, 8, x.shape[1]), 0)


def flip_matrix(size):
    at = lax.broadcasted_iota(jnp.int32, (size, size), 0)
    to = lax.broadcasted_iota(jnp.int32, (size, size), 1)
    return (at + to == size - 1).astype(bf16)


def first_row(shard, device):
    return lax.shift_left(lax.shift_right_logical(shard * device, 11), 4)


def rows_at(at, rows):
    return pl.ds(pl.multiple_of(at, 16), rows)


def piece_place(spot, c, half, q):
    i, j, z = q // 8, (q // 4) % 2, q % 4
    y, x = (j, i) if half else (i, j)
    dp = ((spot[3] + z) % 4) * LINES + (spot[2] + y) % LINES
    return dp, ((spot[1] + x) % COLS) * CORES + (spot[0] + c) % CORES


def unpack_kernel(
    shard, spot, mine_ref, other_ref, taps_ref, one_ref, pw_ref, lin_ref, head_ref, vec_ref, flat
):
    flat[...] = jnp.zeros_like(flat)
    rows = mine_ref.shape[2]
    for c, ref in enumerate((mine_ref, other_ref)):
        for half in range(2):

            def step(q, carry, c=c, ref=ref, half=half):
                dp, mp = piece_place(spot, c, half, q)
                at = first_row(shard, dp * (COLS * CORES) + mp) + rows * half
                flat[rows_at(at, rows), :] += ref[half, q].astype(f32)
                return carry

            lax.fori_loop(0, ref.shape[1], step, 0)
    unpack_flat(flat, taps_ref, one_ref, pw_ref, lin_ref, head_ref, vec_ref)


def unpack_whole_kernel(
    shard, all_ref, taps_ref, one_ref, pw_ref, lin_ref, head_ref, vec_ref, flat
):
    flat[...] = jnp.zeros_like(flat)
    rows = all_ref.shape[1]

    def step(device, carry):
        flat[rows_at(first_row(shard, device), rows), :] += all_ref[device].astype(f32)
        return carry

    lax.fori_loop(0, all_ref.shape[0], step, 0)
    unpack_flat(flat, taps_ref, one_ref, pw_ref, lin_ref, head_ref, vec_ref)


def unpack_flat(flat, taps_ref, one_ref, pw_ref, lin_ref, head_ref, vec_ref):
    one_ref[...] = jnp.zeros_like(one_ref)
    taps_ref[...] = jnp.zeros_like(taps_ref)
    vec_ref[...] = jnp.zeros_like(vec_ref)
    for h in range(2):
        lanes = slice(LANES * h, LANES * h + LANES)
        taps = flat[pl.ds(h, 27, stride=2), :]
        taps_ref[0:27, lanes] = taps
        padded = jnp.concatenate([taps[0:9], jnp.zeros((7, LANES), f32)], 0).astype(bf16)
        for k in range(8):
            one_ref[k, 16 * k : 16 * k + 16, lanes] = padded
        for k in range(2):
            part = flat[pl.ds(ROW_AT[1] + 512 * k + h, CHANNELS, stride=2), :]
            pw_ref[k, :, lanes] = part.astype(bf16)
    for j in range(4):
        lanes = slice(LANES * j, LANES * j + LANES)
        for f in range(F3):
            part = flat[pl.ds(ROW_AT[2] + 1024 * f + j, CHANNELS, stride=4), :]
            lin_ref[f, :, lanes] = part.astype(bf16)
        vec_ref[0:23, lanes] = flat[pl.ds(ROW_AT[4] + j, 23, stride=4), :]
    flip = flip_matrix(LANES)
    column = lax.broadcasted_iota(jnp.int32, (LANES, CPAD), 1)
    for q in range(D // LANES):
        at = ROW_AT[3] + 1025 * q
        wide = jnp.concatenate(
            [flat[pl.ds(at + c, LANES, stride=8), :] for c in range(CPAD // LANES)], 1
        )
        turned = nn(flip, wide.astype(bf16))
        turned = pltpu.roll(turned, CPAD - LANES + 1, 1, stride=1, stride_axis=0)
        turned = jnp.where(column < CLASSES, turned, 0.0)
        head_ref[LANES * q : LANES * q + LANES, :] = nn(flip, turned.astype(bf16)).astype(bf16)


def pack_kernel(shard, n_dp, spot, last_ref, dx_ref, dhead_ref, *refs):
    outs, flat, parts, sem = refs[:4], refs[4], refs[5], refs[6]
    dx = dx_ref[...]
    flat[0 : ROW_AT[2], :] = jnp.zeros((ROW_AT[2], LANES), f32)
    flat[ROW_AT[4] :, :] = jnp.zeros((flat.shape[0] - ROW_AT[4], LANES), f32)
    for f in range(F3):
        grad = tn(last_ref[f], dx)
        for j in range(4):
            flat[pl.ds(ROW_AT[2] + 1024 * f + j, CHANNELS, stride=4), :] = grad[
                :, LANES * j : LANES * j + LANES
            ]
    for q in range(D // LANES):
        at = ROW_AT[3] + 1025 * q
        turned = pltpu.roll(
            dhead_ref[LANES * q : LANES * q + LANES, :].astype(f32), 0, 1, stride=1, stride_axis=0
        )
        flat[pl.ds(at + 8, LANES, stride=8), :] = turned[:, 8 * LANES :]
        flat[at : at + 1, :] = turned[0:1, 0:LANES]
        flat[pl.ds(at + 8, LANES - 1, stride=8), :] += turned[1:, 0:LANES]
        for c in range(1, 8):
            flat[pl.ds(at + c, LANES, stride=8), :] = turned[:, LANES * c : LANES * c + LANES]
    _, _, deep, lines, rows, _ = parts.shape
    copies = []
    each = n_dp // (deep * lines)
    rows = rows // each
    for c in range(CORES):

        def step(q, carry, c=c):
            k = q % each
            z, y, x = (q // each) % lines, (q // (each * lines)) % deep, q // (each * lines * deep)
            mp = ((spot[1] + x) % COLS) * CORES + (spot[0] + c) % CORES
            dp = ((spot[3] + z) % lines) * deep + (spot[2] + y) % deep + k
            row = first_row(shard, dp * (COLS * CORES) + mp)
            for half in range(2):
                part = flat[rows_at(row + rows * half, rows), :]
                parts[half + 2 * c, x, y, z, rows_at(rows * k, rows), :] = part.astype(bf16)
            return carry

        lax.fori_loop(0, COLS * deep * lines * each, step, 0)
        for half in range(2):
            part = half + 2 * c
            copies.append(pltpu.make_async_copy(parts.at[part], outs[part], sem.at[part]))
            copies[-1].start()
    for copy in copies:
        copy.wait()


def stem_chunks(rows):
    for lane in range(0, CHANNELS, LANES):
        for at in range(0, rows, 48):
            yield slice(lane, lane + LANES), at


def stem_scratch(rows):
    return [
        pltpu.VMEM((5, 4 * rows, CHANNELS), f32),
        pltpu.VMEM((F2, 2 * rows, CHANNELS), f32),
        pltpu.VMEM((rows + 8, CHANNELS), f32),
        pltpu.VMEM((rows - EDGE, F3 * CHANNELS), bf16),
        pltpu.VMEM((F3, CHANNELS, D), bf16),
        pltpu.VMEM((F2, 2 * rows, CHANNELS), bf16),
        pltpu.SemaphoreType.DMA((2,)),
    ]


def first_rows(win_ref, one_ref, f):
    return jax.nn.relu(nn(win_ref[f // 8], one_ref[f % 8]))


def staged(sources, targets, sem):
    copies = [pltpu.make_async_copy(s, t, sem.at[k]) for k, (s, t) in enumerate(zip(sources, targets))]
    for copy in copies:
        copy.start()
    return copies


def stem_kernel(
    win_ref,
    one_ref,
    taps_ref,
    pw_ref,
    lin_hbm,
    x0_ref,
    front_hbm,
    mid_ref,
    last_ref,
    t_ref,
    r_ref,
    lag_ref,
    flat,
    lin_ref,
    front_ref,
    sem,
):
    rows = lag_ref.shape[0] - 8
    (lin_copy,) = staged([lin_hbm], [lin_ref], sem.at[pl.ds(0, 1)])
    lag_ref[0:8, :] = jnp.zeros((8, CHANNELS), f32)
    t_ref[4] = jnp.zeros_like(t_ref[4])

    def second(slots, to):
        for lanes, at in stem_chunks(rows):

            def tap(k):
                return taps_ref[k : k + 1, lanes]

            lag, even, odd = 0.0, 0.0, 0.0
            for df, slot in enumerate(slots):
                t0, t1, t2, t3 = (
                    t_ref[slot, a * rows + at : a * rows + at + 48, lanes] for a in range(4)
                )
                lag += t3 * tap(9 + df)
                even += t0 * tap(12 + df) + t1 * tap(15 + df)
                odd += t1 * tap(9 + df) + t2 * tap(12 + df) + t3 * tap(15 + df)
            lag_ref[8 + at : 56 + at, lanes] = lag
            even += lag_ref[7 + at : 55 + at, lanes]
            front_ref[to, at : at + 48, lanes] = even.astype(bf16)
            front_ref[to, rows + at : rows + at + 48, lanes] = odd.astype(bf16)

    def step_front(f, carry):
        for k in range(4):
            t_ref[k] = first_rows(win_ref, one_ref, 4 * f + k)
        second((4, 0, 1), 2 * f)
        second((1, 2, 3), 2 * f + 1)
        t_ref[4] = t_ref[3]
        return carry

    lax.fori_loop(0, F3, step_front, 0)

    def step_point(f, carry):
        for k in range(4):
            r_ref[4 * f + k] = jax.nn.relu(nn(front_ref[4 * f + k], pw_ref[0]))
        return carry

    lax.fori_loop(0, F2 // 4, step_point, 0)

    front_copy = pltpu.make_async_copy(front_ref, front_hbm, sem.at[1])
    front_copy.start()

    def third(f, whole):
        for lanes, at in stem_chunks(rows):

            def tap(k):
                return taps_ref[k : k + 1, lanes]

            lag, out = 0.0, 0.0
            for df in range(0 if whole else 1, 3):
                slot = 2 * f - 1 + df
                even = r_ref[slot, at : at + 48, lanes]
                odd = r_ref[slot, rows + at : rows + at + 48, lanes]
                lag += odd * tap(18 + df)
                out += even * tap(21 + df) + odd * tap(24 + df)
            lag_ref[8 + at : 56 + at, lanes] = lag
            out += lag_ref[7 + at : 55 + at, lanes]
            skip = max(0, EDGE - at)
            mid_ref[f, at + skip - EDGE : at + 48 - EDGE, lanes] = out[skip:].astype(bf16)

    third(0, False)

    def step_mid(f, carry):
        third(f, True)
        return carry

    lax.fori_loop(1, F3, step_mid, 0)
    for f in range(F3):
        last = jax.nn.relu(nn(mid_ref[f], pw_ref[1])).astype(bf16)
        last_ref[f] = last
        flat[:, CHANNELS * f : CHANNELS * f + CHANNELS] = last
    lin_copy.wait()
    x0_ref[...] = nn(flat[...], lin_ref[...].reshape(F3 * CHANNELS, D))
    front_copy.wait()


def back_scratch(rows):
    return [
        pltpu.VMEM((F3, rows - EDGE, CHANNELS), bf16),
        pltpu.VMEM((F3 + 1, rows + 8, CHANNELS), f32),
        pltpu.VMEM((F2 + 1, 3 * rows, CHANNELS), f32),
        pltpu.VMEM((F2, 2 * rows, CHANNELS), f32),
        pltpu.VMEM((F2, 2 * rows, CHANNELS), bf16),
        pltpu.VMEM((2, 4 * rows, CHANNELS), f32),
        pltpu.VMEM((F2, 8 * rows, CHANNELS), bf16),
        pltpu.VMEM((F3, CHANNELS, D), bf16),
        pltpu.VMEM((F3, rows - EDGE, CHANNELS), bf16),
        pltpu.VMEM((F3, rows - EDGE, CHANNELS), bf16),
        pltpu.VMEM((F2, 2 * rows, CHANNELS), bf16),
        pltpu.VMEM((F1 // 8, 4 * rows, LANES), bf16),
        pltpu.VMEM((16, F2 * 8 * rows), bf16),
        pltpu.SemaphoreType.DMA((6,)),
    ]


def stem_back_kernel(
    dx_ref,
    win_hbm,
    turn_hbm,
    one_ref,
    taps_ref,
    pw_ref,
    lin_hbm,
    front_hbm,
    mid_hbm,
    last_hbm,
    g_pw,
    sums,
    g_one,
    g_last,
    g_mid,
    g_front,
    p_ref,
    q_ref,
    t_ref,
    s_ref,
    lin_ref,
    last_ref,
    mid_ref,
    front_ref,
    win_ref,
    turn_ref,
    sem,
):
    copies = staged(
        [lin_hbm, last_hbm, mid_hbm, front_hbm, win_hbm, turn_hbm],
        [lin_ref, last_ref, mid_ref, front_ref, win_ref, turn_ref],
        sem,
    )
    rows = g_mid.shape[1] - 8
    tokens = rows - EDGE
    sums[...] = jnp.zeros_like(sums)
    g_one[...] = jnp.zeros_like(g_one)
    g_mid[:, 0:EDGE, :] = jnp.zeros((F3 + 1, EDGE, CHANNELS), f32)
    g_mid[:, rows:, :] = jnp.zeros((F3 + 1, 8, CHANNELS), f32)
    g_mid[F3] = jnp.zeros_like(g_mid[F3])
    g_front[F2] = jnp.zeros_like(g_front[F2])
    dx = dx_ref[...]
    copies[0].wait()
    copies[1].wait()
    for f in range(F3):
        grad = nt(dx, lin_ref[f])
        grad = jnp.where(last_ref[f].astype(f32) > 0, grad, 0.0).astype(bf16)
        g_last[f] = grad
    for f in range(F3):
        g_mid[f, EDGE:rows, :] = nt(g_last[f], pw_ref[1])
    whole = (F3 * tokens, CHANNELS)
    copies[2].wait()
    g_pw[1] = tn(mid_ref[...].reshape(whole), g_last[...].reshape(whole))

    copies[3].wait()

    def step_point(f, carry):
        for k in range(4):
            p_ref[4 * f + k] = jax.nn.relu(nn(front_ref[4 * f + k], pw_ref[0]))
        return carry

    lax.fori_loop(0, F2 // 4, step_point, 0)

    def step_mid(f, carry):
        for odd in range(2):
            uses = [(f, 2), (f + 1, 0)] if odd else [(f, 1)]
            here = 2 * f + odd
            for lane in range(0, CHANNELS, LANES):
                lanes = slice(lane, lane + LANES)

                def tap(k):
                    return taps_ref[k : k + 1, lanes]

                found = {}
                for at in range(0, rows, 48):
                    p_even = p_ref[here, at : at + 48, lanes]
                    p_odd = p_ref[here, rows + at : rows + at + 48, lanes]
                    d_even, d_odd = 0.0, 0.0
                    for which, df in uses:
                        g = g_mid[which, at : at + 48, lanes]
                        g_up = g_mid[which, at + 1 : at + 49, lanes]
                        d_even += g * tap(21 + df)
                        d_odd += g * tap(24 + df) + g_up * tap(18 + df)
                        for k, x in ((df, g_up * p_odd), (3 + df, g * p_even), (6 + df, g * p_odd)):
                            found[k] = found.get(k, 0.0) + eight(x)
                    q_ref[here, at : at + 48, lanes] = jnp.where(p_even > 0, d_even, 0.0).astype(bf16)
                    q_ref[here, rows + at : rows + at + 48, lanes] = jnp.where(
                        p_odd > 0, d_odd, 0.0
                    ).astype(bf16)
                for k, x in found.items():
                    sums[9 + k, :, lanes] += x
        return carry

    lax.fori_loop(0, F3, step_mid, 0)

    def step_back(f, carry):
        for k in range(4):
            grad = nt(q_ref[4 * f + k], pw_ref[0])
            g_front[4 * f + k, 0 : 2 * rows, :] = grad
            g_front[4 * f + k, 2 * rows :, :] = pltpu.roll(grad[:rows], rows - 1, 0)
        size = (8 * rows, CHANNELS)
        grad = tn(front_ref[pl.ds(4 * f, 4)].reshape(size), q_ref[pl.ds(4 * f, 4)].reshape(size))
        g_pw[0] = jnp.where(f == 0, grad, g_pw[0] + grad)
        return carry

    lax.fori_loop(0, F2 // 4, step_back, 0)

    copies[4].wait()
    copies[5].wait()

    def step_front(f, carry):
        for odd in range(2):
            t_ref[odd] = first_rows(win_ref, one_ref, 2 * f + odd)
        for odd in range(2):
            uses = [(f, 2), (f + 1, 0)] if odd else [(f, 1)]
            for lane in range(0, CHANNELS, LANES):
                lanes = slice(lane, lane + LANES)

                def tap(k):
                    return taps_ref[k : k + 1, lanes]

                found = {}
                for at in range(0, rows, 48):
                    t0, t1, t2, t3 = (
                        t_ref[odd, a * rows + at : a * rows + at + 48, lanes] for a in range(4)
                    )
                    d = [0.0] * 4
                    for which, df in uses:
                        e = g_front[which, at : at + 48, lanes]
                        o = g_front[which, rows + at : rows + at + 48, lanes]
                        e_up = g_front[which, 2 * rows + at : 2 * rows + at + 48, lanes]
                        d[0] += e * tap(12 + df)
                        d[1] += e * tap(15 + df) + o * tap(9 + df)
                        d[2] += o * tap(12 + df)
                        d[3] += o * tap(15 + df) + e_up * tap(9 + df)
                        for k, x in (
                            (df, t1 * o + t3 * e_up),
                            (3 + df, t0 * e + t2 * o),
                            (6 + df, t1 * e + t3 * o),
                        ):
                            found[k] = found.get(k, 0.0) + eight(x)
                    for a, (t, grad) in enumerate(zip((t0, t1, t2, t3), d)):
                        to = (4 * odd + a) * rows + at
                        s_ref[f, to : to + 48, lanes] = jnp.where(t > 0, grad, 0.0).astype(bf16)
                for k, x in found.items():
                    sums[k, :, lanes] += x

        return carry

    lax.fori_loop(0, F2, step_front, 0)
    part = F2 // 4
    for k in range(4):
        at = part * 8 * rows
        g_one[...] += nn(
            turn_ref[:, k * at : (k + 1) * at],
            s_ref[part * k : part * (k + 1)].reshape(at, CHANNELS),
        )


def stem_rows_kernel(
    g_pw, sums, g_one, vg_last, vg_conv, vg_mid, vg_att, out_ref, flat
):
    taps = jnp.concatenate(
        [g_one[0:9, :]]
        + [jnp.sum(sums[k], 0, keepdims=True) for k in range(18)],
        0,
    )
    order = [
        (vg_last, 2),
        (vg_last, 0),
        (vg_conv, 0),
        (vg_mid, 2),
        (vg_mid, 0),
        (vg_last, 3),
        (vg_last, 1),
        (vg_conv, 1),
        (vg_mid, 3),
        (vg_mid, 1),
        (vg_mid, 4),
        (vg_mid, 5),
        (vg_att, 0),
        (vg_att, 1),
    ] + [(vg_conv, k) for k in range(2, 11)]
    flat[ROW_AT[2] + ROWS[4] - 8 :, :] = jnp.zeros((flat.shape[0] - ROW_AT[2] - ROWS[4] + 8, LANES), f32)
    for h in range(2):
        lanes = slice(LANES * h, LANES * h + LANES)
        flat[pl.ds(h, 27, stride=2), :] = taps[:, lanes]
        for k in range(2):
            flat[pl.ds(ROW_AT[1] + 512 * k + h, CHANNELS, stride=2), :] = g_pw[k, :, lanes]
    for k, (ref, row) in enumerate(order):
        for j in range(4):
            at = ROW_AT[2] + 4 * k + j
            flat[at : at + 1, :] = ref[row : row + 1, LANES * j : LANES * j + LANES]
    out_ref[...] = flat[...].astype(bf16)


def ffn_forward(x, vec_ref, which, win, wout, pre_ref, normed_ref):
    normed = layer_norm(x, vec_ref[which : which + 1, :], vec_ref[which + 5 : which + 6, :])
    normed = normed.astype(bf16)
    normed_ref[...] = normed
    total = jnp.zeros_like(x)
    (in_copies, in_buf), (out_copies, out_buf) = win, wout
    for m in range(NPIECE):
        in_copies[m].wait()
        pre = nn(normed, block(in_buf, m))
        pre_ref[m] = pre
        out_copies[m].wait()
        total += nt((pre * sigmoid(pre)).astype(bf16), block(out_buf, m))
    return x + 0.5 * total


def ffn_backward(grad, x, vec_ref, which, in_buf, out_buf, pre_ref, normed_ref, order, write):
    low = (0.5 * grad).astype(bf16)
    back = jnp.zeros_like(x)
    for c, col, m in order:
        pre = pre_ref[m]
        sig = sigmoid(pre)
        write(c, col, 1, tn(low, (pre * sig).astype(bf16)))
        g_pre = (nn(low, block(out_buf, m)) * (sig * (1.0 + pre * (1.0 - sig)))).astype(bf16)
        write(c, col, 0, tn(normed_ref[...], g_pre))
        back += nt(g_pre, block(in_buf, m))
    dx, gain, shift = layer_norm_back(x, vec_ref[which : which + 1, :], back)
    return grad + dx, gain, shift


def first_kernel(
    weights,
    x_ref,
    vec_ref,
    x1_ref,
    pre_ref,
    n1_ref,
    n2_ref,
    in_buf,
    in_sem,
    out_buf,
    out_sem,
):
    win = fetched(weights, 0, 0, D, in_buf, in_sem)
    wout = fetched(weights, 1, 0, D, out_buf, out_sem)
    x1 = ffn_forward(x_ref[...], vec_ref, 0, (win, in_buf), (wout, out_buf), pre_ref, n1_ref)
    x1_ref[...] = x1
    n2_ref[...] = layer_norm(x1, vec_ref[1:2, :], vec_ref[6:7, :]).astype(bf16)


def position_kernel(
    weights, table_ref, n2_ref, vec_ref, pe_ref, qu_ref, qv_ref, buf, sem, q_buf, q_sem
):
    q_copies = fetched(weights, 2, 0, LANES, q_buf, q_sem)
    copies = fetched(weights, 2, 3 * LANES, 4 * LANES, buf, sem)
    for m in range(NPIECE):
        lanes = slice(LANES * m, LANES * m + LANES)
        q_copies[m].wait()
        query = nn(n2_ref[...], block(q_buf, m))
        qu_ref[:, lanes] = (query + vec_ref[12:13, lanes]).astype(bf16)
        qv_ref[:, lanes] = (query + vec_ref[13:14, lanes]).astype(bf16)
        copies[m].wait()
        pe_ref[:, lanes] = nn(table_ref[...], block(buf, m)).astype(bf16)


def head_lanes(h):
    return h // 2, HEAD_DIM * (h % 2), slice(HEAD_DIM * h, HEAD_DIM * h + HEAD_DIM)


def attention_kernel(
    weights,
    all_ref,
    x1_ref,
    qu_ref,
    qv_ref,
    pe_ref,
    vec_ref,
    keep_ref,
    valid_ref,
    x2_ref,
    kv_ref,
    prob_ref,
    att_ref,
    n3_ref,
    ga_ref,
    gb_ref,
    gated_ref,
    low_ref,
    high_ref,
    kv_buf,
    kv_sem,
    abo_buf,
    abo_sem,
):
    kv_copies = fetched(weights, 2, LANES, 3 * LANES, kv_buf, kv_sem)
    abo_copies = fetched(weights, 3, 0, 3 * LANES, abo_buf, abo_sem)
    rows, length = x1_ref.shape[0], all_ref.shape[0]
    width = rows + length
    for m in range(NPIECE):
        kv_copies[m].wait()
        kv_ref[m] = nn(all_ref[...], block(kv_buf, m)).astype(bf16)
    keep = keep_ref[...] > 0
    for h in range(HEADS):
        m, at, lanes = head_lanes(h)
        raw = nt(qu_ref[:, lanes], kv_ref[m, :, at : at + HEAD_DIM])
        far = nt(qv_ref[:, lanes], pe_ref[:, lanes])
        far = pltpu.roll(far, width - rows + 1, 1, stride=1, stride_axis=0)
        scores = jnp.where(keep, (raw + far[:, :length]) * 0.125, -1e30)
        expo = jnp.exp(scores - jnp.max(scores, -1, keepdims=True))
        prob = expo / jnp.sum(expo, -1, keepdims=True)
        prob_ref[h] = prob
        value = kv_ref[m, :, LANES + at : LANES + at + HEAD_DIM]
        att_ref[:, lanes] = nn(prob.astype(bf16), value).astype(bf16)
    x2 = x1_ref[...]
    for m in range(NPIECE):
        abo_copies[m].wait()
        lanes = slice(LANES * m, LANES * m + LANES)
        x2 += nt(att_ref[:, lanes], block(abo_buf, m, slice(2 * LANES, 3 * LANES)))
    x2_ref[...] = x2
    normed = layer_norm(x2, vec_ref[2:3, :], vec_ref[7:8, :]).astype(bf16)
    n3_ref[...] = normed
    for m in range(NPIECE):
        lanes = slice(LANES * m, LANES * m + LANES)
        gates = nn(normed, block(abo_buf, m, slice(0, 2 * LANES)))
        ga, gb = gates[:, :LANES], gates[:, LANES:]
        ga_ref[:, lanes] = ga
        gb_ref[:, lanes] = gb
        gated_ref[:, lanes] = ga * sigmoid(gb) * valid_ref[...]
    low_ref[...] = gated_ref[0:HALO, :]
    high_ref[...] = gated_ref[rows - HALO :, :]


def write_stats(stat_ref, first, second, number=None):
    rows = [x[:, LANES * k : LANES * k + LANES] for x in (first, second) for k in range(4)]
    if number is not None:
        rows.append(jnp.broadcast_to(number, (8, LANES)))
    stat_ref[...] = jnp.broadcast_to(jnp.concatenate(rows, 0)[None], stat_ref.shape)


def read_stats(stat_ref):
    whole = jnp.sum(stat_ref[...], 0)
    first = jnp.concatenate([whole[k : k + 1] for k in range(4)], 1)
    second = jnp.concatenate([whole[k : k + 1] for k in range(4, 8)], 1)
    return first, second, whole[8:9, 0:1] if whole.shape[0] > 8 else None


def conv_kernel(prev_ref, gated_ref, next_ref, vec_ref, valid_ref, hidden_ref, stat_ref, wide):
    rows = gated_ref.shape[0]
    wide[0:HALO, :] = prev_ref[...]
    wide[HALO : HALO + rows, :] = gated_ref[...]
    wide[HALO + rows :, :] = next_ref[...]
    at = HALO - KERNEL // 2
    hidden = sum(wide[at + k : at + k + rows, :] * vec_ref[14 + k : 15 + k, :] for k in range(KERNEL))
    hidden_ref[...] = hidden
    valid = valid_ref[...]
    kept = hidden * valid
    write_stats(
        stat_ref,
        jnp.sum(kept, 0, keepdims=True),
        jnp.sum(kept * hidden, 0, keepdims=True),
        jnp.sum(valid, 0, keepdims=True),
    )


def middle_kernel(
    spot,
    weights,
    more,
    hidden_ref,
    stat_ref,
    x2_ref,
    head_ref,
    vec_ref,
    label_ref,
    weight_ref,
    valid_ref,
    keep_ref,
    send_ref,
    g_head_ref,
    dx3_ref,
    act_ref,
    dy_ref,
    yhat_ref,
    low_ref,
    high_ref,
    part_ref,
    vgrad_ref,
    loss_ref,
    pre_ref,
    n4_ref,
    c_buf,
    c_sem,
    in_buf,
    in_sem,
    out_buf,
    out_sem,
):
    c_copies = fetched(weights, 3, 3 * LANES, 4 * LANES, c_buf, c_sem)
    win = fetched(more, 0, 0, D, in_buf, in_sem), in_buf
    wout = fetched(more, 1, 0, D, out_buf, out_sem), out_buf
    rows = x2_ref.shape[0]
    first, second, count = read_stats(stat_ref)
    mean = first / count
    inverse = lax.rsqrt(second / count - mean * mean + norm_eps)
    yhat = (hidden_ref[...] - mean) * inverse
    yhat_ref[...] = yhat
    c = yhat * vec_ref[10:11, :] + vec_ref[11:12, :]
    sig = sigmoid(c)
    act = (c * sig).astype(bf16)
    act_ref[...] = act
    x3 = x2_ref[...]
    for m in range(NPIECE):
        c_copies[m].wait()
        x3 += nt(act[:, LANES * m : LANES * m + LANES], block(c_buf, m))
    x4 = ffn_forward(x3, vec_ref, 3, win, wout, pre_ref, n4_ref)
    normed = layer_norm(x4, vec_ref[4:5, :], vec_ref[9:10, :]).astype(bf16)
    logits = nn(normed, head_ref[...])
    column = lax.broadcasted_iota(jnp.int32, logits.shape, 1)
    logits = jnp.where(column < CLASSES, logits, -1e30)
    top = jnp.max(logits, -1, keepdims=True)
    total = top + jnp.log(jnp.sum(jnp.exp(logits - top), -1, keepdims=True))
    hit = column == label_ref[...]
    picked = jnp.sum(jnp.where(hit, logits, 0.0), -1, keepdims=True)
    weight = weight_ref[...]
    loss = jnp.sum(weight * (total - picked), 0, keepdims=True)
    g_logits = (jnp.exp(logits - total) - hit.astype(f32)) * (weight / count)
    g_logits = g_logits.astype(bf16)
    g_head_ref[...] = tn(normed, g_logits).astype(bf16)
    dx4, gain, shift = layer_norm_back(x4, vec_ref[4:5, :], nt(g_logits, head_ref[...]))
    vgrad_ref[0:1, :] = gain
    vgrad_ref[1:2, :] = shift
    dx3, gain, shift = ffn_backward(
        dx4,
        x3,
        vec_ref,
        3,
        in_buf,
        out_buf,
        pre_ref,
        n4_ref,
        core_pieces(spot),
        lambda c, *place: write_core_piece((keep_ref, send_ref)[c], *place),
    )
    vgrad_ref[2:3, :] = gain
    vgrad_ref[3:4, :] = shift
    dx3_ref[...] = dx3
    low = dx3.astype(bf16)
    valid = valid_ref[...]
    parts = []
    for m in range(NPIECE):
        lanes = slice(LANES * m, LANES * m + LANES)
        slope = sig[:, lanes] * (1.0 + c[:, lanes] * (1.0 - sig[:, lanes]))
        dc = nn(low, block(c_buf, m)) * slope
        vgrad_ref[4:5, lanes] = jnp.sum(dc * yhat[:, lanes], 0, keepdims=True)
        vgrad_ref[5:6, lanes] = jnp.sum(dc, 0, keepdims=True)
        dy = dc * vec_ref[10:11, lanes]
        dy_ref[:, lanes] = dy
        kept = dy * valid
        parts.append(
            (
                jnp.sum(kept, 0, keepdims=True),
                jnp.sum(kept * yhat[:, lanes], 0, keepdims=True),
            )
        )
    for k, ref in enumerate((dy_ref, yhat_ref)):
        low_ref[HALO * k : HALO * k + HALO, :] = ref[0:HALO, :]
        high_ref[HALO * k : HALO * k + HALO, :] = ref[rows - HALO :, :]
    write_stats(
        part_ref,
        jnp.concatenate([a for a, _ in parts], 1),
        jnp.concatenate([b for _, b in parts], 1),
    )
    loss_ref[...] = loss


def conv_back_kernel(
    weights,
    dy_ref,
    yhat_ref,
    prev_ref,
    next_ref,
    part_ref,
    stat_ref,
    wide_valid_ref,
    gprev_ref,
    gated_ref,
    gnext_ref,
    ga_ref,
    gb_ref,
    x2_ref,
    dx3_ref,
    vec_ref,
    dgate_ref,
    dx2_ref,
    vgrad_ref,
    count_ref,
    wide,
    wide_y,
    dh,
    buf,
    sem,
):
    copies = fetched(weights, 3, 0, 2 * LANES, buf, sem)
    rows = dy_ref.shape[0]
    first, second, count = read_stats(stat_ref)
    mean = first / count
    inverse = lax.rsqrt(second / count - mean * mean + norm_eps)
    first, second, _ = read_stats(part_ref)
    count_ref[...] = count
    wide[0:HALO, :] = prev_ref[0:HALO, :]
    wide[HALO : HALO + rows, :] = dy_ref[...]
    wide[HALO + rows :, :] = next_ref[0:HALO, :]
    wide_y[0:HALO, :] = prev_ref[HALO:, :]
    wide_y[HALO : HALO + rows, :] = yhat_ref[...]
    wide_y[HALO + rows :, :] = next_ref[HALO:, :]
    mean_part = (first + wide_y[...] * second) / count
    dh[...] = inverse * (wide[...] - wide_valid_ref[...] * mean_part)
    wide[0:HALO, :] = gprev_ref[...]
    wide[HALO : HALO + rows, :] = gated_ref[...]
    wide[HALO + rows :, :] = gnext_ref[...]
    half = KERNEL // 2
    own = dh[HALO : HALO + rows, :]
    d_gated = jnp.zeros((rows, D), f32)
    for k in range(KERNEL):
        d_gated += dh[HALO - k + half : HALO - k + half + rows, :] * vec_ref[14 + k : 15 + k, :]
        at = HALO + k - half
        vgrad_ref[2 + k : 3 + k, :] = jnp.sum(own * wide[at : at + rows, :], 0, keepdims=True)
    d_gated = d_gated * wide_valid_ref[HALO : HALO + rows, :]
    sig = sigmoid(gb_ref[...])
    dga = (d_gated * sig).astype(bf16)
    dgb = (d_gated * ga_ref[...] * sig * (1.0 - sig)).astype(bf16)
    back = jnp.zeros((rows, D), f32)
    for m in range(NPIECE):
        lanes = slice(LANES * m, LANES * m + LANES)
        both = jnp.concatenate([dga[:, lanes], dgb[:, lanes]], 1)
        dgate_ref[m] = both
        copies[m].wait()
        back += nt(both, block(buf, m))
    dx, gain, shift = layer_norm_back(x2_ref[...], vec_ref[2:3, :], back)
    vgrad_ref[0:1, :] = gain
    vgrad_ref[1:2, :] = shift
    dx2_ref[...] = dx3_ref[...] + dx


def back_kernel(
    weights,
    dx2_ref,
    prob_ref,
    kv_ref,
    qu_ref,
    qv_ref,
    pe_ref,
    dquery_ref,
    dkv_ref,
    dpe_ref,
    dall_ref,
    down_ref,
    vgrad_ref,
    dq,
    o_buf,
    o_sem,
    mix_buf,
    mix_sem,
):
    o_copies = fetched(weights, 3, 2 * LANES, 3 * LANES, o_buf, o_sem)
    mix_copies = fetched(weights, 2, 0, 3 * LANES, mix_buf, mix_sem)
    rows, length = dx2_ref.shape[0], dall_ref.shape[0]
    low = dx2_ref[...].astype(bf16)
    flip = flip_matrix(rows)
    turned_q = nn(flip, qv_ref[...]).astype(bf16)
    for h in range(HEADS):
        m, at, lanes = head_lanes(h)
        if at == 0:
            o_copies[m].wait()
            d_att = nn(low, block(o_buf, m)).astype(bf16)
        d_out = d_att[:, at : at + HEAD_DIM]
        prob = prob_ref[h]
        key = kv_ref[m, :, at : at + HEAD_DIM]
        value = kv_ref[m, :, LANES + at : LANES + at + HEAD_DIM]
        d_prob = nt(d_out, value)
        d_scores = prob * (d_prob - jnp.sum(prob * d_prob, -1, keepdims=True))
        d_raw = (d_scores * 0.125).astype(bf16)
        dkv_ref[m, :, LANES + at : LANES + at + HEAD_DIM] = tn(prob.astype(bf16), d_out).astype(bf16)
        dkv_ref[m, :, at : at + HEAD_DIM] = tn(d_raw, qu_ref[:, lanes]).astype(bf16)
        dq[0:rows, lanes] = nn(d_raw, key)
        turned = nn(flip, d_raw)
        turned = jnp.concatenate([turned, jnp.zeros((rows, rows), f32)], 1)
        turned = pltpu.roll(turned, 0, 1, stride=1, stride_axis=0).astype(bf16)
        dq[rows : 2 * rows, lanes] = nn(turned, pe_ref[:, lanes])
        dpe_ref[:, lanes] = tn(turned, turned_q[:, lanes]).astype(bf16)
    d_u, d_v = dq[0:rows, :], dq[rows : 2 * rows, :]
    vgrad_ref[0:1, :] = jnp.sum(d_u, 0, keepdims=True)
    vgrad_ref[1:2, :] = jnp.sum(d_v, 0, keepdims=True)
    straight = jnp.dot(
        flip.astype(f32), d_v, precision=lax.Precision.HIGHEST, preferred_element_type=f32
    )
    dquery = (d_u + straight).astype(bf16)
    dquery_ref[...] = dquery
    d_all = jnp.zeros((length, D), f32)
    d_own = jnp.zeros((rows, D), f32)
    for m in range(NPIECE):
        mix_copies[m].wait()
        d_own += nt(dquery[:, LANES * m : LANES * m + LANES], block(mix_buf, m, slice(0, LANES)))
        d_all += nt(dkv_ref[m], block(mix_buf, m, slice(LANES, 3 * LANES)))
    dall_ref[...] = d_all.astype(bf16)
    down_ref[...] = d_own


def mix_grad_kernel(
    spot,
    dx2_ref,
    dx3_ref,
    dgate_ref,
    n3_ref,
    act_ref,
    att_ref,
    n2_ref,
    all_ref,
    table_ref,
    dquery_ref,
    dkv_ref,
    dpe_ref,
    *parts,
):
    low = dx2_ref[...].astype(bf16)
    low_three = dx3_ref[...].astype(bf16)
    for c, x, m in pieces(spot):
        lanes = aligned(LANES * m)
        grads = [
            tn(n2_ref[...], dquery_ref[:, lanes]),
            tn(all_ref[...], dkv_ref[m]),
            tn(table_ref[...], dpe_ref[:, lanes]),
        ]
        write_piece(spot, parts[c], 0, x, jnp.concatenate(grads, 1))
        grads = [
            tn(n3_ref[...], dgate_ref[m]),
            tn(low, att_ref[:, lanes]),
            tn(low_three, act_ref[:, lanes]),
        ]
        write_piece(spot, parts[c], 1, x, jnp.concatenate(grads, 1))


def last_kernel(
    spot,
    weights,
    dx2_ref,
    d_all_ref,
    d_own_ref,
    x1_ref,
    x0_ref,
    pre_ref,
    n1_ref,
    vec_ref,
    keep_ref,
    send_ref,
    dx0_ref,
    vgrad_ref,
    in_buf,
    in_sem,
    out_buf,
    out_sem,
):
    copies = fetched(weights, 0, 0, D, in_buf, in_sem)
    copies += fetched(weights, 1, 0, D, out_buf, out_sem)
    grad = total(*[d_all_ref[k] for k in range(d_all_ref.shape[0])]) + d_own_ref[...]
    dx, gain, shift = layer_norm_back(x1_ref[...], vec_ref[1:2, :], grad)
    vgrad_ref[0:1, :] = gain
    vgrad_ref[1:2, :] = shift
    for copy in copies:
        copy.wait()
    dx0, gain, shift = ffn_backward(
        dx2_ref[...] + dx,
        x0_ref[...],
        vec_ref,
        0,
        in_buf,
        out_buf,
        pre_ref,
        n1_ref,
        pieces(spot),
        lambda c, x, half, grad: write_piece(spot, (keep_ref, send_ref)[c], half, x, grad),
    )
    vgrad_ref[2:3, :] = gain
    vgrad_ref[3:4, :] = shift
    dx0_ref[...] = dx0.astype(bf16)


def adam(state, grad, rate):
    first_new = beta_one * state[1] + (1.0 - beta_one) * grad
    second_new = beta_two * state[2] + (1.0 - beta_two) * grad * grad
    direction = (
        first_new
        / (1.0 - beta_one**STEP)
        / (jnp.sqrt(second_new / (1.0 - beta_two**STEP)) + adam_eps)
    )
    weight_new = state[0] - rate * (direction + decay_rate * state[0])
    return (weight_new, first_new, second_new)


def small_rate(positions):
    rate = jnp.full(positions.shape, small_rates[-1], f32)
    for k in range(3, -1, -1):
        rate = jnp.where(positions < sum(SIZES[: k + 1]), small_rates[k], rate)
    return rate


def mel_windows(mel, utter_len, rank, tokens):
    frame = rank * (8 * tokens) + jnp.arange(8 * tokens, dtype=jnp.int32)
    kept = jnp.where((frame < utter_len)[:, None], mel, jnp.zeros((), bf16))
    prior = passed_along(kept[-8:], 1)
    rows = tokens + EDGE
    field = jnp.concatenate([jnp.zeros((8 * (EDGE - 1), MEL), bf16), prior, kept], 0)
    field = field.reshape(rows, 8, MEL).transpose(1, 2, 0)
    lag = jnp.concatenate([jnp.zeros((1, MEL, 1), bf16), field[7:8, :, :-1]], 2)
    field = jnp.concatenate([lag, field], 0)
    field = jnp.pad(field, ((0, 0), (1, 1), (0, 0))).reshape(9, F1 + 1, 2, rows)
    bands = [field[:, :F1, 0], field[:, :F1, 1], field[:, 1:, 0]]
    taps = [bands[df][dt : dt + 7 : 2] for dt in range(3) for df in range(3)]
    taps = jnp.stack(taps + [jnp.zeros_like(taps[0])] * 7, 0)
    turned = taps.transpose(0, 2, 1, 3).reshape(16, F1 * 4 * rows)
    wide = taps.reshape(16, 4, F1 // 8, 8, rows).transpose(2, 1, 4, 3, 0)
    return wide.reshape(F1 // 8, 4 * rows, LANES), turned


def position_table(rank, rows, length):
    distance = (rows * rank + rows - 1 - jnp.arange(rows + length)).astype(f32)[:, None]
    inverse_freq = jnp.exp(jnp.arange(D // 2).astype(f32) * (-2.0 * math.log(10000.0) / D))
    angles = distance * inverse_freq[None, :]
    return jnp.concatenate([jnp.sin(angles), jnp.cos(angles)], 1).astype(bf16)


def gathered_heads(n2, planned_mesh):
    if not planned_mesh:
        return lax.all_gather(n2, "mp", axis=0, tiled=True)
    rows = n2.shape[0]
    pair = jnp.stack([n2, sent(n2, "x")])
    both = jnp.stack([pair, sent(pair, "c")])
    rank = lax.axis_index("mp")
    order = [(rank % 2, rank // 2)]
    whole = jnp.zeros((4, rows, D), bf16)
    c, x = order[0]
    for i in range(2):
        for j in range(2):
            at = ((x + j) % 2) * 2 + (c + i) % 2
            whole = lax.dynamic_update_slice(whole, both[i, j][None], (at, 0, 0))
    return whole.reshape(4 * rows, D)


def body(mel, lengths, alignment, loss_mask, ff_in, ff_out, mix_in, mix_out, small):
    n_dp, n_mp = lax.axis_size("dp"), lax.axis_size("mp")
    ndev = n_dp * n_mp
    plan = planned(n_dp, n_mp)
    rank, dp_rank = lax.axis_index("mp"), lax.axis_index("dp")
    device = lax.axis_index(("dp", "mp"))
    tokens = alignment.shape[1]
    length = tokens * n_mp
    rows = tokens + EDGE
    own_rows = ff_in.shape[2]
    shard = small.shape[1]
    half = -(-(-(-(shard + 16 * LANES - 1) // LANES)) // 32) * 16
    chunk = 2 * half
    flat_rows = max((shard * (ndev - 1)) // (16 * LANES) * 16 + chunk, NROWS)
    flat_rows = -(-flat_rows // 8) * 8
    if plan:
        spot = jnp.stack([rank % 2, rank // 2, dp_rank % 2, dp_rank // 2])
        deep, lines = LINES, n_dp // LINES
    else:
        spot = jnp.zeros((4,), jnp.int32)
        deep, lines = 1, 1
    spot = spot.astype(jnp.int32), pltpu.SMEM
    piece_rows = D // (deep * lines)
    small_rows = half * (n_dp // (deep * lines))

    row = first_row(shard, device)
    offset = shard * device - row * LANES
    small_low = lax.dynamic_update_slice_in_dim(
        jnp.zeros((chunk * LANES,), bf16), small[0].astype(bf16), offset, 0
    ).reshape(chunk, LANES)
    in_low = ff_in[0].astype(bf16)
    out_low = ff_out[0].astype(bf16).transpose(0, 2, 1)
    mix_low = mix_in[0].astype(bf16)
    mixo_low = mix_out[0].astype(bf16).transpose(0, 2, 1)
    qkvp_low = mix_low[:, 0:4].reshape(own_rows, 4 * LANES)
    abo_low = jnp.concatenate([mix_low[:, 4], mix_low[:, 5], mixo_low[0], mixo_low[1]], 1)
    def gathered(low):
        whole = lax.all_gather(jnp.stack(low), ("dp", "mp"), axis=0)
        whole = whole.reshape(n_dp, n_mp, len(low), own_rows, D)
        if not plan:
            whole = whole.transpose(1, 2, 0, 3, 4).reshape(1, n_mp, len(low), D, D)
        return whole

    big_all = gathered([in_low[0], out_low[0], qkvp_low, abo_low])
    more_all = gathered([in_low[1], out_low[1]])
    weights, more = (big_all, pl.ANY), (more_all, pl.ANY)
    utter_len = lengths[0]
    windows, windows_t = mel_windows(mel[0], utter_len, rank, tokens)
    table = position_table(rank, tokens, length)
    if plan:
        few_all = Gathered(small_low)
        few_all.lines(), few_all.after(windows, windows_t, table).first(), few_all.second()
        small_all = few_all.cores()
    else:
        small_all = [lax.all_gather(small_low, ("dp", "mp"), axis=0)]

    frames = jnp.arange(length, dtype=jnp.int32)
    keep_row = (8 * frames < utter_len).astype(f32)[None, :]
    wide_frame = rank * tokens - HALO + jnp.arange(tokens + 2 * HALO, dtype=jnp.int32)
    wide_valid = (wide_frame >= 0) & (wide_frame < length) & (8 * wide_frame < utter_len)
    wide_valid = wide_valid.astype(f32)[:, None]
    valid = wide_valid[HALO : HALO + tokens]
    weight = valid * loss_mask[0].astype(f32)[:, None]

    def split(each):
        return [((COLS, deep, lines, each, D), bf16)] * 4

    unpack = functools.partial(unpack_kernel if plan else unpack_whole_kernel, shard)
    taps, tap_one, pointwise, linear, head, vec = call(
        unpack,
        [
            ((32, CHANNELS), f32),
            ((8, LANES, CHANNELS), bf16),
            ((2, CHANNELS, CHANNELS), bf16),
            ((F3, CHANNELS, D), bf16),
            ((D, CPAD), bf16),
            ((24, D), f32),
        ],
        ([spot] if plan else []) + small_all,
        [pltpu.VMEM((flat_rows, LANES), f32)],
        us=7,
        name="unpack",
    )
    x0, front, mid, last = call(
        stem_kernel,
        [
            ((tokens, D), f32),
            ((F2, 2 * rows, CHANNELS), bf16),
            ((F3, tokens, CHANNELS), bf16),
            ((F3, tokens, CHANNELS), bf16),
        ],
        [windows, tap_one, taps, pointwise, (linear, pl.ANY)],
        stem_scratch(rows),
        us=13,
        out_any=(1,),
        name="stem",
    )
    x1, pre_one, n1, n2 = call(
        first_kernel,
        [
            ((tokens, D), f32),
            ((n_mp, tokens, D), f32),
            ((tokens, D), bf16),
            ((tokens, D), bf16),
        ],
        [weights, x0, vec],
        buffers(big_all, D, D),
        us=6,
        name="first",
    )
    n_all = gathered_heads(n2, plan)
    pe, qu, qv = call(
        position_kernel,
        [((tokens + length, D), bf16), ((tokens, D), bf16), ((tokens, D), bf16)],
        [weights, table, n2, vec],
        buffers(big_all, LANES, LANES),
        us=5,
        name="position",
    )
    x2, kv, prob, att, n3, ga, gb, gated, g_low, g_high = call(
        attention_kernel,
        [
            ((tokens, D), f32),
            ((n_mp, length, 2 * LANES), bf16),
            ((HEADS, tokens, length), f32),
            ((tokens, D), bf16),
            ((tokens, D), bf16),
            ((tokens, D), f32),
            ((tokens, D), f32),
            ((tokens, D), f32),
            ((HALO, D), f32),
            ((HALO, D), f32),
        ],
        [weights, n_all, x1, qu, qv, pe, vec, keep_row, valid],
        buffers(big_all, 2 * LANES, 3 * LANES),
        us=10,
        name="attention",
    )
    g_prev, g_next = passed_along(g_high, 1), passed_along(g_low, -1)
    stat_shape = ((ndev, 16, LANES), f32)
    wide = pltpu.VMEM((tokens + 2 * HALO, D), f32)
    hidden, stat = call(
        conv_kernel,
        [((tokens, D), f32), stat_shape],
        [g_prev, gated, g_next, vec, valid],
        [wide],
        us=2,
        name="conv",
    )
    stat = spread(stat)
    two_keep, two_send, g_head, dx3, act, dy, yhat, b_low, b_high, part, vg_mid, loss = call(
        middle_kernel,
        [
            *[((n_dp if plan else 1, COLS, 2, own_rows if plan else D, D), bf16)] * 2,
            ((D, CPAD), bf16),
            ((tokens, D), f32),
            ((tokens, D), bf16),
            ((tokens, D), f32),
            ((tokens, D), f32),
            ((2 * HALO, D), f32),
            ((2 * HALO, D), f32),
            ((ndev, 8, LANES), f32),
            ((6, D), f32),
            ((1, 1), f32),
        ],
        [spot, weights, more, hidden, stat, x2, head, vec, alignment[0][:, None], weight, valid],
        [
            pltpu.VMEM((n_mp, tokens, D), f32),
            pltpu.VMEM((tokens, D), bf16),
            *buffers(big_all, LANES, D, D),
        ],
        us=13,
        name="middle",
    )
    b_prev, b_next = passed_along(b_high, 1), passed_along(b_low, -1)
    part = spread(part)
    two_both, own_two = reduced_cores(two_keep, two_send, plan)
    dgate, dx2, vg_conv, count = call(
        conv_back_kernel,
        [
            ((n_mp, tokens, 2 * LANES), bf16),
            ((tokens, D), f32),
            ((11, D), f32),
            ((1, 1), f32),
        ],
        [
            weights,
            dy,
            yhat,
            b_prev,
            b_next,
            part,
            stat,
            wide_valid,
            g_prev,
            gated,
            g_next,
            ga,
            gb,
            x2,
            dx3,
            vec,
        ],
        [wide, wide, wide, *buffers(big_all, 2 * LANES)],
        us=4,
        name="conv_back",
    )
    dquery, dkv, dpe, d_all, d_own, vg_att = call(
        back_kernel,
        [
            ((tokens, D), bf16),
            ((n_mp, length, 2 * LANES), bf16),
            ((tokens + length, D), bf16),
            ((length, D), bf16),
            ((tokens, D), f32),
            ((2, D), f32),
        ],
        [weights, dx2, prob, kv, qu, qv, pe],
        [pltpu.VMEM((2 * tokens, D), f32), *buffers(big_all, LANES, 3 * LANES)],
        us=10,
        after=two_both,
        name="back",
    )
    if plan:
        pair = d_all.reshape(2, 2, tokens, D)
        core, col = rank % 2, rank // 2
        other = lax.dynamic_slice_in_dim(pair, 1 - core, 1, 1)[:, 0]
        own = lax.dynamic_slice_in_dim(pair, core, 1, 1)[:, 0]
        pair = low_total(own, sent(other, "c"))
        wait = [pair]
        other = lax.dynamic_slice_in_dim(pair, 1 - col, 1, 0)
        own = lax.dynamic_slice_in_dim(pair, col, 1, 0)
        d_mine = jnp.concatenate([own, sent(other, "x")], 0)
    else:
        d_mine = lax.psum_scatter(d_all, "mp", scatter_dimension=0, tiled=True)[None]
        wait = ()
    one_way = [((COLS, deep, lines, 2 * piece_rows, D), bf16)] * 2
    mix = call(
        mix_grad_kernel,
        one_way,
        [spot, dx2, dx3, dgate, n3, act, att, n2, n_all, table, dquery, dkv, dpe],
        us=7,
        after=wait,
        name="mix_grad",
    )
    mix_sum = ReducedOneWay(*mix, "xy")
    *one, dx0, vg_last = call(
        last_kernel,
        [*one_way, ((tokens, D), bf16), ((4, D), f32)],
        [spot, weights, dx2, d_mine, d_own, x1, x0, pre_one, n1, vec],
        buffers(big_all, D, D),
        us=8,
        after=mix[:1],
        name="last",
    )
    one_sum = ReducedOneWay(*one, "yx")
    few_parts = call(
        functools.partial(pack_kernel, shard, n_dp),
        [((COLS, deep, lines, small_rows, LANES), bf16)] * 4,
        [spot, last, dx0, g_head],
        [
            pltpu.VMEM((flat_rows, LANES), f32),
            pltpu.VMEM((4, COLS, deep, lines, small_rows, LANES), bf16),
            pltpu.SemaphoreType.DMA((4,)),
        ],
        out_any=(0, 1, 2, 3),
        us=5,
        after=mix_sum.cores() if plan else (),
        name="pack",
    )
    few_sum = Reduced(*few_parts)
    g_pw, sums, g_one = call(
        stem_back_kernel,
        [
            ((2, CHANNELS, CHANNELS), f32),
            ((18, 8, CHANNELS), f32),
            ((16, CHANNELS), f32),
        ],
        [
            dx0,
            (windows, pl.ANY),
            (windows_t, pl.ANY),
            tap_one,
            taps,
            pointwise,
            (linear, pl.ANY),
            (front, pl.ANY),
            (mid, pl.ANY),
            (last, pl.ANY),
        ],
        back_scratch(rows),
        us=27,
        after=one_sum.cores() if plan else (),
        name="stem_back",
    )
    used = ROW_AT[2] + ROWS[4]
    share = -(-(-(-used // ndev)) // 16) * 16
    (few,) = call(
        stem_rows_kernel,
        [((ndev * share, LANES), bf16)],
        [g_pw, sums, g_one, vg_last, vg_conv, vg_mid, vg_att],
        [pltpu.VMEM((ndev * share, LANES), f32)],
        us=2,
        after=mix_sum.first() + one_sum.first() + few_sum.cores() if plan else (),
        name="stem_rows",
    )
    few = jnp.sum(spread(few.reshape(ndev, share, LANES)).astype(f32), 0)

    if plan:
        mix_sum.second()
        own_mix, own_abo = mix_sum.lines()
        few_sum.first()
        one_sum.second()
        own_in_one, own_out_one = one_sum.lines()
        few_sum.second()
        own_few = few_sum.lines()
    else:

        def halves(keep, send):
            return [x[..., D * k : D * k + D, :] for x in (keep, send) for k in range(2)]

        own_mix, own_abo = reduced_whole(halves(*mix), own_rows)
        own_in_one, own_out_one = reduced_whole(halves(*one), own_rows)
        own_few = reduced_whole(few_parts, half)
    own_chunk = jnp.concatenate(own_few, 0)

    own_in_two, own_out_two = held(own_two, [few]).reshape(2, own_rows, D).astype(f32)
    start = shard * device
    positions = start + jnp.arange(shard, dtype=jnp.int32)
    own = [own_in_one, own_out_one, own_mix, own_abo, own_in_two, own_out_two]
    packed = lax.dynamic_slice_in_dim(own_chunk.reshape(-1), offset, shard, 0)
    local_sq = sum(jnp.sum(grad * grad) for grad in own) + jnp.sum(packed * packed)
    numbers = []
    for value in (local_sq, loss[0, 0]):
        for _ in range(3):
            numbers.append(value.astype(bf16))
            value = value - numbers[-1].astype(f32)
    number = jnp.pad(jnp.stack(numbers), (0, LANES - len(numbers)))
    number = jnp.broadcast_to(number, (16, LANES))
    known = jnp.concatenate([few.astype(bf16), number], 0)
    known = spread(jnp.broadcast_to(known[None], (ndev, share + 16, LANES))).astype(f32)
    few = known[:, :share].reshape(ndev * share, LANES)
    total_sq = jnp.sum(known[:, share, 0:3]) + jnp.sum(few * few)
    grad_norm = jnp.sqrt(total_sq)
    factor = clip_norm / jnp.maximum(grad_norm, clip_norm)

    rows_of = row + jnp.arange(chunk, dtype=jnp.int32)[:, None]
    few = jnp.concatenate([few, jnp.zeros((chunk, LANES), f32)], 0)

    def window(begin, end, at):
        start_at = jnp.clip(row - begin + at, 0, few.shape[0] - chunk)
        part = lax.dynamic_slice_in_dim(few, start_at, chunk, 0)
        return jnp.where((rows_of >= begin) & (rows_of < end), part, 0.0)

    own_chunk = own_chunk + window(0, ROW_AT[2], 0) + window(ROW_AT[4], NROWS, ROW_AT[2])
    own_small = lax.dynamic_slice_in_dim(own_chunk.reshape(-1), offset, shard, 0)

    grad_in = jnp.stack([own_in_one, own_in_two])
    grad_out = jnp.stack([own_out_one, own_out_two]).transpose(0, 2, 1)
    grad_mix = jnp.concatenate([own_mix, own_abo[:, : 2 * LANES]], 1).reshape(own_rows, 6, LANES)
    grad_mixo = own_abo[:, 2 * LANES :].reshape(own_rows, 2, LANES).transpose(1, 2, 0)
    rates = (0.1, 0.05, 0.1, jnp.array([1.0, 0.1], f32)[:, None, None])
    states = (ff_in, ff_out, mix_in, mix_out)
    grads = (grad_in, grad_out, grad_mix, grad_mixo)
    outs = []
    for state, grad, rate in zip(states, grads, rates):
        outs.extend(adam(state, grad * factor, rate))
    outs.extend(adam(small, own_small * factor, small_rate(positions)))
    vec_grad = few[ROW_AT[2] : used].reshape(23, D) * factor
    return (*outs, vec_grad, jnp.sum(known[:, share, 3:6]) / count[0, 0], grad_norm)


def solution(mesh):
    in_specs = (
        P("dp", "mp", None),
        P("dp"),
        P("dp", "mp"),
        P("dp", "mp"),
        P(None, None, "dp", "mp"),
        P(None, None, "mp", "dp"),
        P(None, "dp", None, "mp"),
        P(None, None, "mp", "dp"),
        P(None, ("dp", "mp")),
    )
    in_block, out_block = P(None, "dp", "mp"), P(None, "mp", "dp")
    mix_block, flat = P("dp", None, "mp"), P(("dp", "mp"))
    out_specs = (
        (in_block,) * 3 + (out_block,) * 3 + (mix_block,) * 3 + (out_block,) * 3 + (flat,) * 3
    )
    out_specs = out_specs + (P(), P(), P())
    return jax.shard_map(body, mesh=mesh, in_specs=in_specs, out_specs=out_specs, check_vma=False)
```
